32 devices in a mesh: groups: 2 (over x), blocks: 16 (over z, y, core).
Axes of the slice: x: 2, y: 2, z: 4, core: 2. Of those that a mesh axis runs over, the one named last changes fastest.
Arguments:
- sketches: bfloat16 [24576, 8192], P(('groups', 'blocks')), parts along dimension 0, may hold values from -60 to 60
- test_sketches: bfloat16 [128, 8192], replicated, may hold values from -60 to 60
- domain_map: int32 [24576], P(('groups', 'blocks')), parts along dimension 0, may hold values from 0 to 63
Outputs:
- gram_tiles: float32 [2, 24576, 768], P(None, ('groups', 'blocks')), parts along dimension 1
- redundancy: float32 [24576], P(('groups', 'blocks')), parts along dimension 0
- domain_scores: float32 [128, 128], P(('groups', 'blocks')), parts along dimension 0
The draws below stay inside these ranges and needn't reach their ends.
There are 2 independent parts, one for each index of `groups`. The reference program is written for one: setup_inputs(seed, part) draws one part's arguments, and reference() takes and returns one part's arrays. A program takes and returns all parts, laid end to end along the dimension named above; an argument that names none is the same for every part. Nothing has to cross between parts.
All inputs are finite; a program needn't handle non-finite values.
Results may differ from the reference program's by a relative error of at most 0.0029.
Values may be sent and summed in bfloat16 or wider, within the bound.
No kernel may reach another device: no remote copies, remote signals or barrier semaphores. Data moves between devices by JAX's collectives and lax.ppermute only.
A program may use at most 128 MiB of HBM per device.

```python
import math
import jax
import jax.numpy as jnp
from jax import lax

K = 8192
R = 768
ROUNDS = 2
TESTS = 128
DOM_DEV = 4
EX = 12288
DOMAINS = 64
N_BLOCKS = 16


def draw_sketches(key, part):
    key = jax.random.fold_in(key, 11)
    key_base, key_rows, key_cols = jax.random.split(key, 3)
    base = jnp.clip(jax.random.normal(key_base, (EX, K), jnp.float32), -6.0, 6.0)
    row_scale = jnp.exp(jax.random.uniform(key_rows, (EX, 1), jnp.float32, math.log(0.3), math.log(3.0)))
    col_scale = jnp.exp(jax.random.uniform(key_cols, (1, K), jnp.float32, math.log(0.3), math.log(3.0)))
    return (base * row_scale * col_scale).astype(jnp.bfloat16)


def draw_test_sketches(key, part):
    key = jax.random.fold_in(key, 23)
    key_base, key_rows, key_cols = jax.random.split(key, 3)
    base = jnp.clip(jax.random.normal(key_base, (TESTS, K), jnp.float32), -6.0, 6.0)
    row_scale = jnp.exp(jax.random.uniform(key_rows, (TESTS, 1), jnp.float32, math.log(0.3), math.log(3.0)))
    col_scale = jnp.exp(jax.random.uniform(key_cols, (1, K), jnp.float32, math.log(0.3), math.log(3.0)))
    return (base * row_scale * col_scale).astype(jnp.bfloat16)


def touch_ends(array, own_key, smallest, high):
    place = [jax.random.randint(jax.random.fold_in(own_key, axis), (), 0, length) for axis, length in enumerate(array.shape)]
    longest = array.shape.index(max(array.shape))
    neighbour = place[:longest] + [(place[longest] + 1) % array.shape[longest]] + place[longest + 1:]
    return array.at[tuple(place)].set(smallest).at[tuple(neighbour)].set(high)


def setup_inputs(seed: int = 0, part: int = 0) -> dict:
    arg_keys = jax.random.split(jax.random.key(seed), 4)
    own_keys = jax.random.split(jax.random.fold_in(arg_keys[3], part), 4)
    sketches = draw_sketches(jax.random.fold_in(jax.random.fold_in(arg_keys[3], part), 71), part)
    test_sketches = draw_test_sketches(jax.random.fold_in(arg_keys[3], 71), part)
    domain_map = touch_ends(jax.random.randint(own_keys[2], (EX,), 0, DOMAINS), jax.random.fold_in(own_keys[2], 1), 0, DOMAINS - 1).astype(jnp.int32)
    return {"sketches": sketches, "test_sketches": test_sketches, "domain_map": domain_map}


def inverse_norm(matrix):
    values = matrix.astype(jnp.float32)
    return lax.rsqrt(lax.optimization_barrier(jnp.mean(values * values, axis=1)) + 1e-06)

def cross_tile(left, right, left_inverse, right_inverse):
    product = lax.dot_general(left, right, (((1,), (1,)), ((), ())), preferred_element_type=jnp.float32)
    return product * left_inverse[:, None] * right_inverse[None, :] * (1.0 / math.sqrt(K))

def reference(sketches, test_sketches, domain_map):
    stacked = sketches.reshape(N_BLOCKS, R, K)
    inverse = lax.map(inverse_norm, stacked)
    block_ids = jnp.arange(N_BLOCKS, dtype=jnp.int32)
    all_tiles = []
    mass = jnp.zeros((N_BLOCKS, R), jnp.float32)
    for offset in range(1, ROUNDS + 1):

        def one_block(index, offset=offset):
            other = ((index - offset) % N_BLOCKS).astype(jnp.int32)
            return cross_tile(stacked[index], stacked[other], inverse[index], inverse[other])
        tiles_now = lax.map(one_block, block_ids)
        squared = tiles_now * tiles_now
        mass = mass + lax.optimization_barrier(jnp.sum(squared, axis=2)) + jnp.roll(lax.optimization_barrier(jnp.sum(squared, axis=1)), -offset, axis=0)
        all_tiles.append(tiles_now.reshape(EX, R))
    gram_tiles = jnp.stack(all_tiles)
    redundancy = (mass / float(2 * ROUNDS * R)).reshape(EX)
    test_inverse = inverse_norm(test_sketches)
    domains_by_block = domain_map.reshape(N_BLOCKS, R)
    domain_ids = jnp.arange(DOMAINS, dtype=jnp.int32)

    def domain_block(index):
        similarity = cross_tile(stacked[index], test_sketches, inverse[index], test_inverse).astype(jnp.bfloat16)
        members = (domains_by_block[index][:, None] == domain_ids[None, :]).astype(jnp.bfloat16)
        return lax.dot_general(members, similarity, (((0,), (0,)), ((), ())), preferred_element_type=jnp.float32)
    totals = lax.optimization_barrier(jnp.sum(lax.map(domain_block, block_ids), axis=0))
    domain_scores = totals * (1.0 / math.sqrt(R / DOM_DEV))
    return (gram_tiles, redundancy, domain_scores)
```

```python
import functools
import math

import jax
import jax.numpy as jnp
from jax import lax
from jax.experimental import pallas as pl
from jax.experimental.pallas import tpu as pltpu
from jax.sharding import PartitionSpec as P

ROUNDS = 2
DOM_DEV = 4
LATE = 128
DEPTH = 512
NT = (((1,), (1,)), ((), ()))


def send(value, pairs):
    return lax.ppermute(value, "blocks", pairs)


def inverse_norm(matrix):
    values = matrix.astype(jnp.float32)
    return lax.rsqrt(jnp.mean(values * values, axis=1) + 1e-06)


def nt(left, right):
    return lax.dot_general(left, right, NT, preferred_element_type=jnp.float32)


def early_kernel(place, own, partner, near, other, u_out, v_out, x_out, s, w, u, v, x):
    step = pl.program_id(0)
    upper = place[0] == 1

    @pl.when(step == 0)
    def _():
        for total in (u, v, x):
            total[...] = jnp.zeros_like(total)

    s[...] = jnp.where(upper, near[...], own[...])
    w[...] = jnp.where(upper, own[...], near[...])
    u[...] += nt(partner[...], s[...])
    v[...] += nt(w[...], partner[...])

    @pl.when(place[1] == 0)
    def _():
        x[...] += nt(w[...], other[...])

    @pl.when(place[1] == 1)
    def _():
        x[...] += nt(other[...], s[...])

    @pl.when(step == pl.num_programs(0) - 1)
    def _():
        u_out[...] = u[...].astype(u_out.dtype)
        v_out[...] = v[...].astype(v_out.dtype)
        x_out[...] = x[...].astype(x_out.dtype)


def early_tiles(place, own, partner, near, other):
    early, half = partner.shape
    steps = half // DEPTH
    block = pl.BlockSpec((early, DEPTH), lambda k, place: (0, k))
    mine = pl.BlockSpec((early, DEPTH), lambda k, place: (0, place[0] * steps + k))
    whole = pl.BlockSpec((early, early), lambda k, place: (0, 0))
    tile = jax.ShapeDtypeStruct((early, early), jnp.bfloat16)
    return pl.pallas_call(
        early_kernel,
        grid_spec=pltpu.PrefetchScalarGridSpec(
            num_scalar_prefetch=1,
            grid=(steps,),
            in_specs=[mine, block, block, block],
            out_specs=[whole] * 3,
            scratch_shapes=[pltpu.VMEM((early, DEPTH), jnp.bfloat16)] * 2
            + [pltpu.VMEM((early, early), jnp.float32)] * 3,
        ),
        out_shape=[tile] * 3,
        compiler_params=pltpu.CompilerParams(vmem_limit_bytes=40 * 2**20),
        cost_estimate=pl.CostEstimate(
            flops=6 * early * early * half, bytes_accessed=8 * early * half, transcendentals=0
        ),
    )(place, own, partner, near, other)


def late_kernel(
    place, own1, own2, partner1, partner2, near1, near2, other1, other2,
    u_out, v_out, x_out, s, w, ur, uc, vr, vc, xr, xc,
):
    step = pl.program_id(0)
    upper = place[0] == 1
    early = own1.shape[0]

    @pl.when(step == 0)
    def _():
        for total in (ur, uc, vr, vc, xr, xc):
            total[...] = jnp.zeros_like(total)

    s[:early] = jnp.where(upper, near1[...], own1[...])
    s[early:] = jnp.where(upper, near2[...], own2[...])
    w[:early] = jnp.where(upper, own1[...], near1[...])
    w[early:] = jnp.where(upper, own2[...], near2[...])
    ur[...] += nt(partner2[...], s[...])
    uc[...] += nt(partner1[...], s[early:])
    vr[:, :early] += nt(w[early:], partner1[...])
    vr[:, early:] += nt(w[early:], partner2[...])
    vc[...] += nt(w[:early], partner2[...])

    @pl.when(place[1] == 0)
    def _():
        xr[:, :early] += nt(w[early:], other1[...])
        xr[:, early:] += nt(w[early:], other2[...])
        xc[...] += nt(w[:early], other2[...])

    @pl.when(place[1] == 1)
    def _():
        xr[...] += nt(other2[...], s[...])
        xc[...] += nt(other1[...], s[early:])

    @pl.when(step == pl.num_programs(0) - 1)
    def _():
        for out, rows, columns in ((u_out, ur, uc), (v_out, vr, vc), (x_out, xr, xc)):
            late, width = rows.shape
            out[:, :width] = rows[...].astype(out.dtype)
            for j in range(early // late):
                out[:, width + j * late : width + (j + 1) * late] = columns[
                    j * late : (j + 1) * late
                ].astype(out.dtype)


def late_tiles(place, own, partner1, partner2, near1, near2, other1, other2):
    early, half = partner1.shape
    late = partner2.shape[0]
    rows = early + late
    steps = half // DEPTH
    block1 = pl.BlockSpec((early, DEPTH), lambda k, place: (0, k))
    block2 = pl.BlockSpec((late, DEPTH), lambda k, place: (0, k))
    mine1 = pl.BlockSpec((early, DEPTH), lambda k, place: (0, place[0] * steps + k))
    mine2 = pl.BlockSpec((late, DEPTH), lambda k, place: (early // late, place[0] * steps + k))
    whole = pl.BlockSpec((late, rows + early), lambda k, place: (0, 0))
    out = jax.ShapeDtypeStruct((late, rows + early), jnp.bfloat16)
    totals = [pltpu.VMEM((late, rows), jnp.float32), pltpu.VMEM((early, late), jnp.float32)]
    return pl.pallas_call(
        late_kernel,
        grid_spec=pltpu.PrefetchScalarGridSpec(
            num_scalar_prefetch=1,
            grid=(steps,),
            in_specs=[mine1, mine2] + [block1, block2] * 3,
            out_specs=[whole] * 3,
            scratch_shapes=[pltpu.VMEM((rows, DEPTH), jnp.bfloat16)] * 2 + totals * 3,
        ),
        out_shape=[out] * 3,
        compiler_params=pltpu.CompilerParams(vmem_limit_bytes=40 * 2**20),
        cost_estimate=pl.CostEstimate(
            flops=6 * late * (rows + early) * half, bytes_accessed=8 * rows * half, transcendentals=0
        ),
    )(place, own, own, partner1, partner2, near1, near2, other1, other2)


def join_kernel(
    scale, place, u1, u2r, u2c, v1, v2r, v2c, y1, y2r, y2c, z1, z2r, z2c, local,
    inverse, behind1, behind2, gram, row_mass, column_mass,
):
    step = pl.program_id(0)
    last = pl.num_programs(0) - 1
    early = u1.shape[1]

    @pl.when(step == 0)
    def _():
        column_mass[...] = jnp.zeros_like(column_mass)

    def f32(ref):
        return ref[...].astype(jnp.float32)

    @pl.when(step < last)
    def _():
        gram[0, :, :early] = f32(y1) + f32(z1)
        gram[0, :, early:] = f32(y2c) + f32(z2c)
        gram[1, :, :early] = f32(u1) + f32(v1)
        gram[1, :, early:] = f32(u2c) + f32(v2c)

    @pl.when(step == last)
    def _():
        gram[0] = f32(y2r) + f32(z2r)
        gram[1] = f32(u2r) + f32(v2r)

    first = jnp.where(place[1] == 1, local[...], gram[0])
    left = inverse[...]
    first = first * left * behind1[...] * scale
    second = gram[1] * left * behind2[...] * scale
    gram[0] = first
    gram[1] = second
    first2 = first * first
    second2 = second * second
    column_mass[0:1] += jnp.sum(first2, axis=0, keepdims=True)
    column_mass[1:2] += jnp.sum(second2, axis=0, keepdims=True)
    sums = jnp.sum(first2 + second2, axis=1, keepdims=True)
    size = sums.shape[0]
    row_mass[...] = jnp.broadcast_to(sums, (size, size)).T[0:1]


def join(scale, place, u, v, y, z, local, inverse, behind1, behind2):
    early = u[0].shape[0]
    late = u[1].shape[0]
    rows = early + late
    last = early // late - 1
    first = pl.BlockSpec((late, early), lambda j, place: (jnp.minimum(j, last), 0))
    bottom = pl.BlockSpec((late, rows), lambda j, place: (0, 0))
    side = pl.BlockSpec((late, late), lambda j, place: (0, rows // late + jnp.minimum(j, last)))
    by_rows = pl.BlockSpec((late, rows), lambda j, place: (j, 0))
    column = pl.BlockSpec((late, 1), lambda j, place: (j, 0))
    row = pl.BlockSpec((1, rows), lambda j, place: (0, 0))
    operands = [part for first_, second_ in (u, v, y, z) for part in (first_, second_, second_)]
    return pl.pallas_call(
        functools.partial(join_kernel, scale),
        grid_spec=pltpu.PrefetchScalarGridSpec(
            num_scalar_prefetch=1,
            grid=(rows // late,),
            in_specs=[first, bottom, side] * 4 + [by_rows, column, row, row],
            out_specs=[
                pl.BlockSpec((2, late, rows), lambda j, place: (0, j, 0)),
                pl.BlockSpec((1, late), lambda j, place: (0, j)),
                pl.BlockSpec((2, rows), lambda j, place: (0, 0)),
            ],
        ),
        out_shape=[
            jax.ShapeDtypeStruct((2, rows, rows), jnp.float32),
            jax.ShapeDtypeStruct((1, rows), jnp.float32),
            jax.ShapeDtypeStruct((2, rows), jnp.float32),
        ],
        compiler_params=pltpu.CompilerParams(vmem_limit_bytes=40 * 2**20),
        cost_estimate=pl.CostEstimate(
            flops=20 * rows * rows, bytes_accessed=20 * rows * rows, transcendentals=0
        ),
    )(place, *operands, local, inverse[:, None], behind1[None, :], behind2[None, :])


def scatter_sum(value, index, size, waits):
    bit = size // 2
    for wait in waits:
        half = value.shape[0] // 2
        mine = (index // bit) % 2
        away = lax.dynamic_slice_in_dim(value, (1 - mine) * half, half)
        kept = lax.dynamic_slice_in_dim(value, mine * half, half)
        if wait is not None:
            away, _ = lax.optimization_barrier((away, wait))
        value = kept + send(away, [(i, i ^ bit) for i in range(size)])
        bit //= 2
    return value


def local(sketches, test_sketches, domain_map):
    rows, depth = sketches.shape
    size = lax.axis_size("blocks")
    index = lax.axis_index("blocks")
    half = depth // 2
    early = rows - LATE
    blocks = range(size)
    upper = (index // 2) % 2
    core = index % 2
    place = jnp.stack([upper, core]).astype(jnp.int32)

    across = [(i, i ^ 2) for i in blocks]
    along = [(i, (i + (4 if i & 2 else -4)) % size) for i in blocks]
    swap = [(i, i ^ 1) for i in blocks]

    def part(start, count, side):
        return lax.dynamic_slice(sketches, (start, side * half), (count, half))

    partner1 = send(part(0, early, 1 - upper), across)
    near1 = send(part(0, early, upper), along)
    partner2 = send(part(early, LATE, 1 - upper), across)
    near2 = send(part(early, LATE, upper), along)
    even = send(sketches, [(i, i + 1) for i in blocks if i % 2 == 0])

    inverse = inverse_norm(sketches)
    behind1 = send(inverse, [(i, (i + 1) % size) for i in blocks])
    behind2 = send(inverse, [(i, (i + 2) % size) for i in blocks])
    scale = 1.0 / math.sqrt(depth)

    test_inverse = inverse_norm(test_sketches)
    similarity = (
        nt(sketches, test_sketches) * inverse[:, None] * test_inverse[None, :] * scale
    ).astype(jnp.bfloat16)
    members = (
        domain_map[:, None] == lax.iota(jnp.int32, DOM_DEV * size)[None, :]
    ).astype(jnp.bfloat16)
    sums = lax.dot_general(
        members, similarity, (((0,), (0,)), ((), ())), preferred_element_type=jnp.float32
    )
    inside = nt(sketches, even)

    other1 = send(partner1, swap)
    other2 = send(partner2, swap)

    u1, v1, x1 = early_tiles(place, sketches, partner1, near1, other1)
    u2, v2, x2 = late_tiles(
        place, sketches, partner1, partner2, near1, near2, other1, other2
    )

    back_v = [(i, i) if i & 2 else (i, (i + 4) % size) for i in blocks]
    back_y = [(i, i ^ 3) for i in blocks if i & 1]
    back_z = [pair for pair in back_v if pair[0] % 2 == 0]
    u1r, y1, v1r, z1 = send(u1, across), send(x1, back_y), send(v1, back_v), send(x1, back_z)
    u2r, y2, v2r, z2 = send(u2, across), send(x2, back_y), send(v2, back_v), send(x2, back_z)

    bits = size.bit_length() - 1
    waits = ([None, partner1, partner2, u1r] + [u1r] * bits)[:bits]
    domain_scores = scatter_sum(sums, index, size, waits) * (1.0 / math.sqrt(rows / DOM_DEV))

    gram, row_mass, column_mass = join(
        scale, place, (u1r, u2r), (v1r, v2r), (y1, y2), (z1, z2), inside, inverse, behind1, behind2
    )
    mass = (
        row_mass[0]
        + send(column_mass[0], [(i, (i - 1) % size) for i in blocks])
        + send(column_mass[1], [(i, (i - 2) % size) for i in blocks])
    )
    redundancy = mass / float(2 * ROUNDS * rows)
    return (gram, redundancy, domain_scores)


def solution(mesh):
    in_specs = (P(("groups", "blocks"), None), P(), P(("groups", "blocks")))
    out_specs = (
        P(None, ("groups", "blocks"), None),
        P(("groups", "blocks")),
        P(("groups", "blocks"), None),
    )
    return jax.shard_map(local, mesh=mesh, in_specs=in_specs, out_specs=out_specs, check_vma=False)
```

```python
import functools
import math

import jax
import jax.numpy as jnp
from jax import lax
from jax.experimental import pallas as pl
from jax.experimental.pallas import tpu as pltpu
from jax.sharding import PartitionSpec as P

ROUNDS = 2
DOM_DEV = 4
LATE = 256
DEPTH = 1024
NT = (((1,), (1,)), ((), ()))
VMEM_LIMIT = 48 * 2**20


def send(value, pairs):
    return lax.ppermute(value, "blocks", pairs)


def after(value, *others):
    return lax.optimization_barrier((value, *others))[0]


def inverse_norm(matrix):
    values = matrix.astype(jnp.float32)
    return lax.rsqrt(jnp.mean(values * values, axis=1) + 1e-06)


def nt(left, right):
    return lax.dot_general(left, right, NT, preferred_element_type=jnp.float32)


def params():
    return pltpu.CompilerParams(vmem_limit_bytes=VMEM_LIMIT)


def cost(flops, bytes_accessed):
    return pl.CostEstimate(flops=flops, bytes_accessed=bytes_accessed, transcendentals=0)


def clear(*totals):
    @pl.when(pl.program_id(0) == 0)
    def _():
        for total in totals:
            total[...] = jnp.zeros_like(total)


def at_end(body):
    pl.when(pl.program_id(0) == pl.num_programs(0) - 1)(body)


def early_kernel(place, own, partner, near, u_out, v_out, u, v):
    clear(u, v)

    @pl.when(place[0] == 0)
    def _():
        u[...] += nt(partner[...], own[...])
        v[...] += nt(near[...], partner[...])

    @pl.when(place[0] == 1)
    def _():
        u[...] += nt(partner[...], near[...])
        v[...] += nt(own[...], partner[...])

    @at_end
    def _():
        u_out[...] = u[...].astype(u_out.dtype)
        v_out[...] = v[...].astype(v_out.dtype)


def early_tiles(place, own, partner, near):
    early, half = partner.shape
    steps = half // DEPTH
    block = pl.BlockSpec((early, DEPTH), lambda k, place: (0, k))
    mine = pl.BlockSpec((early, DEPTH), lambda k, place: (0, place[0] * steps + k))
    whole = pl.BlockSpec((early, early), lambda k, place: (0, 0))
    return pl.pallas_call(
        early_kernel,
        grid_spec=pltpu.PrefetchScalarGridSpec(
            num_scalar_prefetch=1,
            grid=(steps,),
            in_specs=[mine, block, block],
            out_specs=[whole] * 2,
            scratch_shapes=[pltpu.VMEM((early, early), jnp.float32)] * 2,
        ),
        out_shape=[jax.ShapeDtypeStruct((early, early), jnp.bfloat16)] * 2,
        compiler_params=params(),
        cost_estimate=cost(early, early),
    )(place, own, partner, near)


def late_kernel(
    place, own1, own2, partner1, partner2, near1, near2, u_out, v_out, ur, uc, vr, vc
):
    clear(ur, uc, vr, vc)
    early = own1.shape[0]

    def add(s1, s2, w1, w2):
        ur[:, :early] += nt(partner2[...], s1[...])
        ur[:, early:] += nt(partner2[...], s2[...])
        uc[...] += nt(partner1[...], s2[...])
        vr[:, :early] += nt(w2[...], partner1[...])
        vr[:, early:] += nt(w2[...], partner2[...])
        vc[...] += nt(w1[...], partner2[...])

    @pl.when(place[0] == 0)
    def _():
        add(own1, own2, near1, near2)

    @pl.when(place[0] == 1)
    def _():
        add(near1, near2, own1, own2)

    @at_end
    def _():
        for out, rows, columns in ((u_out, ur, uc), (v_out, vr, vc)):
            late, width = rows.shape
            out[:, :width] = rows[...].astype(out.dtype)
            for j in range(early // late):
                out[:, width + j * late : width + (j + 1) * late] = columns[
                    j * late : (j + 1) * late
                ].astype(out.dtype)


def late_tiles(place, own, partner1, partner2, near1, near2):
    early, half = partner1.shape
    late = partner2.shape[0]
    rows = early + late
    steps = half // DEPTH
    block1 = pl.BlockSpec((early, DEPTH), lambda k, place: (0, k))
    block2 = pl.BlockSpec((late, DEPTH), lambda k, place: (0, k))
    mine1 = pl.BlockSpec((early, DEPTH), lambda k, place: (0, place[0] * steps + k))
    mine2 = pl.BlockSpec((late, DEPTH), lambda k, place: (early // late, place[0] * steps + k))
    whole = pl.BlockSpec((late, rows + early), lambda k, place: (0, 0))
    totals = [pltpu.VMEM((late, rows), jnp.float32), pltpu.VMEM((early, late), jnp.float32)]
    return pl.pallas_call(
        late_kernel,
        grid_spec=pltpu.PrefetchScalarGridSpec(
            num_scalar_prefetch=1,
            grid=(steps,),
            in_specs=[mine1, mine2] + [block1, block2] * 2,
            out_specs=[whole] * 2,
            scratch_shapes=totals * 2,
        ),
        out_shape=[jax.ShapeDtypeStruct((late, rows + early), jnp.bfloat16)] * 2,
        compiler_params=params(),
        cost_estimate=cost(4 * late * (rows + early) * half, 6 * rows * half),
    )(place, own, own, partner1, partner2, near1, near2)


def cross_kernel(place, own, near1, near2, other1, other2, out, x):
    clear(x)
    early = near1.shape[0]
    first, second = slice(None, early), slice(early, None)
    near = ((first, near1), (second, near2))
    other = ((first, other1), (second, other2))
    mine = ((slice(None), own),)

    def add(left, right):
        for rows, left_ref in left:
            for columns, right_ref in right:
                x[rows, columns] += nt(left_ref[...], right_ref[...])

    code = place[0] * 2 + place[1]
    for number, pair in enumerate(((near, other), (other, mine), (mine, other), (other, near))):

        @pl.when(code == number)
        def _(pair=pair):
            add(*pair)

    @at_end
    def _():
        out[...] = x[...].astype(out.dtype)


def cross_tile(place, own, near1, near2, other1, other2):
    early, half = near1.shape
    late = near2.shape[0]
    rows = early + late
    steps = half // DEPTH
    block1 = pl.BlockSpec((early, DEPTH), lambda k, place: (0, k))
    block2 = pl.BlockSpec((late, DEPTH), lambda k, place: (0, k))
    mine = pl.BlockSpec((rows, DEPTH), lambda k, place: (0, place[0] * steps + k))
    return pl.pallas_call(
        cross_kernel,
        grid_spec=pltpu.PrefetchScalarGridSpec(
            num_scalar_prefetch=1,
            grid=(steps,),
            in_specs=[mine] + [block1, block2] * 2,
            out_specs=pl.BlockSpec((rows, rows), lambda k, place: (0, 0)),
            scratch_shapes=[pltpu.VMEM((rows, rows), jnp.float32)],
        ),
        out_shape=jax.ShapeDtypeStruct((rows, rows), jnp.bfloat16),
        compiler_params=params(),
        cost_estimate=cost(2 * rows * rows * half, 6 * rows * half),
    )(place, own, near1, near2, other1, other2)


def finish(tile, row_mass, column_mass):
    @pl.when(pl.program_id(0) == 0)
    def _():
        column_mass[...] = jnp.zeros_like(column_mass)

    squared = tile * tile
    column_mass[...] += jnp.sum(squared, axis=0, keepdims=True)
    sums = jnp.sum(squared, axis=1, keepdims=True)
    size = sums.shape[0]
    row_mass[...] = jnp.broadcast_to(sums, (size, size)).T[0:1]


def second_kernel(
    scale, u1, u2r, u2c, v1, v2r, v2c, inverse, behind, gram, row_mass, column_mass
):
    step = pl.program_id(0)
    last = pl.num_programs(0) - 1
    early = u1.shape[1]

    def f32(ref):
        return ref[...].astype(jnp.float32)

    @pl.when(step < last)
    def _():
        gram[0, :, :early] = f32(u1) + f32(v1)
        gram[0, :, early:] = f32(u2c) + f32(v2c)

    @pl.when(step == last)
    def _():
        gram[0] = f32(u2r) + f32(v2r)

    tile = gram[0] * inverse[...] * behind[...] * scale
    gram[0] = tile
    finish(tile, row_mass, column_mass)


def mass_shapes(rows, late):
    specs = [
        pl.BlockSpec((1, late), lambda j, *_: (0, j)),
        pl.BlockSpec((1, rows), lambda j, *_: (0, 0)),
    ]
    return specs, [jax.ShapeDtypeStruct((1, rows), jnp.float32)] * 2


def second_tiles(scale, u1, u2, v1, v2, inverse, behind):
    early = u1.shape[0]
    late = u2.shape[0]
    rows = early + late
    last = early // late - 1
    first = pl.BlockSpec((late, early), lambda j: (jnp.minimum(j, last), 0))
    bottom = pl.BlockSpec((late, rows), lambda j: (0, 0))
    side = pl.BlockSpec((late, late), lambda j: (0, rows // late + jnp.minimum(j, last)))
    mass_specs, mass_types = mass_shapes(rows, late)
    return pl.pallas_call(
        functools.partial(second_kernel, scale),
        grid=(rows // late,),
        in_specs=[first, bottom, side] * 2
        + [
            pl.BlockSpec((late, 1), lambda j: (j, 0)),
            pl.BlockSpec((1, rows), lambda j: (0, 0)),
        ],
        out_specs=[pl.BlockSpec((1, late, rows), lambda j: (1, j, 0))] + mass_specs,
        out_shape=[jax.ShapeDtypeStruct((2, rows, rows), jnp.float32)] + mass_types,
        compiler_params=params(),
        cost_estimate=cost(8 * rows * rows, 160 * rows * rows),
    )(u1, u2, u2, v1, v2, v2, inverse[:, None], behind[None, :])


def first_kernel(
    scale, place, y, z, local, inverse, behind, gram_in, gram, row_mass, column_mass
):
    del gram_in
    summed = y[...].astype(jnp.float32) + z[...].astype(jnp.float32)
    tile = jnp.where(place[1] == 1, local[...], summed)
    tile = tile * inverse[...] * behind[...] * scale
    gram[0] = tile
    finish(tile, row_mass, column_mass)


def first_tiles(scale, place, y, z, local, inverse, behind, gram, late):
    rows = y.shape[0]
    block = pl.BlockSpec((late, rows), lambda j, place: (j, 0))
    mass_specs, mass_types = mass_shapes(rows, late)
    return pl.pallas_call(
        functools.partial(first_kernel, scale),
        grid_spec=pltpu.PrefetchScalarGridSpec(
            num_scalar_prefetch=1,
            grid=(rows // late,),
            in_specs=[block] * 3
            + [
                pl.BlockSpec((late, 1), lambda j, place: (j, 0)),
                pl.BlockSpec((1, rows), lambda j, place: (0, 0)),
                pl.BlockSpec(memory_space=pl.ANY),
            ],
            out_specs=[pl.BlockSpec((1, late, rows), lambda j, place: (0, j, 0))] + mass_specs,
        ),
        out_shape=[jax.ShapeDtypeStruct((2, rows, rows), jnp.float32)] + mass_types,
        input_output_aliases={6: 0},
        compiler_params=params(),
        cost_estimate=cost(8 * rows * rows, 12 * rows * rows),
    )(place, y, z, local, inverse[:, None], behind[None, :], gram)


def scatter_sum(value, index, size, waits):
    bit = size // 2
    for wait in waits:
        half = value.shape[0] // 2
        mine = (index // bit) % 2
        away = lax.dynamic_slice_in_dim(value, (1 - mine) * half, half)
        kept = lax.dynamic_slice_in_dim(value, mine * half, half)
        if wait is not None:
            away = after(away, wait)
        value = kept + send(away, [(i, i ^ bit) for i in range(size)])
        bit //= 2
    return value


def local(sketches, test_sketches, domain_map):
    rows, depth = sketches.shape
    size = lax.axis_size("blocks")
    index = lax.axis_index("blocks")
    half = depth // 2
    early = rows - LATE
    blocks = range(size)
    upper = (index // 2) % 2
    core = index % 2
    place = jnp.stack([upper, core]).astype(jnp.int32)

    across = [(i, i ^ 2) for i in blocks]
    along = [(i, (i + (4 if i & 2 else -4)) % size) for i in blocks]
    swap = [(i, i ^ 1) for i in blocks]

    def part(source, start, count, side):
        return lax.dynamic_slice(source, (start, side * half), (count, half))

    out1 = part(sketches, 0, early, 1 - upper)
    partner1 = send(out1, across)
    source = after(sketches, out1)
    side1 = part(source, 0, early, upper)
    near1 = send(side1, along)
    source = after(source, side1)
    partner2 = send(part(source, early, LATE, 1 - upper), across)
    near2 = send(part(source, early, LATE, upper), along)
    even = send(sketches, [(i, i + 1) for i in blocks if i % 2 == 0])

    inverse = inverse_norm(sketches)
    behind1 = send(inverse, [(i, (i + 1) % size) for i in blocks])
    behind2 = send(inverse, [(i, (i + 2) % size) for i in blocks])
    scale = 1.0 / math.sqrt(depth)

    test_inverse = inverse_norm(test_sketches)
    similarity = (
        nt(sketches, test_sketches) * inverse[:, None] * test_inverse[None, :] * scale
    ).astype(jnp.bfloat16)
    members = (
        domain_map[:, None] == lax.iota(jnp.int32, DOM_DEV * size)[None, :]
    ).astype(jnp.bfloat16)
    sums = lax.dot_general(
        members, similarity, (((0,), (0,)), ((), ())), preferred_element_type=jnp.float32
    )
    inside = nt(sketches, even)

    partner1 = after(partner1, inside, sums)
    u1, v1 = early_tiles(place, sketches, partner1, near1)
    other1 = send(partner1, swap)
    partner2 = after(partner2, u1, behind1, behind2)
    other2 = send(partner2, swap)
    u2, v2 = late_tiles(place, sketches, partner1, partner2, near1, after(near2, u1))
    x = cross_tile(place, sketches, near1, near2, other1, after(other2, u2))

    back_v = [(i, i) if i & 2 else (i, (i + 4) % size) for i in blocks]
    back_y = [(i, i ^ 3) for i in blocks if i & 1]
    back_z = [pair for pair in back_v if pair[0] % 2 == 0]
    u1r, v1r = send(u1, across), send(v1, back_v)
    u2r, v2r = send(u2, across), send(v2, back_v)
    y, z = send(x, back_y), send(x, back_z)

    bits = size.bit_length() - 1
    waits = ([None, u1, u2, x] + [x] * bits)[:bits]
    domain_scores = scatter_sum(sums, index, size, waits) * (1.0 / math.sqrt(rows / DOM_DEV))

    gram, row_mass2, column_mass2 = second_tiles(scale, u1r, u2r, v1r, v2r, inverse, behind2)
    gram, row_mass1, column_mass1 = first_tiles(
        scale, place, y, z, inside, inverse, behind1, gram, LATE
    )
    mass = (
        row_mass1[0]
        + row_mass2[0]
        + send(column_mass1[0], [(i, (i - 1) % size) for i in blocks])
        + send(column_mass2[0], [(i, (i - 2) % size) for i in blocks])
    )
    redundancy = mass / float(2 * ROUNDS * rows)
    return (gram, redundancy, domain_scores)


def solution(mesh):
    in_specs = (P(("groups", "blocks"), None), P(), P(("groups", "blocks")))
    out_specs = (
        P(None, ("groups", "blocks"), None),
        P(("groups", "blocks")),
        P(("groups", "blocks"), None),
    )
    return jax.shard_map(local, mesh=mesh, in_specs=in_specs, out_specs=out_specs, check_vma=False)
```

```python
import functools
import math

import jax
import jax.numpy as jnp
from jax import lax
from jax.experimental import pallas as pl
from jax.experimental.pallas import tpu as pltpu
from jax.sharding import PartitionSpec as P

ROUNDS = 2
DOM_DEV = 4
LATE = 256
DEPTH = 1024
NT = (((1,), (1,)), ((), ()))
VMEM_LIMIT = 48 * 2**20


def send(value, pairs):
    return lax.ppermute(value, "blocks", pairs)


def after(value, *others):
    return lax.optimization_barrier((value, *others))[0]


def inverse_norm(matrix):
    values = matrix.astype(jnp.float32)
    return lax.rsqrt(jnp.mean(values * values, axis=1) + 1e-06)


def nt(left, right):
    return lax.dot_general(left, right, NT, preferred_element_type=jnp.float32)


def params():
    return pltpu.CompilerParams(vmem_limit_bytes=VMEM_LIMIT)


def cost(flops, bytes_accessed):
    return pl.CostEstimate(flops=flops, bytes_accessed=bytes_accessed, transcendentals=0)


def clear(*totals):
    @pl.when(pl.program_id(0) == 0)
    def _():
        for total in totals:
            total[...] = jnp.zeros_like(total)


def at_end(body):
    pl.when(pl.program_id(0) == pl.num_programs(0) - 1)(body)


def early_kernel(place, own, partner, near, u_out, v_out, u, v):
    clear(u, v)

    @pl.when(place[0] == 0)
    def _():
        u[...] += nt(partner[...], own[...])
        v[...] += nt(near[...], partner[...])

    @pl.when(place[0] == 1)
    def _():
        u[...] += nt(partner[...], near[...])
        v[...] += nt(own[...], partner[...])

    @at_end
    def _():
        u_out[...] = u[...].astype(u_out.dtype)
        v_out[...] = v[...].astype(v_out.dtype)


def early_tiles(place, own, partner, near):
    early, half = partner.shape
    steps = half // DEPTH
    block = pl.BlockSpec((early, DEPTH), lambda k, place: (0, k))
    mine = pl.BlockSpec((early, DEPTH), lambda k, place: (0, place[0] * steps + k))
    whole = pl.BlockSpec((early, early), lambda k, place: (0, 0))
    return pl.pallas_call(
        early_kernel,
        grid_spec=pltpu.PrefetchScalarGridSpec(
            num_scalar_prefetch=1,
            grid=(steps,),
            in_specs=[mine, block, block],
            out_specs=[whole] * 2,
            scratch_shapes=[pltpu.VMEM((early, early), jnp.float32)] * 2,
        ),
        out_shape=[jax.ShapeDtypeStruct((early, early), jnp.bfloat16)] * 2,
        compiler_params=params(),
        cost_estimate=cost(early, early),
    )(place, own, partner, near)


def late_kernel(
    place, own1, own2, partner1, partner2, near1, near2, u_out, v_out, ur, uc, vr, vc
):
    clear(ur, uc, vr, vc)
    early = own1.shape[0]

    def add(s1, s2, w1, w2):
        ur[:, :early] += nt(partner2[...], s1[...])
        ur[:, early:] += nt(partner2[...], s2[...])
        uc[...] += nt(partner1[...], s2[...])
        vr[:, :early] += nt(w2[...], partner1[...])
        vr[:, early:] += nt(w2[...], partner2[...])
        vc[...] += nt(w1[...], partner2[...])

    @pl.when(place[0] == 0)
    def _():
        add(own1, own2, near1, near2)

    @pl.when(place[0] == 1)
    def _():
        add(near1, near2, own1, own2)

    @at_end
    def _():
        for out, rows, columns in ((u_out, ur, uc), (v_out, vr, vc)):
            late, width = rows.shape
            out[:, :width] = rows[...].astype(out.dtype)
            for j in range(early // late):
                out[:, width + j * late : width + (j + 1) * late] = columns[
                    j * late : (j + 1) * late
                ].astype(out.dtype)


def late_tiles(place, own, partner1, partner2, near1, near2):
    early, half = partner1.shape
    late = partner2.shape[0]
    rows = early + late
    steps = half // DEPTH
    block1 = pl.BlockSpec((early, DEPTH), lambda k, place: (0, k))
    block2 = pl.BlockSpec((late, DEPTH), lambda k, place: (0, k))
    mine1 = pl.BlockSpec((early, DEPTH), lambda k, place: (0, place[0] * steps + k))
    mine2 = pl.BlockSpec((late, DEPTH), lambda k, place: (early // late, place[0] * steps + k))
    whole = pl.BlockSpec((late, rows + early), lambda k, place: (0, 0))
    totals = [pltpu.VMEM((late, rows), jnp.float32), pltpu.VMEM((early, late), jnp.float32)]
    return pl.pallas_call(
        late_kernel,
        grid_spec=pltpu.PrefetchScalarGridSpec(
            num_scalar_prefetch=1,
            grid=(steps,),
            in_specs=[mine1, mine2] + [block1, block2] * 2,
            out_specs=[whole] * 2,
            scratch_shapes=totals * 2,
        ),
        out_shape=[jax.ShapeDtypeStruct((late, rows + early), jnp.bfloat16)] * 2,
        compiler_params=params(),
        cost_estimate=cost(4 * late * (rows + early) * half, 6 * rows * half),
    )(place, own, own, partner1, partner2, near1, near2)


def cross_kernel(place, own, near1, near2, other1, other2, out, x):
    clear(x)
    early = near1.shape[0]
    first, second = slice(None, early), slice(early, None)
    near = ((first, near1), (second, near2))
    other = ((first, other1), (second, other2))
    mine = ((slice(None), own),)

    def add(left, right):
        for rows, left_ref in left:
            for columns, right_ref in right:
                x[rows, columns] += nt(left_ref[...], right_ref[...])

    code = place[0] * 2 + place[1]
    for number, pair in enumerate(((near, other), (other, mine), (mine, other), (other, near))):

        @pl.when(code == number)
        def _(pair=pair):
            add(*pair)

    @at_end
    def _():
        out[...] = x[...].astype(out.dtype)


def cross_tile(place, own, near1, near2, other1, other2):
    early, half = near1.shape
    late = near2.shape[0]
    rows = early + late
    steps = half // DEPTH
    block1 = pl.BlockSpec((early, DEPTH), lambda k, place: (0, k))
    block2 = pl.BlockSpec((late, DEPTH), lambda k, place: (0, k))
    mine = pl.BlockSpec((rows, DEPTH), lambda k, place: (0, place[0] * steps + k))
    return pl.pallas_call(
        cross_kernel,
        grid_spec=pltpu.PrefetchScalarGridSpec(
            num_scalar_prefetch=1,
            grid=(steps,),
            in_specs=[mine] + [block1, block2] * 2,
            out_specs=pl.BlockSpec((rows, rows), lambda k, place: (0, 0)),
            scratch_shapes=[pltpu.VMEM((rows, rows), jnp.float32)],
        ),
        out_shape=jax.ShapeDtypeStruct((rows, rows), jnp.bfloat16),
        compiler_params=params(),
        cost_estimate=cost(2 * rows * rows * half, 6 * rows * half),
    )(place, own, near1, near2, other1, other2)


def copy_kernel(place, *refs):
    del place
    count = len(refs) // 2
    for source, target in zip(refs[:count], refs[count:]):
        target[...] = source[...]


def halves(place, own, start, count, sides):
    half = own.shape[1] // 2
    tall = 64
    first = start // tall

    def source(side):
        return pl.BlockSpec((tall, half), lambda i, place: (first + i, (place[0] + side) % 2))

    return pl.pallas_call(
        copy_kernel,
        grid_spec=pltpu.PrefetchScalarGridSpec(
            num_scalar_prefetch=1,
            grid=(count // tall,),
            in_specs=[source(side) for side in sides],
            out_specs=[pl.BlockSpec((tall, half), lambda i, place: (i, 0)) for _ in sides],
        ),
        out_shape=[jax.ShapeDtypeStruct((count, half), own.dtype) for _ in sides],
        compiler_params=params(),
        cost_estimate=cost(0, 4 * count * half * len(sides)),
    )(place, *([own] * len(sides)))


def finish(tile, row_mass, column_mass):
    @pl.when(pl.program_id(0) == 0)
    def _():
        column_mass[...] = jnp.zeros_like(column_mass)

    squared = tile * tile
    column_mass[...] += jnp.sum(squared, axis=0, keepdims=True)
    sums = jnp.sum(squared, axis=1, keepdims=True)
    size = sums.shape[0]
    row_mass[...] = jnp.broadcast_to(sums, (size, size)).T[0:1]


def second_kernel(
    scale, u1, u2r, u2c, v1, v2r, v2c, inverse, behind, gram, row_mass, column_mass
):
    step = pl.program_id(0)
    last = pl.num_programs(0) - 1
    early = u1.shape[1]

    def f32(ref):
        return ref[...].astype(jnp.float32)

    @pl.when(step < last)
    def _():
        gram[0, :, :early] = f32(u1) + f32(v1)
        gram[0, :, early:] = f32(u2c) + f32(v2c)

    @pl.when(step == last)
    def _():
        gram[0] = f32(u2r) + f32(v2r)

    tile = gram[0] * inverse[...] * behind[...] * scale
    gram[0] = tile
    finish(tile, row_mass, column_mass)


def mass_shapes(rows, late):
    specs = [
        pl.BlockSpec((1, late), lambda j, *_: (0, j)),
        pl.BlockSpec((1, rows), lambda j, *_: (0, 0)),
    ]
    return specs, [jax.ShapeDtypeStruct((1, rows), jnp.float32)] * 2


def second_tiles(scale, u1, u2, v1, v2, inverse, behind):
    early = u1.shape[0]
    late = u2.shape[0]
    rows = early + late
    last = early // late - 1
    first = pl.BlockSpec((late, early), lambda j: (jnp.minimum(j, last), 0))
    bottom = pl.BlockSpec((late, rows), lambda j: (0, 0))
    side = pl.BlockSpec((late, late), lambda j: (0, rows // late + jnp.minimum(j, last)))
    mass_specs, mass_types = mass_shapes(rows, late)
    return pl.pallas_call(
        functools.partial(second_kernel, scale),
        grid=(rows // late,),
        in_specs=[first, bottom, side] * 2
        + [
            pl.BlockSpec((late, 1), lambda j: (j, 0)),
            pl.BlockSpec((1, rows), lambda j: (0, 0)),
        ],
        out_specs=[pl.BlockSpec((1, late, rows), lambda j: (1, j, 0))] + mass_specs,
        out_shape=[jax.ShapeDtypeStruct((2, rows, rows), jnp.float32)] + mass_types,
        compiler_params=params(),
        cost_estimate=cost(60000 * rows * rows, 160 * rows * rows),
    )(u1, u2, u2, v1, v2, v2, inverse[:, None], behind[None, :])


def first_kernel(
    scale, place, y, z, local, inverse, behind, gram_in, gram, row_mass, column_mass
):
    del gram_in
    summed = y[...].astype(jnp.float32) + z[...].astype(jnp.float32)
    tile = jnp.where(place[1] == 1, local[...], summed)
    tile = tile * inverse[...] * behind[...] * scale
    gram[0] = tile
    finish(tile, row_mass, column_mass)


def first_tiles(scale, place, y, z, local, inverse, behind, gram, late):
    rows = y.shape[0]
    block = pl.BlockSpec((late, rows), lambda j, place: (j, 0))
    mass_specs, mass_types = mass_shapes(rows, late)
    return pl.pallas_call(
        functools.partial(first_kernel, scale),
        grid_spec=pltpu.PrefetchScalarGridSpec(
            num_scalar_prefetch=1,
            grid=(rows // late,),
            in_specs=[block] * 3
            + [
                pl.BlockSpec((late, 1), lambda j, place: (j, 0)),
                pl.BlockSpec((1, rows), lambda j, place: (0, 0)),
                pl.BlockSpec(memory_space=pl.ANY),
            ],
            out_specs=[pl.BlockSpec((1, late, rows), lambda j, place: (0, j, 0))] + mass_specs,
        ),
        out_shape=[jax.ShapeDtypeStruct((2, rows, rows), jnp.float32)] + mass_types,
        input_output_aliases={6: 0},
        compiler_params=params(),
        cost_estimate=cost(8 * rows * rows, 12 * rows * rows),
    )(place, y, z, local, inverse[:, None], behind[None, :], gram)


def local(sketches, test_sketches, domain_map):
    rows, depth = sketches.shape
    size = lax.axis_size("blocks")
    index = lax.axis_index("blocks")
    half = depth // 2
    early = rows - LATE
    blocks = range(size)
    upper = (index // 2) % 2
    core = index % 2
    place = jnp.stack([upper, core]).astype(jnp.int32)

    across = [(i, i ^ 2) for i in blocks]
    along = [(i, (i + (4 if i & 2 else -4)) % size) for i in blocks]
    swap = [(i, i ^ 1) for i in blocks]

    even = send(sketches, swap)
    (out1,) = halves(place, sketches, 0, early, (1,))
    partner1 = send(out1, across)
    (side1,) = halves(place, after(sketches, out1), 0, early, (0,))
    near1 = send(side1, along)
    out2, side2 = halves(place, after(sketches, side1), early, LATE, (1, 0))
    partner2 = send(out2, across)
    near2 = send(side2, along)

    inverse = inverse_norm(sketches)
    inverses = lax.all_gather(inverse, "blocks")
    scale = 1.0 / math.sqrt(depth)

    test_inverse = inverse_norm(test_sketches)
    similarity = (
        nt(sketches, test_sketches) * inverse[:, None] * test_inverse[None, :] * scale
    ).astype(jnp.bfloat16)
    members = (
        domain_map[:, None] == lax.iota(jnp.int32, DOM_DEV * size)[None, :]
    ).astype(jnp.bfloat16)
    sums = lax.dot_general(
        members, similarity, (((0,), (0,)), ((), ())), preferred_element_type=jnp.float32
    )
    inside = nt(sketches, even)

    grouped = jnp.pad(sums.reshape(size, DOM_DEV, -1), ((0, 0), (0, DOM_DEV), (0, 0)))
    total = lax.psum_scatter(
        grouped.reshape(2 * DOM_DEV * size, -1), "blocks", scatter_dimension=0, tiled=True
    )

    back_v = [(i, i) if i & 2 else (i, (i + 4) % size) for i in blocks]
    back_y = [(i, i ^ 3) for i in blocks if i & 1]
    back_z = [pair for pair in back_v if pair[0] % 2 == 0]
    partner1 = after(partner1, inside, sums)
    u1, v1 = early_tiles(place, sketches, partner1, near1)
    u1r, v1r = send(u1, across), send(v1, back_v)
    other1 = send(partner1, swap)
    partner2, near2, inverses, total, _ = lax.optimization_barrier(
        (partner2, near2, inverses, total, u1)
    )
    behind1 = lax.dynamic_index_in_dim(inverses, (index - 1) % size, 0, False)
    behind2 = lax.dynamic_index_in_dim(inverses, (index - 2) % size, 0, False)
    domain_scores = total[:DOM_DEV] * (1.0 / math.sqrt(rows / DOM_DEV))
    other2 = send(partner2, swap)
    u2, v2 = late_tiles(place, sketches, partner1, partner2, near1, near2)
    u2r, v2r = send(u2, across), send(v2, back_v)
    other2 = lax.optimization_barrier((other2, u2, u1r, v1r))[0]
    x = cross_tile(place, sketches, near1, near2, other1, other2)
    y, z = send(x, back_y), send(x, back_z)

    gram, row_mass2, column_mass2 = second_tiles(scale, u1r, u2r, v1r, v2r, inverse, behind2)
    gram, row_mass1, column_mass1 = first_tiles(
        scale, place, y, z, inside, inverse, behind1, gram, LATE
    )
    mass = (
        row_mass1[0]
        + row_mass2[0]
        + send(column_mass1[0], [(i, (i - 1) % size) for i in blocks])
        + send(column_mass2[0], [(i, (i - 2) % size) for i in blocks])
    )
    redundancy = mass / float(2 * ROUNDS * rows)
    return (gram, redundancy, domain_scores)


def solution(mesh):
    in_specs = (P(("groups", "blocks"), None), P(), P(("groups", "blocks")))
    out_specs = (
        P(None, ("groups", "blocks"), None),
        P(("groups", "blocks")),
        P(("groups", "blocks"), None),
    )
    return jax.shard_map(local, mesh=mesh, in_specs=in_specs, out_specs=out_specs, check_vma=False)
```

```python
import functools
import math

import jax
import jax.numpy as jnp
from jax import lax
from jax.experimental import pallas as pl
from jax.experimental.pallas import tpu as pltpu
from jax.sharding import PartitionSpec as P

ROUNDS = 2
DOM_DEV = 4
LATE = 256
DEPTH = 1024
NT = (((1,), (1,)), ((), ()))
VMEM_LIMIT = 52 * 2**20
PIECES = 4


def send(value, pairs):
    return lax.ppermute(value, "blocks", pairs)


def after(value, *others):
    return lax.optimization_barrier((value, *others))[0]


def inverse_norm(matrix):
    values = matrix.astype(jnp.float32)
    return lax.rsqrt(jnp.mean(values * values, axis=1) + 1e-06)


def nt(left, right):
    return lax.dot_general(left, right, NT, preferred_element_type=jnp.float32)


def params():
    return pltpu.CompilerParams(vmem_limit_bytes=VMEM_LIMIT)


def cost(flops, bytes_accessed):
    return pl.CostEstimate(flops=flops, bytes_accessed=bytes_accessed, transcendentals=0)


def clear(*totals):
    @pl.when(pl.program_id(0) == 0)
    def _():
        for total in totals:
            total[...] = jnp.zeros_like(total)


def at_end(body):
    pl.when(pl.program_id(0) == pl.num_programs(0) - 1)(body)


def early_kernel(place, own, partner, near, u_out, v_out, u, v):
    clear(u, v)

    @pl.when(place[0] == 0)
    def _():
        u[...] += nt(partner[...], own[...])
        v[...] += nt(near[...], partner[...])

    @pl.when(place[0] == 1)
    def _():
        u[...] += nt(partner[...], near[...])
        v[...] += nt(own[...], partner[...])

    @at_end
    def _():
        u_out[...] = u[...].astype(u_out.dtype)
        v_out[...] = v[...].astype(v_out.dtype)


def early_tiles(place, own, partner, near):
    early, half = partner.shape
    steps = half // DEPTH
    block = pl.BlockSpec((early, DEPTH), lambda k, place: (0, k))
    mine = pl.BlockSpec((early, DEPTH), lambda k, place: (0, place[0] * steps + k))
    whole = pl.BlockSpec((early, early), lambda k, place: (0, 0))
    return pl.pallas_call(
        early_kernel,
        grid_spec=pltpu.PrefetchScalarGridSpec(
            num_scalar_prefetch=1,
            grid=(steps,),
            in_specs=[mine, block, block],
            out_specs=[whole] * 2,
            scratch_shapes=[pltpu.VMEM((early, early), jnp.float32)] * 2,
        ),
        out_shape=[jax.ShapeDtypeStruct((early, early), jnp.bfloat16)] * 2,
        compiler_params=params(),
        cost_estimate=cost(early, early),
    )(place, own, partner, near)


def late_kernel(
    place, own1, own2, partner1, partner2, near1, near2, u_out, v_out, ur, uc, vr, vc
):
    clear(ur, uc, vr, vc)
    early = own1.shape[0]

    def add(s1, s2, w1, w2):
        ur[:, :early] += nt(partner2[...], s1[...])
        ur[:, early:] += nt(partner2[...], s2[...])
        uc[...] += nt(partner1[...], s2[...])
        vr[:, :early] += nt(w2[...], partner1[...])
        vr[:, early:] += nt(w2[...], partner2[...])
        vc[...] += nt(w1[...], partner2[...])

    @pl.when(place[0] == 0)
    def _():
        add(own1, own2, near1, near2)

    @pl.when(place[0] == 1)
    def _():
        add(near1, near2, own1, own2)

    @at_end
    def _():
        for out, rows, columns in ((u_out, ur, uc), (v_out, vr, vc)):
            late, width = rows.shape
            out[:, :width] = rows[...].astype(out.dtype)
            for j in range(early // late):
                out[:, width + j * late : width + (j + 1) * late] = columns[
                    j * late : (j + 1) * late
                ].astype(out.dtype)


def late_tiles(place, own, partner1, partner2, near1, near2):
    early, half = partner1.shape
    late = partner2.shape[0]
    rows = early + late
    steps = half // DEPTH
    block1 = pl.BlockSpec((early, DEPTH), lambda k, place: (0, k))
    block2 = pl.BlockSpec((late, DEPTH), lambda k, place: (0, k))
    mine1 = pl.BlockSpec((early, DEPTH), lambda k, place: (0, place[0] * steps + k))
    mine2 = pl.BlockSpec((late, DEPTH), lambda k, place: (early // late, place[0] * steps + k))
    whole = pl.BlockSpec((late, rows + early), lambda k, place: (0, 0))
    totals = [pltpu.VMEM((late, rows), jnp.float32), pltpu.VMEM((early, late), jnp.float32)]
    return pl.pallas_call(
        late_kernel,
        grid_spec=pltpu.PrefetchScalarGridSpec(
            num_scalar_prefetch=1,
            grid=(steps,),
            in_specs=[mine1, mine2] + [block1, block2] * 2,
            out_specs=[whole] * 2,
            scratch_shapes=totals * 2,
        ),
        out_shape=[jax.ShapeDtypeStruct((late, rows + early), jnp.bfloat16)] * 2,
        compiler_params=params(),
        cost_estimate=cost(4 * late * (rows + early) * half, 6 * rows * half),
    )(place, own, own, partner1, partner2, near1, near2)


def cross_kernel(place, own, near1, near2, other1, other2, out, x):
    clear(x)
    early = near1.shape[0]
    first, second = slice(None, early), slice(early, None)
    near = ((first, near1), (second, near2))
    other = ((first, other1), (second, other2))
    mine = ((slice(None), own),)

    def add(left, right):
        for rows, left_ref in left:
            for columns, right_ref in right:
                x[rows, columns] += nt(left_ref[...], right_ref[...])

    code = place[0] * 2 + place[1]
    for number, pair in enumerate(((near, other), (other, mine), (mine, other), (other, near))):

        @pl.when(code == number)
        def _(pair=pair):
            add(*pair)

    @at_end
    def _():
        out[...] = x[...].astype(out.dtype)


def cross_tile(place, own, near1, near2, other1, other2):
    early, half = near1.shape
    late = near2.shape[0]
    rows = early + late
    steps = half // DEPTH
    block1 = pl.BlockSpec((early, DEPTH), lambda k, place: (0, k))
    block2 = pl.BlockSpec((late, DEPTH), lambda k, place: (0, k))
    mine = pl.BlockSpec((rows, DEPTH), lambda k, place: (0, place[0] * steps + k))
    return pl.pallas_call(
        cross_kernel,
        grid_spec=pltpu.PrefetchScalarGridSpec(
            num_scalar_prefetch=1,
            grid=(steps,),
            in_specs=[mine] + [block1, block2] * 2,
            out_specs=pl.BlockSpec((rows, rows), lambda k, place: (0, 0)),
            scratch_shapes=[pltpu.VMEM((rows, rows), jnp.float32)],
        ),
        out_shape=jax.ShapeDtypeStruct((rows, rows), jnp.bfloat16),
        compiler_params=params(),
        cost_estimate=cost(2 * rows * rows * half, 6 * rows * half),
    )(place, own, near1, near2, other1, other2)


def halves_kernel(start, sides, place, own, *rest):
    outs, sems = rest[: len(sides)], rest[len(sides)]
    copies = []
    for number, (side, out) in enumerate(zip(sides, outs)):
        count, half = out.shape
        left = pl.multiple_of(((place[0] + side) % 2) * half, half)
        piece = count // PIECES
        for i in range(PIECES):
            copies.append(
                pltpu.make_async_copy(
                    own.at[pl.ds(start + i * piece, piece), pl.ds(left, half)],
                    out.at[pl.ds(i * piece, piece)],
                    sems.at[number * PIECES + i],
                )
            )
    for copy in copies:
        copy.start()
    for copy in copies:
        copy.wait()


def halves(place, own, start, count, sides):
    half = own.shape[1] // 2
    anywhere = pl.BlockSpec(memory_space=pltpu.HBM)
    return pl.pallas_call(
        functools.partial(halves_kernel, start, sides),
        in_specs=[pl.BlockSpec(memory_space=pltpu.SMEM), anywhere],
        out_specs=[anywhere] * len(sides),
        out_shape=[jax.ShapeDtypeStruct((count, half), own.dtype) for _ in sides],
        scratch_shapes=[pltpu.SemaphoreType.DMA((PIECES * len(sides),))],
        compiler_params=params(),
        cost_estimate=cost(0, 4 * count * half * len(sides)),
    )(place, own)


def finish(tile, row_mass, column_mass):
    @pl.when(pl.program_id(0) == 0)
    def _():
        column_mass[...] = jnp.zeros_like(column_mass)

    squared = tile * tile
    column_mass[...] += jnp.sum(squared, axis=0, keepdims=True)
    sums = jnp.sum(squared, axis=1, keepdims=True)
    size = sums.shape[0]
    row_mass[...] = jnp.broadcast_to(sums, (size, size)).T[0:1]


def second_kernel(
    scale, u1, u2r, u2c, v1, v2r, v2c, inverse, behind, gram, row_mass, column_mass
):
    step = pl.program_id(0)
    last = pl.num_programs(0) - 1
    early = u1.shape[1]

    def f32(ref):
        return ref[...].astype(jnp.float32)

    @pl.when(step < last)
    def _():
        gram[0, :, :early] = f32(u1) + f32(v1)
        gram[0, :, early:] = f32(u2c) + f32(v2c)

    @pl.when(step == last)
    def _():
        gram[0] = f32(u2r) + f32(v2r)

    tile = gram[0] * inverse[...] * behind[...] * scale
    gram[0] = tile
    finish(tile, row_mass, column_mass)


def mass_shapes(rows, late):
    specs = [
        pl.BlockSpec((1, late), lambda j, *_: (0, j)),
        pl.BlockSpec((1, rows), lambda j, *_: (0, 0)),
    ]
    return specs, [jax.ShapeDtypeStruct((1, rows), jnp.float32)] * 2


def second_tiles(scale, u1, u2, v1, v2, inverse, behind):
    early = u1.shape[0]
    late = u2.shape[0]
    rows = early + late
    last = early // late - 1
    first = pl.BlockSpec((late, early), lambda j: (jnp.minimum(j, last), 0))
    bottom = pl.BlockSpec((late, rows), lambda j: (0, 0))
    side = pl.BlockSpec((late, late), lambda j: (0, rows // late + jnp.minimum(j, last)))
    mass_specs, mass_types = mass_shapes(rows, late)
    return pl.pallas_call(
        functools.partial(second_kernel, scale),
        grid=(rows // late,),
        in_specs=[first, bottom, side] * 2
        + [
            pl.BlockSpec((late, 1), lambda j: (j, 0)),
            pl.BlockSpec((1, rows), lambda j: (0, 0)),
        ],
        out_specs=[pl.BlockSpec((1, late, rows), lambda j: (1, j, 0))] + mass_specs,
        out_shape=[jax.ShapeDtypeStruct((2, rows, rows), jnp.float32)] + mass_types,
        compiler_params=params(),
        cost_estimate=cost(60000 * rows * rows, 160 * rows * rows),
    )(u1, u2, u2, v1, v2, v2, inverse[:, None], behind[None, :])


def first_kernel(
    scale, place, y, z, local, inverse, behind, gram_in, gram, row_mass, column_mass
):
    del gram_in
    summed = y[...].astype(jnp.float32) + z[...].astype(jnp.float32)
    tile = jnp.where(place[1] == 1, local[...], summed)
    tile = tile * inverse[...] * behind[...] * scale
    gram[0] = tile
    finish(tile, row_mass, column_mass)


def first_tiles(scale, place, y, z, local, inverse, behind, gram, late):
    rows = y.shape[0]
    block = pl.BlockSpec((late, rows), lambda j, place: (j, 0))
    mass_specs, mass_types = mass_shapes(rows, late)
    return pl.pallas_call(
        functools.partial(first_kernel, scale),
        grid_spec=pltpu.PrefetchScalarGridSpec(
            num_scalar_prefetch=1,
            grid=(rows // late,),
            in_specs=[block] * 3
            + [
                pl.BlockSpec((late, 1), lambda j, place: (j, 0)),
                pl.BlockSpec((1, rows), lambda j, place: (0, 0)),
                pl.BlockSpec(memory_space=pl.ANY),
            ],
            out_specs=[pl.BlockSpec((1, late, rows), lambda j, place: (0, j, 0))] + mass_specs,
        ),
        out_shape=[jax.ShapeDtypeStruct((2, rows, rows), jnp.float32)] + mass_types,
        input_output_aliases={6: 0},
        compiler_params=params(),
        cost_estimate=cost(8 * rows * rows, 12 * rows * rows),
    )(place, y, z, local, inverse[:, None], behind[None, :], gram)


def local(sketches, test_sketches, domain_map):
    rows, depth = sketches.shape
    size = lax.axis_size("blocks")
    index = lax.axis_index("blocks")
    half = depth // 2
    early = rows - LATE
    blocks = range(size)
    upper = (index // 2) % 2
    core = index % 2
    place = jnp.stack([upper, core]).astype(jnp.int32)

    across = [(i, i ^ 2) for i in blocks]
    along = [(i, (i + (4 if i & 2 else -4)) % size) for i in blocks]
    swap = [(i, i ^ 1) for i in blocks]

    even = send(sketches, swap)
    (out1,) = halves(place, sketches, 0, early, (1,))
    partner1 = send(out1, across)
    (side1,) = halves(place, after(sketches, out1), 0, early, (0,))
    near1 = send(side1, along)
    out2, side2 = halves(place, after(sketches, side1), early, LATE, (1, 0))
    partner2 = send(out2, across)
    near2 = send(side2, along)

    inverse = inverse_norm(sketches)
    scale = 1.0 / math.sqrt(depth)

    test_inverse = inverse_norm(test_sketches)
    similarity = (
        nt(sketches, test_sketches) * inverse[:, None] * test_inverse[None, :] * scale
    ).astype(jnp.bfloat16)
    members = (
        domain_map[:, None] == lax.iota(jnp.int32, DOM_DEV * size)[None, :]
    ).astype(jnp.bfloat16)
    sums = lax.dot_general(
        members, similarity, (((0,), (0,)), ((), ())), preferred_element_type=jnp.float32
    )
    inside = nt(sketches, even)


    def halve(value, bit, *waits):
        count = value.shape[0] // 2
        mine = (index // bit) % 2
        away = lax.dynamic_slice_in_dim(value, (1 - mine) * count, count)
        kept = lax.dynamic_slice_in_dim(value, mine * count, count)
        return kept, send(after(away, *waits), [(i, i ^ bit) for i in blocks])

    bits = [size >> (step + 1) for step in range(size.bit_length() - 1)]
    back_v = [(i, i) if i & 2 else (i, (i + 4) % size) for i in blocks]
    back_y = [(i, i ^ 3) for i in blocks if i & 1]
    back_z = [pair for pair in back_v if pair[0] % 2 == 0]
    partner1 = after(partner1, inside, sums)
    u1, v1 = early_tiles(place, sketches, partner1, near1)
    u1r, v1r = send(u1, across), send(v1, back_v)
    other1 = send(partner1, swap)
    behind1 = send(after(inverse, partner1), [(i, (i + 1) % size) for i in blocks])
    behind2 = send(after(inverse, partner1), [(i, (i + 2) % size) for i in blocks])
    partner2, near2, behind1, behind2, _ = lax.optimization_barrier(
        (partner2, near2, behind1, behind2, u1)
    )
    other2 = send(partner2, swap)
    for bit in bits[:-4]:
        kept, came = halve(sums, bit, partner2)
        sums = kept + came
    kept, came = halve(sums, bits[-4], partner2)
    u2, v2 = late_tiles(place, sketches, partner1, partner2, near1, near2)
    u2r, v2r = send(u2, across), send(v2, back_v)
    sums = kept + came
    other2, sums, _, _, _ = lax.optimization_barrier((other2, sums, u2, u1r, v1r))
    kept, came = halve(sums, bits[-3], u2)
    x = cross_tile(place, sketches, near1, near2, other1, other2)
    y, z = send(x, back_y), send(x, back_z)
    sums = kept + came

    gram, row_mass2, column_mass2 = second_tiles(scale, u1r, u2r, v1r, v2r, inverse, behind2)
    kept, came = halve(sums, bits[-2], row_mass2)
    y, sums = lax.optimization_barrier((y, kept + came))
    gram, row_mass1, column_mass1 = first_tiles(
        scale, place, y, z, inside, inverse, behind1, gram, LATE
    )
    kept, came = halve(sums, bits[-1], row_mass1)
    domain_scores = (kept + came) * (1.0 / math.sqrt(rows / DOM_DEV))
    mass = (
        row_mass1[0]
        + row_mass2[0]
        + send(column_mass1[0], [(i, (i - 1) % size) for i in blocks])
        + send(column_mass2[0], [(i, (i - 2) % size) for i in blocks])
    )
    redundancy = mass / float(2 * ROUNDS * rows)
    return (gram, redundancy, domain_scores)


def solution(mesh):
    in_specs = (P(("groups", "blocks"), None), P(), P(("groups", "blocks")))
    out_specs = (
        P(None, ("groups", "blocks"), None),
        P(("groups", "blocks")),
        P(("groups", "blocks"), None),
    )
    return jax.shard_map(local, mesh=mesh, in_specs=in_specs, out_specs=out_specs, check_vma=False)
```

```python
import functools
import math

import jax
import jax.numpy as jnp
from jax import lax
from jax.experimental import pallas as pl
from jax.experimental.pallas import tpu as pltpu
from jax.sharding import PartitionSpec as P

ROUNDS = 2
DOM_DEV = 4
DEPTH = 1024
TALL = 256
PIECES = 4
NT = (((1,), (1,)), ((), ()))
VMEM_LIMIT = 40 * 2**20


def send(value, pairs):
    return lax.ppermute(value, "blocks", pairs)


def after(value, *others):
    return lax.optimization_barrier((value, *others))[0]


def inverse_norm(matrix):
    values = matrix.astype(jnp.float32)
    return lax.rsqrt(jnp.mean(values * values, axis=1) + 1e-06)


def nt(left, right):
    return lax.dot_general(left, right, NT, preferred_element_type=jnp.float32)


def params():
    return pltpu.CompilerParams(vmem_limit_bytes=VMEM_LIMIT)


def cost(flops, bytes_accessed):
    return pl.CostEstimate(flops=flops, bytes_accessed=bytes_accessed, transcendentals=0)


def clear(*totals):
    @pl.when(pl.program_id(0) == 0)
    def _():
        for total in totals:
            total[...] = jnp.zeros_like(total)


def halves_kernel(start, sides, place, own, *rest):
    count = len(sides)
    outs, (buffer, reads, writes) = rest[:count], rest[count:]
    rows, width = outs[0].shape
    half = own.shape[1] // 2
    piece = rows // PIECES
    inward, outward = [], []
    for number, (side, out) in enumerate(zip(sides, outs)):
        left = pl.multiple_of(((place[0] + side) % 2) * half + start, 128)
        for i in range(PIECES):
            part = pl.ds(i * piece, piece)
            slot = number * PIECES + i
            held = buffer.at[number, part]
            inward.append(
                pltpu.make_async_copy(own.at[part, pl.ds(left, width)], held, reads.at[slot])
            )
            outward.append(pltpu.make_async_copy(held, out.at[part], writes.at[slot]))
    for copy in inward:
        copy.start()
    for arrived, copy in zip(inward, outward):
        arrived.wait()
        copy.start()
    for copy in outward:
        copy.wait()


def halves(place, own, start, width, sides):
    rows = own.shape[0]
    slots = PIECES * len(sides)
    anywhere = pl.BlockSpec(memory_space=pltpu.HBM)
    return pl.pallas_call(
        functools.partial(halves_kernel, start, sides),
        in_specs=[pl.BlockSpec(memory_space=pltpu.SMEM), anywhere],
        out_specs=[anywhere] * len(sides),
        out_shape=[jax.ShapeDtypeStruct((rows, width), own.dtype) for _ in sides],
        scratch_shapes=[
            pltpu.VMEM((len(sides), rows, width), own.dtype),
            pltpu.SemaphoreType.DMA((slots,)),
            pltpu.SemaphoreType.DMA((slots,)),
        ],
        compiler_params=params(),
        cost_estimate=cost(0, 4 * rows * width * len(sides)),
    )(place, own)


def early_kernel(place, own, partner, near, u, v):
    clear(u, v)

    @pl.when(place[0] == 0)
    def _():
        u[...] += nt(partner[...], own[...])
        v[...] += nt(near[...], partner[...])

    @pl.when(place[0] == 1)
    def _():
        u[...] += nt(partner[...], near[...])
        v[...] += nt(own[...], partner[...])


def early_tiles(place, own, partner, near):
    rows, width = partner.shape
    half = own.shape[1] // 2
    block = pl.BlockSpec((rows, DEPTH), lambda k, place: (0, k))
    mine = pl.BlockSpec((rows, DEPTH), lambda k, place: (0, place[0] * (half // DEPTH) + k))
    whole = pl.BlockSpec((rows, rows), lambda k, place: (0, 0))
    return pl.pallas_call(
        early_kernel,
        grid_spec=pltpu.PrefetchScalarGridSpec(
            num_scalar_prefetch=1,
            grid=(width // DEPTH,),
            in_specs=[mine, block, block],
            out_specs=[whole] * 2,
        ),
        out_shape=[jax.ShapeDtypeStruct((rows, rows), jnp.float32)] * 2,
        compiler_params=params(),
        cost_estimate=cost(rows, rows),
    )(place, own, partner, near)


def late_kernel(place, own, partner, near, u, v, u_out, v_out):
    rows = pl.ds(pl.program_id(0) * TALL, TALL)

    @pl.when(place[0] == 0)
    def _():
        u_out[...] = (u[...] + nt(partner[rows, :], own[...])).astype(u_out.dtype)
        v_out[...] = (v[...] + nt(near[rows, :], partner[...])).astype(v_out.dtype)

    @pl.when(place[0] == 1)
    def _():
        u_out[...] = (u[...] + nt(partner[rows, :], near[...])).astype(u_out.dtype)
        v_out[...] = (v[...] + nt(own[rows, :], partner[...])).astype(v_out.dtype)


def late_tiles(place, own, partner, near, u, v):
    rows, width = partner.shape
    half = own.shape[1] // 2
    block = pl.BlockSpec((rows, width), lambda j, place: (0, 0))
    mine = pl.BlockSpec((rows, width), lambda j, place: (0, (place[0] + 1) * (half // width) - 1))
    part = pl.BlockSpec((TALL, rows), lambda j, place: (j, 0))
    return pl.pallas_call(
        late_kernel,
        grid_spec=pltpu.PrefetchScalarGridSpec(
            num_scalar_prefetch=1,
            grid=(rows // TALL,),
            in_specs=[mine, block, block, part, part],
            out_specs=[part] * 2,
        ),
        out_shape=[jax.ShapeDtypeStruct((rows, rows), jnp.bfloat16)] * 2,
        compiler_params=params(),
        cost_estimate=cost(60000 * rows * rows, 160 * rows * rows),
    )(place, own, partner, near, u, v)


def cross_kernel(place, own, near1, near2, other1, other2, out, x):
    clear(x)
    step = pl.program_id(0)
    last = pl.num_programs(0) - 1
    code = place[0] * 2 + place[1]

    def add(near, other):
        pairs = ((near, other), (other, own), (own, other), (other, near))
        for number, (left, right) in enumerate(pairs):

            @pl.when(code == number)
            def _(left=left, right=right):
                x[...] += nt(left[...], right[...])

    pl.when(step < last)(functools.partial(add, near1, other1))
    pl.when(step == last)(functools.partial(add, near2, other2))

    @pl.when(step == last)
    def _():
        out[...] = x[...].astype(out.dtype)


def cross_tile(place, own, near1, near2, other1, other2):
    rows, width = near1.shape
    steps = own.shape[1] // 2 // DEPTH
    block1 = pl.BlockSpec((rows, DEPTH), lambda k, place: (0, jnp.minimum(k, steps - 2)))
    block2 = pl.BlockSpec((rows, DEPTH), lambda k, place: (0, 0))
    mine = pl.BlockSpec((rows, DEPTH), lambda k, place: (0, place[0] * steps + k))
    return pl.pallas_call(
        cross_kernel,
        grid_spec=pltpu.PrefetchScalarGridSpec(
            num_scalar_prefetch=1,
            grid=(steps,),
            in_specs=[mine] + [block1, block2] * 2,
            out_specs=pl.BlockSpec((rows, rows), lambda k, place: (0, 0)),
            scratch_shapes=[pltpu.VMEM((rows, rows), jnp.float32)],
        ),
        out_shape=jax.ShapeDtypeStruct((rows, rows), jnp.bfloat16),
        compiler_params=params(),
        cost_estimate=cost(2 * rows * rows * width, 6 * rows * width),
    )(place, own, near1, near2, other1, other2)


def finish(tile, gram, row_mass, column_mass):
    @pl.when(pl.program_id(0) == 0)
    def _():
        column_mass[...] = jnp.zeros_like(column_mass)

    gram[0] = tile
    squared = tile * tile
    column_mass[...] += jnp.sum(squared, axis=0, keepdims=True)
    sums = jnp.sum(squared, axis=1, keepdims=True)
    size = sums.shape[0]
    row_mass[...] = jnp.broadcast_to(sums, (size, size)).T[0:1]


def second_kernel(scale, u, v, inverse, behind, gram, row_mass, column_mass):
    tile = u[...].astype(jnp.float32) + v[...].astype(jnp.float32)
    finish(tile * inverse[...] * behind[...] * scale, gram, row_mass, column_mass)


def first_kernel(
    scale, place, y, z, local, inverse, behind, gram_in, gram, row_mass, column_mass
):
    del gram_in
    tile = y[...].astype(jnp.float32) + z[...].astype(jnp.float32)
    tile = jnp.where(place[1] == 1, local[...], tile)
    finish(tile * inverse[...] * behind[...] * scale, gram, row_mass, column_mass)


def mass_shapes(rows):
    specs = [
        pl.BlockSpec((1, TALL), lambda j, *_: (0, j)),
        pl.BlockSpec((1, rows), lambda j, *_: (0, 0)),
    ]
    return specs, [jax.ShapeDtypeStruct((1, rows), jnp.float32)] * 2


def second_tiles(scale, u, v, inverse, behind):
    rows = u.shape[0]
    block = pl.BlockSpec((TALL, rows), lambda j: (j, 0))
    mass_specs, mass_types = mass_shapes(rows)
    return pl.pallas_call(
        functools.partial(second_kernel, scale),
        grid=(rows // TALL,),
        in_specs=[
            block,
            block,
            pl.BlockSpec((TALL, 1), lambda j: (j, 0)),
            pl.BlockSpec((1, rows), lambda j: (0, 0)),
        ],
        out_specs=[pl.BlockSpec((1, TALL, rows), lambda j: (1, j, 0))] + mass_specs,
        out_shape=[jax.ShapeDtypeStruct((2, rows, rows), jnp.float32)] + mass_types,
        compiler_params=params(),
        cost_estimate=cost(60000 * rows * rows, 160 * rows * rows),
    )(u, v, inverse[:, None], behind[None, :])


def first_tiles(scale, place, y, z, local, inverse, behind, gram):
    rows = y.shape[0]
    block = pl.BlockSpec((TALL, rows), lambda j, place: (j, 0))
    mass_specs, mass_types = mass_shapes(rows)
    return pl.pallas_call(
        functools.partial(first_kernel, scale),
        grid_spec=pltpu.PrefetchScalarGridSpec(
            num_scalar_prefetch=1,
            grid=(rows // TALL,),
            in_specs=[block] * 3
            + [
                pl.BlockSpec((TALL, 1), lambda j, place: (j, 0)),
                pl.BlockSpec((1, rows), lambda j, place: (0, 0)),
                pl.BlockSpec(memory_space=pl.ANY),
            ],
            out_specs=[pl.BlockSpec((1, TALL, rows), lambda j, place: (0, j, 0))] + mass_specs,
        ),
        out_shape=[jax.ShapeDtypeStruct((2, rows, rows), jnp.float32)] + mass_types,
        input_output_aliases={6: 0},
        compiler_params=params(),
        cost_estimate=cost(8 * rows * rows, 12 * rows * rows),
    )(place, y, z, local, inverse[:, None], behind[None, :], gram)


def local(sketches, test_sketches, domain_map):
    rows, depth = sketches.shape
    size = lax.axis_size("blocks")
    index = lax.axis_index("blocks")
    half = depth // 2
    first = half - DEPTH
    blocks = range(size)
    upper = (index // 2) % 2
    core = index % 2
    place = jnp.stack([upper, core]).astype(jnp.int32)

    across = [(i, i ^ 2) for i in blocks]
    along = [(i, (i + (4 if i & 2 else -4)) % size) for i in blocks]
    swap = [(i, i ^ 1) for i in blocks]

    even = send(sketches, swap)
    (out1,) = halves(place, sketches, 0, first, (1,))
    partner1 = send(out1, across)
    (side1,) = halves(place, after(sketches, out1), 0, first, (0,))
    near1 = send(side1, along)
    out2, side2 = halves(place, after(sketches, side1), first, DEPTH, (1, 0))
    partner2 = send(out2, across)
    near2 = send(side2, along)

    inverse = inverse_norm(sketches)
    scale = 1.0 / math.sqrt(depth)

    test_inverse = inverse_norm(test_sketches)
    similarity = (
        nt(sketches, test_sketches) * inverse[:, None] * test_inverse[None, :] * scale
    ).astype(jnp.bfloat16)
    members = (
        domain_map[:, None] == lax.iota(jnp.int32, DOM_DEV * size)[None, :]
    ).astype(jnp.bfloat16)
    sums = lax.dot_general(
        members, similarity, (((0,), (0,)), ((), ())), preferred_element_type=jnp.float32
    )
    inside = nt(sketches, even)


    def halve(value, bit, *waits):
        count = value.shape[0] // 2
        mine = (index // bit) % 2
        away = lax.dynamic_slice_in_dim(value, (1 - mine) * count, count)
        kept = lax.dynamic_slice_in_dim(value, mine * count, count)
        return kept, send(after(away, *waits), [(i, i ^ bit) for i in blocks])

    bits = [size >> (step + 1) for step in range(size.bit_length() - 1)]
    back_v = [(i, i) if i & 2 else (i, (i + 4) % size) for i in blocks]
    back_y = [(i, i ^ 3) for i in blocks if i & 1]
    back_z = [pair for pair in back_v if pair[0] % 2 == 0]
    partner1 = after(partner1, inside, sums)
    u, v = early_tiles(place, sketches, partner1, near1)
    other1 = send(partner1, swap)
    partner2, near2, u, v = lax.optimization_barrier((partner2, near2, u, v))
    behind1 = send(after(inverse, partner2), [(i, (i + 1) % size) for i in blocks])
    behind2 = send(after(inverse, partner2), [(i, (i + 2) % size) for i in blocks])
    other2 = send(partner2, swap)
    for bit in bits[:-4]:
        kept, came = halve(sums, bit, partner2)
        sums = kept + came
    kept, came = halve(sums, bits[-4], partner2)
    u, v = late_tiles(place, sketches, partner2, near2, u, v)
    u, v, sums, behind1, behind2 = lax.optimization_barrier((u, v, kept + came, behind1, behind2))
    ur, vr = send(u, across), send(v, back_v)
    kept, came = halve(sums, bits[-3], u)
    x = cross_tile(place, sketches, near1, near2, after(other1, u), after(other2, u))
    y, z = send(x, back_y), send(x, back_z)

    gram, row_mass2, column_mass2 = second_tiles(scale, ur, vr, inverse, behind2)
    kept, came = halve(kept + after(came, row_mass2), bits[-2])
    kept, came = halve(kept + came, bits[-1])
    y, domain_sums = lax.optimization_barrier((y, kept + came))
    domain_scores = domain_sums * (1.0 / math.sqrt(rows / DOM_DEV))
    gram, row_mass1, column_mass1 = first_tiles(
        scale, place, y, z, inside, inverse, behind1, gram
    )
    mass = (
        row_mass1[0]
        + row_mass2[0]
        + send(column_mass1[0], [(i, (i - 1) % size) for i in blocks])
        + send(column_mass2[0], [(i, (i - 2) % size) for i in blocks])
    )
    redundancy = mass / float(2 * ROUNDS * rows)
    return (gram, redundancy, domain_scores)


def solution(mesh):
    in_specs = (P(("groups", "blocks"), None), P(), P(("groups", "blocks")))
    out_specs = (
        P(None, ("groups", "blocks"), None),
        P(("groups", "blocks")),
        P(("groups", "blocks"), None),
    )
    return jax.shard_map(local, mesh=mesh, in_specs=in_specs, out_specs=out_specs, check_vma=False)
```

```python
import functools
import math

import jax
import jax.numpy as jnp
from jax import lax
from jax.experimental import pallas as pl
from jax.experimental.pallas import tpu as pltpu
from jax.sharding import PartitionSpec as P

ROUNDS = 2
DOM_DEV = 4
DEPTH = 1024
TALL = 128
BAND = 256
PIECES = 4
NT = (((1,), (1,)), ((), ()))
VMEM_LIMIT = 36 * 2**20


def send(value, pairs):
    return lax.ppermute(value, "blocks", pairs)


def after(value, *others):
    return lax.optimization_barrier((value, *others))[0]


def inverse_norm(matrix):
    values = matrix.astype(jnp.float32)
    return lax.rsqrt(jnp.mean(values * values, axis=1) + 1e-06)


def nt(left, right):
    return lax.dot_general(left, right, NT, preferred_element_type=jnp.float32)


def params():
    return pltpu.CompilerParams(vmem_limit_bytes=VMEM_LIMIT)


def cost(flops, bytes_accessed):
    return pl.CostEstimate(flops=flops, bytes_accessed=bytes_accessed, transcendentals=0)


def clear(*totals):
    @pl.when(pl.program_id(0) == 0)
    def _():
        for total in totals:
            total[...] = jnp.zeros_like(total)


def halves_kernel(start, sides, place, own, *rest):
    count = len(sides)
    outs, reads = rest[:count], rest[count]
    rows, width = outs[0].shape
    half = own.shape[1] // 2
    piece = rows // PIECES
    copies = []
    for number, (side, out) in enumerate(zip(sides, outs)):
        left = pl.multiple_of(((place[0] + side) % 2) * half + start, 128)
        for i in range(PIECES):
            part = pl.ds(i * piece, piece)
            copies.append(
                pltpu.make_async_copy(
                    own.at[part, pl.ds(left, width)],
                    out.at[part],
                    reads.at[number * PIECES + i],
                )
            )
    for copy in copies:
        copy.start()
    for copy in copies:
        copy.wait()


def halves(place, own, start, width, sides):
    rows = own.shape[0]
    return pl.pallas_call(
        functools.partial(halves_kernel, start, sides),
        in_specs=[pl.BlockSpec(memory_space=pltpu.SMEM), pl.BlockSpec(memory_space=pltpu.HBM)],
        out_specs=[pl.BlockSpec(memory_space=pltpu.VMEM)] * len(sides),
        out_shape=[pltpu.VMEM((rows, width), own.dtype) for _ in sides],
        scratch_shapes=[pltpu.SemaphoreType.DMA((PIECES * len(sides),))],
        compiler_params=params(),
        cost_estimate=cost(0, 2 * rows * width * len(sides)),
    )(place, own)


def early_kernel(place, own, partner, near, u, v):
    clear(u, v)

    @pl.when(place[0] == 0)
    def _():
        u[...] += nt(partner[...], own[...])
        v[...] += nt(near[...], partner[...])

    @pl.when(place[0] == 1)
    def _():
        u[...] += nt(partner[...], near[...])
        v[...] += nt(own[...], partner[...])


def early_tiles(place, own, partner, near):
    rows, width = partner.shape
    half = own.shape[1] // 2
    block = pl.BlockSpec((rows, DEPTH), lambda k, place: (0, k))
    mine = pl.BlockSpec((rows, DEPTH), lambda k, place: (0, place[0] * (half // DEPTH) + k))
    whole = pl.BlockSpec((rows, rows), lambda k, place: (0, 0))
    return pl.pallas_call(
        early_kernel,
        grid_spec=pltpu.PrefetchScalarGridSpec(
            num_scalar_prefetch=1,
            grid=(width // DEPTH,),
            in_specs=[mine, block, block],
            out_specs=[whole] * 2,
        ),
        out_shape=[jax.ShapeDtypeStruct((rows, rows), jnp.float32)] * 2,
        compiler_params=params(),
        cost_estimate=cost(rows, rows),
    )(place, own, partner, near)


def late_kernel(place, mine, partner, near, u, v, u_out, v_out):
    def add(s, w):
        for start in range(0, u.shape[0], BAND):
            rows = pl.ds(start, BAND)
            u_out[rows, :] = (u[rows, :] + nt(partner[rows, :], s[...])).astype(u_out.dtype)
            v_out[rows, :] = (v[rows, :] + nt(w[rows, :], partner[...])).astype(v_out.dtype)

    @pl.when(place[0] == 0)
    def _():
        add(mine, near)

    @pl.when(place[0] == 1)
    def _():
        add(near, mine)


def late_tiles(place, mine, partner, near, u, v):
    rows, width = partner.shape
    return pl.pallas_call(
        late_kernel,
        in_specs=[pl.BlockSpec(memory_space=pltpu.SMEM)]
        + [pl.BlockSpec(memory_space=pltpu.VMEM)] * 5,
        out_specs=[pl.BlockSpec(memory_space=pltpu.VMEM)] * 2,
        out_shape=[pltpu.VMEM((rows, rows), jnp.bfloat16)] * 2,
        compiler_params=params(),
        cost_estimate=cost(60000 * rows * rows, 160 * rows * rows),
    )(place, mine, partner, near, u, v)


def cross_kernel(place, own, near1, near2, other1, other2, out, x):
    clear(x)
    step = pl.program_id(0)
    last = pl.num_programs(0) - 1
    code = place[0] * 2 + place[1]

    def add(near, other):
        pairs = ((near, other), (other, own), (own, other), (other, near))
        for number, (left, right) in enumerate(pairs):

            @pl.when(code == number)
            def _(left=left, right=right):
                x[...] += nt(left[...], right[...])

    pl.when(step < last)(functools.partial(add, near1, other1))
    pl.when(step == last)(functools.partial(add, near2, other2))

    @pl.when(step == last)
    def _():
        out[...] = x[...].astype(out.dtype)


def cross_tile(place, own, near1, near2, other1, other2):
    rows, width = near1.shape
    steps = own.shape[1] // 2 // DEPTH
    block1 = pl.BlockSpec((rows, DEPTH), lambda k, place: (0, jnp.minimum(k, steps - 2)))
    block2 = pl.BlockSpec((rows, DEPTH), lambda k, place: (0, 0))
    mine = pl.BlockSpec((rows, DEPTH), lambda k, place: (0, place[0] * steps + k))
    return pl.pallas_call(
        cross_kernel,
        grid_spec=pltpu.PrefetchScalarGridSpec(
            num_scalar_prefetch=1,
            grid=(steps,),
            in_specs=[mine] + [block1, block2] * 2,
            out_specs=pl.BlockSpec((rows, rows), lambda k, place: (0, 0)),
            scratch_shapes=[pltpu.VMEM((rows, rows), jnp.float32)],
        ),
        out_shape=jax.ShapeDtypeStruct((rows, rows), jnp.bfloat16),
        compiler_params=params(),
        cost_estimate=cost(2 * rows * rows * width, 6 * rows * width),
    )(place, own, near1, near2, other1, other2)


def finish(tile, gram, row_mass, column_mass):
    @pl.when(pl.program_id(0) == 0)
    def _():
        column_mass[...] = jnp.zeros_like(column_mass)

    gram[0] = tile
    squared = tile * tile
    column_mass[...] += jnp.sum(squared, axis=0, keepdims=True)
    sums = jnp.sum(squared, axis=1, keepdims=True)
    size = sums.shape[0]
    row_mass[...] = jnp.broadcast_to(sums, (size, size)).T[0:1]


def second_kernel(scale, u, v, inverse, behind, gram, row_mass, column_mass):
    tile = u[...].astype(jnp.float32) + v[...].astype(jnp.float32)
    finish(tile * inverse[...] * behind[...] * scale, gram, row_mass, column_mass)


def first_kernel(
    scale, place, y, z, local, inverse, behind, gram_in, gram, row_mass, column_mass
):
    del gram_in
    tile = y[...].astype(jnp.float32) + z[...].astype(jnp.float32)
    tile = jnp.where(place[1] == 1, local[...], tile)
    finish(tile * inverse[...] * behind[...] * scale, gram, row_mass, column_mass)


def mass_shapes(rows):
    specs = [
        pl.BlockSpec((1, TALL), lambda j, *_: (0, j)),
        pl.BlockSpec((1, rows), lambda j, *_: (0, 0)),
    ]
    return specs, [jax.ShapeDtypeStruct((1, rows), jnp.float32)] * 2


def second_tiles(scale, u, v, inverse, behind):
    rows = u.shape[0]
    block = pl.BlockSpec((TALL, rows), lambda j: (j, 0))
    mass_specs, mass_types = mass_shapes(rows)
    return pl.pallas_call(
        functools.partial(second_kernel, scale),
        grid=(rows // TALL,),
        in_specs=[
            block,
            block,
            pl.BlockSpec((TALL, 1), lambda j: (j, 0)),
            pl.BlockSpec((1, rows), lambda j: (0, 0)),
        ],
        out_specs=[pl.BlockSpec((1, TALL, rows), lambda j: (1, j, 0))] + mass_specs,
        out_shape=[jax.ShapeDtypeStruct((2, rows, rows), jnp.float32)] + mass_types,
        compiler_params=params(),
        cost_estimate=cost(60000 * rows * rows, 160 * rows * rows),
    )(u, v, inverse[:, None], behind[None, :])


def first_tiles(scale, place, y, z, local, inverse, behind, gram):
    rows = y.shape[0]
    block = pl.BlockSpec((TALL, rows), lambda j, place: (j, 0))
    mass_specs, mass_types = mass_shapes(rows)
    return pl.pallas_call(
        functools.partial(first_kernel, scale),
        grid_spec=pltpu.PrefetchScalarGridSpec(
            num_scalar_prefetch=1,
            grid=(rows // TALL,),
            in_specs=[block] * 3
            + [
                pl.BlockSpec((TALL, 1), lambda j, place: (j, 0)),
                pl.BlockSpec((1, rows), lambda j, place: (0, 0)),
                pl.BlockSpec(memory_space=pl.ANY),
            ],
            out_specs=[pl.BlockSpec((1, TALL, rows), lambda j, place: (0, j, 0))] + mass_specs,
        ),
        out_shape=[jax.ShapeDtypeStruct((2, rows, rows), jnp.float32)] + mass_types,
        input_output_aliases={6: 0},
        compiler_params=params(),
        cost_estimate=cost(8 * rows * rows, 12 * rows * rows),
    )(place, y, z, local, inverse[:, None], behind[None, :], gram)


def local(sketches, test_sketches, domain_map):
    rows, depth = sketches.shape
    size = lax.axis_size("blocks")
    index = lax.axis_index("blocks")
    half = depth // 2
    first = half - DEPTH
    blocks = range(size)
    upper = (index // 2) % 2
    core = index % 2
    place = jnp.stack([upper, core]).astype(jnp.int32)

    across = [(i, i ^ 2) for i in blocks]
    along = [(i, (i + (4 if i & 2 else -4)) % size) for i in blocks]
    swap = [(i, i ^ 1) for i in blocks]

    even = send(sketches, swap)
    (out1,) = halves(place, sketches, 0, first, (1,))
    partner1 = send(out1, across)
    (side1,) = halves(place, after(sketches, out1), 0, first, (0,))
    near1 = send(side1, along)
    out2, side2 = halves(place, after(sketches, side1), first, DEPTH, (1, 0))
    partner2 = send(out2, across)
    near2 = send(side2, along)

    inverse = inverse_norm(sketches)
    scale = 1.0 / math.sqrt(depth)

    test_inverse = inverse_norm(test_sketches)
    similarity = (
        nt(sketches, test_sketches) * inverse[:, None] * test_inverse[None, :] * scale
    ).astype(jnp.bfloat16)
    members = (
        domain_map[:, None] == lax.iota(jnp.int32, DOM_DEV * size)[None, :]
    ).astype(jnp.bfloat16)
    sums = lax.dot_general(
        members, similarity, (((0,), (0,)), ((), ())), preferred_element_type=jnp.float32
    )
    inside = nt(sketches, even)


    def halve(value, bit, *waits):
        count = value.shape[0] // 2
        mine = (index // bit) % 2
        away = lax.dynamic_slice_in_dim(value, (1 - mine) * count, count)
        kept = lax.dynamic_slice_in_dim(value, mine * count, count)
        return kept, send(after(away, *waits), [(i, i ^ bit) for i in blocks])

    bits = [size >> (step + 1) for step in range(size.bit_length() - 1)]
    back_v = [(i, i) if i & 2 else (i, (i + 4) % size) for i in blocks]
    back_y = [(i, i ^ 3) for i in blocks if i & 1]
    back_z = [pair for pair in back_v if pair[0] % 2 == 0]
    partner1 = after(partner1, inside, sums)
    u, v = early_tiles(place, sketches, partner1, near1)
    other1 = send(partner1, swap)
    behind1 = send(after(inverse, partner1), [(i, (i + 1) % size) for i in blocks])
    behind2 = send(after(inverse, partner1), [(i, (i + 2) % size) for i in blocks])
    for bit in bits[:-4]:
        kept, came = halve(sums, bit, partner1)
        sums = kept + came
    kept, came = halve(sums, bits[-4], u)
    partner2, near2, u, v, behind1, behind2, came = lax.optimization_barrier(
        (partner2, near2, u, v, behind1, behind2, came)
    )
    other2 = send(partner2, swap)
    u, v = late_tiles(place, side2, partner2, near2, u, v)
    ur, vr = send(u, across), send(v, back_v)
    kept, came = halve(kept + came, bits[-3], u)
    x = cross_tile(place, sketches, near1, near2, after(other1, u), after(other2, u))
    y, z = send(x, back_y), send(x, back_z)

    gram, row_mass2, column_mass2 = second_tiles(scale, ur, vr, inverse, behind2)
    kept, came = halve(kept + after(came, row_mass2), bits[-2])
    y, sums = lax.optimization_barrier((y, kept + came))
    gram, row_mass1, column_mass1 = first_tiles(
        scale, place, y, z, inside, inverse, behind1, gram
    )
    kept, came = halve(sums, bits[-1], row_mass1)
    domain_scores = (kept + came) * (1.0 / math.sqrt(rows / DOM_DEV))
    mass = (
        row_mass1[0]
        + row_mass2[0]
        + send(column_mass1[0], [(i, (i - 1) % size) for i in blocks])
        + send(after(column_mass2[0], row_mass1), [(i, (i - 2) % size) for i in blocks])
    )
    redundancy = mass / float(2 * ROUNDS * rows)
    return (gram, redundancy, domain_scores)


def solution(mesh):
    in_specs = (P(("groups", "blocks"), None), P(), P(("groups", "blocks")))
    out_specs = (
        P(None, ("groups", "blocks"), None),
        P(("groups", "blocks")),
        P(("groups", "blocks"), None),
    )
    return jax.shard_map(local, mesh=mesh, in_specs=in_specs, out_specs=out_specs, check_vma=False)
```

```python
import functools
import math

import jax
import jax.numpy as jnp
from jax import lax
from jax.experimental import pallas as pl
from jax.experimental.pallas import tpu as pltpu
from jax.sharding import PartitionSpec as P

ROUNDS = 2
DOM_DEV = 4
DEPTH = 1024
TALL = 384
BAND = 256
PIECES = 4
NT = (((1,), (1,)), ((), ()))
VMEM_LIMIT = 40 * 2**20


def send(value, pairs):
    return lax.ppermute(value, "blocks", pairs)


def after(value, *others):
    return lax.optimization_barrier((value, *others))[0]


def inverse_norm(matrix):
    values = matrix.astype(jnp.float32)
    return lax.rsqrt(jnp.mean(values * values, axis=1) + 1e-06)


def nt(left, right):
    return lax.dot_general(left, right, NT, preferred_element_type=jnp.float32)


def params():
    return pltpu.CompilerParams(vmem_limit_bytes=VMEM_LIMIT)


def cost(flops, bytes_accessed):
    return pl.CostEstimate(flops=flops, bytes_accessed=bytes_accessed, transcendentals=0)


def clear(*totals):
    @pl.when(pl.program_id(0) == 0)
    def _():
        for total in totals:
            total[...] = jnp.zeros_like(total)


def halves_kernel(start, sides, place, own, *rest):
    count = len(sides)
    outs, (buffer, reads, writes) = rest[:count], rest[count:]
    rows, width = outs[0].shape
    half = own.shape[1] // 2
    piece = rows // PIECES
    inward, outward = [], []
    for number, (side, out) in enumerate(zip(sides, outs)):
        left = pl.multiple_of(((place[0] + side) % 2) * half + start, 128)
        for i in range(PIECES):
            part = pl.ds(i * piece, piece)
            slot = number * PIECES + i
            held = buffer.at[number, part]
            inward.append(
                pltpu.make_async_copy(own.at[part, pl.ds(left, width)], held, reads.at[slot])
            )
            outward.append(pltpu.make_async_copy(held, out.at[part], writes.at[slot]))
    for copy in inward:
        copy.start()
    for arrived, copy in zip(inward, outward):
        arrived.wait()
        copy.start()
    for copy in outward:
        copy.wait()


def halves(place, own, start, width, sides):
    rows = own.shape[0]
    slots = PIECES * len(sides)
    anywhere = pl.BlockSpec(memory_space=pltpu.HBM)
    return pl.pallas_call(
        functools.partial(halves_kernel, start, sides),
        in_specs=[pl.BlockSpec(memory_space=pltpu.SMEM), anywhere],
        out_specs=[anywhere] * len(sides),
        out_shape=[jax.ShapeDtypeStruct((rows, width), own.dtype) for _ in sides],
        scratch_shapes=[
            pltpu.VMEM((len(sides), rows, width), own.dtype),
            pltpu.SemaphoreType.DMA((slots,)),
            pltpu.SemaphoreType.DMA((slots,)),
        ],
        compiler_params=params(),
        cost_estimate=cost(0, 4 * rows * width * len(sides)),
    )(place, own)


def early_kernel(place, own, partner, near, u, v):
    clear(u, v)

    @pl.when(place[0] == 0)
    def _():
        u[...] += nt(partner[...], own[...])
        v[...] += nt(near[...], partner[...])

    @pl.when(place[0] == 1)
    def _():
        u[...] += nt(partner[...], near[...])
        v[...] += nt(own[...], partner[...])


def early_tiles(place, own, partner, near):
    rows, width = partner.shape
    half = own.shape[1] // 2
    block = pl.BlockSpec((rows, DEPTH), lambda k, place: (0, k))
    mine = pl.BlockSpec((rows, DEPTH), lambda k, place: (0, place[0] * (half // DEPTH) + k))
    whole = pl.BlockSpec((rows, rows), lambda k, place: (0, 0))
    return pl.pallas_call(
        early_kernel,
        grid_spec=pltpu.PrefetchScalarGridSpec(
            num_scalar_prefetch=1,
            grid=(width // DEPTH,),
            in_specs=[mine, block, block],
            out_specs=[whole] * 2,
        ),
        out_shape=[jax.ShapeDtypeStruct((rows, rows), jnp.float32)] * 2,
        compiler_params=params(),
        cost_estimate=cost(rows, rows),
    )(place, own, partner, near)


def late_kernel(place, mine, partner, near, u, v, u_out, v_out):
    def add(s, w):
        for start in range(0, u.shape[0], BAND):
            rows = pl.ds(start, BAND)
            u_out[rows, :] = (u[rows, :] + nt(partner[rows, :], s[...])).astype(u_out.dtype)
            v_out[rows, :] = (v[rows, :] + nt(w[rows, :], partner[...])).astype(v_out.dtype)

    @pl.when(place[0] == 0)
    def _():
        add(mine, near)

    @pl.when(place[0] == 1)
    def _():
        add(near, mine)


def late_tiles(place, mine, partner, near, u, v):
    rows, width = partner.shape
    return pl.pallas_call(
        late_kernel,
        in_specs=[pl.BlockSpec(memory_space=pltpu.SMEM)]
        + [pl.BlockSpec(memory_space=pltpu.VMEM)] * 5,
        out_specs=[pl.BlockSpec(memory_space=pltpu.VMEM)] * 2,
        out_shape=[pltpu.VMEM((rows, rows), jnp.bfloat16)] * 2,
        compiler_params=params(),
        cost_estimate=cost(60000 * rows * rows, 160 * rows * rows),
    )(place, mine, partner, near, u, v)


def cross_kernel(place, own, near1, near2, other1, other2, out, x):
    clear(x)
    step = pl.program_id(0)
    last = pl.num_programs(0) - 1
    code = place[0] * 2 + place[1]

    def add(near, other):
        pairs = ((near, other), (other, own), (own, other), (other, near))
        for number, (left, right) in enumerate(pairs):

            @pl.when(code == number)
            def _(left=left, right=right):
                x[...] += nt(left[...], right[...])

    pl.when(step < last)(functools.partial(add, near1, other1))
    pl.when(step == last)(functools.partial(add, near2, other2))

    @pl.when(step == last)
    def _():
        out[...] = x[...].astype(out.dtype)


def cross_tile(place, own, near1, near2, other1, other2):
    rows, width = near1.shape
    steps = own.shape[1] // 2 // DEPTH
    block1 = pl.BlockSpec((rows, DEPTH), lambda k, place: (0, jnp.minimum(k, steps - 2)))
    block2 = pl.BlockSpec((rows, DEPTH), lambda k, place: (0, 0))
    mine = pl.BlockSpec((rows, DEPTH), lambda k, place: (0, place[0] * steps + k))
    return pl.pallas_call(
        cross_kernel,
        grid_spec=pltpu.PrefetchScalarGridSpec(
            num_scalar_prefetch=1,
            grid=(steps,),
            in_specs=[mine] + [block1, block2] * 2,
            out_specs=pl.BlockSpec((rows, rows), lambda k, place: (0, 0)),
            scratch_shapes=[pltpu.VMEM((rows, rows), jnp.float32)],
        ),
        out_shape=jax.ShapeDtypeStruct((rows, rows), jnp.bfloat16),
        compiler_params=params(),
        cost_estimate=cost(2 * rows * rows * width, 6 * rows * width),
    )(place, own, near1, near2, other1, other2)


def finish(tile, gram, row_mass, column_mass):
    @pl.when(pl.program_id(0) == 0)
    def _():
        column_mass[...] = jnp.zeros_like(column_mass)

    gram[0] = tile
    squared = tile * tile
    column_mass[...] += jnp.sum(squared, axis=0, keepdims=True)
    sums = jnp.sum(squared, axis=1, keepdims=True)
    size = sums.shape[0]
    row_mass[...] = jnp.broadcast_to(sums, (size, size)).T[0:1]


def second_kernel(scale, place, u, v, kept, inverse, behind, gram, row_mass, column_mass):
    other = jnp.where(place[0] == 1, kept[...], v[...])
    tile = u[...].astype(jnp.float32) + other.astype(jnp.float32)
    finish(tile * inverse[...] * behind[...] * scale, gram, row_mass, column_mass)


def first_kernel(
    scale, place, y, z, kept, local, inverse, behind, gram_in, gram, row_mass, column_mass
):
    del gram_in
    other = jnp.where(place[0] == 1, kept[...], z[...])
    tile = y[...].astype(jnp.float32) + other.astype(jnp.float32)
    tile = jnp.where(place[1] == 1, local[...], tile)
    finish(tile * inverse[...] * behind[...] * scale, gram, row_mass, column_mass)


def mass_shapes(rows):
    specs = [
        pl.BlockSpec((1, TALL), lambda j, *_: (0, j)),
        pl.BlockSpec((1, rows), lambda j, *_: (0, 0)),
    ]
    return specs, [jax.ShapeDtypeStruct((1, rows), jnp.float32)] * 2


def join(kernel, index, scale, place, tiles, inverse, behind, gram=()):
    rows = tiles[0].shape[0]
    mass_specs, mass_types = mass_shapes(rows)
    return pl.pallas_call(
        functools.partial(kernel, scale),
        grid_spec=pltpu.PrefetchScalarGridSpec(
            num_scalar_prefetch=1,
            grid=(rows // TALL,),
            in_specs=[pl.BlockSpec((TALL, rows), lambda j, place: (j, 0))] * len(tiles)
            + [
                pl.BlockSpec((TALL, 1), lambda j, place: (j, 0)),
                pl.BlockSpec((1, rows), lambda j, place: (0, 0)),
            ]
            + [pl.BlockSpec(memory_space=pl.ANY)] * len(gram),
            out_specs=[pl.BlockSpec((1, TALL, rows), lambda j, place: (index, j, 0))] + mass_specs,
        ),
        out_shape=[jax.ShapeDtypeStruct((2, rows, rows), jnp.float32)] + mass_types,
        input_output_aliases={len(tiles) + 3: 0} if gram else {},
        compiler_params=params(),
        cost_estimate=cost(60000 * rows * rows, 160 * rows * rows)
        if index
        else cost(8 * rows * rows, 12 * rows * rows),
    )(place, *tiles, inverse[:, None], behind[None, :], *gram)


def local(sketches, test_sketches, domain_map):
    rows, depth = sketches.shape
    size = lax.axis_size("blocks")
    index = lax.axis_index("blocks")
    half = depth // 2
    first = half - DEPTH
    blocks = range(size)
    upper = (index // 2) % 2
    core = index % 2
    place = jnp.stack([upper, core]).astype(jnp.int32)

    across = [(i, i ^ 2) for i in blocks]
    along = [(i, (i + (4 if i & 2 else -4)) % size) for i in blocks]
    swap = [(i, i ^ 1) for i in blocks]

    even = send(sketches, swap)
    out1, side1 = halves(place, sketches, 0, first, (1, 0))
    partner1 = send(out1, across)
    near1 = send(side1, along)
    out2, side2 = halves(place, after(sketches, side1), first, DEPTH, (1, 0))
    partner2 = send(out2, across)
    near2 = send(side2, along)

    inverse = inverse_norm(sketches)
    scale = 1.0 / math.sqrt(depth)

    test_inverse = inverse_norm(test_sketches)
    similarity = (
        nt(sketches, test_sketches) * inverse[:, None] * test_inverse[None, :] * scale
    ).astype(jnp.bfloat16)
    members = (
        domain_map[:, None] == lax.iota(jnp.int32, DOM_DEV * size)[None, :]
    ).astype(jnp.bfloat16)
    sums = lax.dot_general(
        members, similarity, (((0,), (0,)), ((), ())), preferred_element_type=jnp.float32
    )
    inside = nt(sketches, even)

    def halve(value, bit, *waits):
        count = value.shape[0] // 2
        mine = (index // bit) % 2
        away = lax.dynamic_slice_in_dim(value, (1 - mine) * count, count)
        kept = lax.dynamic_slice_in_dim(value, mine * count, count)
        return kept, send(after(away, *waits), [(i, i ^ bit) for i in blocks])

    bits = [size >> (step + 1) for step in range(size.bit_length() - 1)]
    back_v = [(i, (i + 4) % size) for i in blocks if not i & 2]
    back_y = [(i, i ^ 3) for i in blocks if i & 1]
    back_z = [pair for pair in back_v if pair[0] % 2 == 0]
    partner1 = after(partner1, inside, sums)
    u, v = early_tiles(place, sketches, partner1, near1)
    other1 = send(partner1, swap)
    behind1 = send(after(inverse, partner1), [(i, (i + 1) % size) for i in blocks])
    behind2 = send(after(inverse, partner1), [(i, (i + 2) % size) for i in blocks])
    for bit in bits[:-4]:
        kept, came = halve(sums, bit, partner1)
        sums = kept + came
    kept, came = halve(sums, bits[-4], u)
    partner2, near2, u, v, behind1, behind2, came = lax.optimization_barrier(
        (partner2, near2, u, v, behind1, behind2, came)
    )
    other2 = send(partner2, swap)
    u, v = late_tiles(place, side2, partner2, near2, u, v)
    ur, vr = send(u, across), send(v, back_v)
    kept, came = halve(kept + came, bits[-3], u)
    x = cross_tile(place, sketches, near1, near2, after(other1, u), after(other2, u))
    y, z = send(x, back_y), send(x, back_z)

    gram, row_mass2, column_mass2 = join(
        second_kernel, 1, scale, place, (ur, vr, v), inverse, behind2
    )
    kept, came = halve(kept + after(came, row_mass2), bits[-2])
    y, sums = lax.optimization_barrier((y, kept + came))
    gram, row_mass1, column_mass1 = join(
        first_kernel, 0, scale, place, (y, z, x, inside), inverse, behind1, (gram,)
    )
    kept, came = halve(sums, bits[-1], row_mass1)
    domain_scores = (kept + came) * (1.0 / math.sqrt(rows / DOM_DEV))
    mass = (
        row_mass1[0]
        + row_mass2[0]
        + send(column_mass1[0], [(i, (i - 1) % size) for i in blocks])
        + send(after(column_mass2[0], row_mass1), [(i, (i - 2) % size) for i in blocks])
    )
    redundancy = mass / float(2 * ROUNDS * rows)
    return (gram, redundancy, domain_scores)


def solution(mesh):
    in_specs = (P(("groups", "blocks"), None), P(), P(("groups", "blocks")))
    out_specs = (
        P(None, ("groups", "blocks"), None),
        P(("groups", "blocks")),
        P(("groups", "blocks"), None),
    )
    return jax.shard_map(local, mesh=mesh, in_specs=in_specs, out_specs=out_specs, check_vma=False)
```

```python
import functools
import math

import jax
import jax.numpy as jnp
from jax import lax
from jax.experimental import pallas as pl
from jax.experimental.pallas import tpu as pltpu
from jax.sharding import PartitionSpec as P

ROUNDS = 2
DOM_DEV = 4
DEPTH = 1024
TALL = 384
BAND = 256
PIECES = 4
NT = (((1,), (1,)), ((), ()))
VMEM_LIMIT = 40 * 2**20


def send(value, pairs):
    return lax.ppermute(value, "blocks", pairs)


def after(value, *others):
    return lax.optimization_barrier((value, *others))[0]


def inverse_norm(matrix):
    values = matrix.astype(jnp.float32)
    return lax.rsqrt(jnp.mean(values * values, axis=1) + 1e-06)


def nt(left, right):
    return lax.dot_general(left, right, NT, preferred_element_type=jnp.float32)


def params():
    return pltpu.CompilerParams(vmem_limit_bytes=VMEM_LIMIT)


def cost(flops, bytes_accessed):
    return pl.CostEstimate(flops=flops, bytes_accessed=bytes_accessed, transcendentals=0)


def clear(*totals):
    @pl.when(pl.program_id(0) == 0)
    def _():
        for total in totals:
            total[...] = jnp.zeros_like(total)


def halves_kernel(start, sides, place, own, *rest):
    count = len(sides)
    outs, (buffer, reads, writes) = rest[:count], rest[count:]
    rows, width = outs[0].shape
    half = own.shape[1] // 2
    piece = rows // PIECES
    inward, outward = [], []
    for number, (side, out) in enumerate(zip(sides, outs)):
        left = pl.multiple_of(((place[0] + side) % 2) * half + start, 128)
        for i in range(PIECES):
            part = pl.ds(i * piece, piece)
            slot = number * PIECES + i
            held = buffer.at[number, part]
            inward.append(
                pltpu.make_async_copy(own.at[part, pl.ds(left, width)], held, reads.at[slot])
            )
            outward.append(pltpu.make_async_copy(held, out.at[part], writes.at[slot]))
    for copy in inward:
        copy.start()
    for arrived, copy in zip(inward, outward):
        arrived.wait()
        copy.start()
    for copy in outward:
        copy.wait()


def halves(place, own, start, width, sides):
    rows = own.shape[0]
    slots = PIECES * len(sides)
    anywhere = pl.BlockSpec(memory_space=pltpu.HBM)
    return pl.pallas_call(
        functools.partial(halves_kernel, start, sides),
        in_specs=[pl.BlockSpec(memory_space=pltpu.SMEM), anywhere],
        out_specs=[anywhere] * len(sides),
        out_shape=[jax.ShapeDtypeStruct((rows, width), own.dtype) for _ in sides],
        scratch_shapes=[
            pltpu.VMEM((len(sides), rows, width), own.dtype),
            pltpu.SemaphoreType.DMA((slots,)),
            pltpu.SemaphoreType.DMA((slots,)),
        ],
        compiler_params=params(),
        cost_estimate=cost(0, 4 * rows * width * len(sides)),
    )(place, own)


def early_kernel(place, own, partner, near, u, v):
    clear(u, v)

    @pl.when(place[0] == 0)
    def _():
        u[...] += nt(partner[...], own[...])
        v[...] += nt(near[...], partner[...])

    @pl.when(place[0] == 1)
    def _():
        u[...] += nt(partner[...], near[...])
        v[...] += nt(own[...], partner[...])


def early_tiles(place, own, partner, near):
    rows, width = partner.shape
    half = own.shape[1] // 2
    block = pl.BlockSpec((rows, DEPTH), lambda k, place: (0, k))
    mine = pl.BlockSpec((rows, DEPTH), lambda k, place: (0, place[0] * (half // DEPTH) + k))
    whole = pl.BlockSpec((rows, rows), lambda k, place: (0, 0))
    return pl.pallas_call(
        early_kernel,
        grid_spec=pltpu.PrefetchScalarGridSpec(
            num_scalar_prefetch=1,
            grid=(width // DEPTH,),
            in_specs=[mine, block, block],
            out_specs=[whole] * 2,
        ),
        out_shape=[jax.ShapeDtypeStruct((rows, rows), jnp.float32)] * 2,
        compiler_params=params(),
        cost_estimate=cost(rows, rows),
    )(place, own, partner, near)


def late_kernel(place, mine, partner, near, u, v, u_out, v_out):
    def add(s, w):
        for start in range(0, u.shape[0], BAND):
            rows = pl.ds(start, BAND)
            u_out[rows, :] = (u[rows, :] + nt(partner[rows, :], s[...])).astype(u_out.dtype)
            v_out[rows, :] = (v[rows, :] + nt(w[rows, :], partner[...])).astype(v_out.dtype)

    @pl.when(place[0] == 0)
    def _():
        add(mine, near)

    @pl.when(place[0] == 1)
    def _():
        add(near, mine)


def late_tiles(place, mine, partner, near, u, v):
    rows, width = partner.shape
    return pl.pallas_call(
        late_kernel,
        in_specs=[pl.BlockSpec(memory_space=pltpu.SMEM)]
        + [pl.BlockSpec(memory_space=pltpu.VMEM)] * 5,
        out_specs=[pl.BlockSpec(memory_space=pltpu.VMEM)] * 2,
        out_shape=[pltpu.VMEM((rows, rows), jnp.bfloat16)] * 2,
        compiler_params=params(),
        cost_estimate=cost(60000 * rows * rows, 160 * rows * rows),
    )(place, mine, partner, near, u, v)


def cross_kernel(place, own, near1, near2, other1, other2, out, x):
    clear(x)
    step = pl.program_id(0)
    last = pl.num_programs(0) - 1
    code = place[0] * 2 + place[1]

    def add(near, other):
        pairs = ((near, other), (other, own), (own, other), (other, near))
        for number, (left, right) in enumerate(pairs):

            @pl.when(code == number)
            def _(left=left, right=right):
                x[...] += nt(left[...], right[...])

    pl.when(step < last)(functools.partial(add, near1, other1))
    pl.when(step == last)(functools.partial(add, near2, other2))

    @pl.when(step == last)
    def _():
        out[...] = x[...].astype(out.dtype)


def cross_tile(place, own, near1, near2, other1, other2):
    rows, width = near1.shape
    steps = own.shape[1] // 2 // DEPTH
    block1 = pl.BlockSpec((rows, DEPTH), lambda k, place: (0, jnp.minimum(k, steps - 2)))
    block2 = pl.BlockSpec((rows, DEPTH), lambda k, place: (0, 0))
    mine = pl.BlockSpec((rows, DEPTH), lambda k, place: (0, place[0] * steps + k))
    return pl.pallas_call(
        cross_kernel,
        grid_spec=pltpu.PrefetchScalarGridSpec(
            num_scalar_prefetch=1,
            grid=(steps,),
            in_specs=[mine] + [block1, block2] * 2,
            out_specs=pl.BlockSpec((rows, rows), lambda k, place: (0, 0)),
            scratch_shapes=[pltpu.VMEM((rows, rows), jnp.float32)],
        ),
        out_shape=jax.ShapeDtypeStruct((rows, rows), jnp.bfloat16),
        compiler_params=params(),
        cost_estimate=cost(2 * rows * rows * width, 6 * rows * width),
    )(place, own, near1, near2, other1, other2)


def finish(tile, gram, row_mass, column_mass):
    @pl.when(pl.program_id(0) == 0)
    def _():
        column_mass[...] = jnp.zeros_like(column_mass)

    gram[0] = tile
    squared = tile * tile
    column_mass[...] += jnp.sum(squared, axis=0, keepdims=True)
    sums = jnp.sum(squared, axis=1, keepdims=True)
    size = sums.shape[0]
    row_mass[...] = jnp.broadcast_to(sums, (size, size)).T[0:1]


def second_kernel(scale, place, u, v, kept, inverse, behind, gram, row_mass, column_mass):
    other = jnp.where(place[0] == 1, kept[...], v[...])
    tile = u[...].astype(jnp.float32) + other.astype(jnp.float32)
    finish(tile * inverse[...] * behind[...] * scale, gram, row_mass, column_mass)


def first_kernel(
    scale, place, y, z, kept, local, inverse, behind, gram_in, gram, row_mass, column_mass
):
    del gram_in
    other = jnp.where(place[0] == 1, kept[...], z[...])
    tile = y[...].astype(jnp.float32) + other.astype(jnp.float32)
    tile = jnp.where(place[1] == 1, local[...], tile)
    finish(tile * inverse[...] * behind[...] * scale, gram, row_mass, column_mass)


def mass_shapes(rows):
    specs = [
        pl.BlockSpec((1, TALL), lambda j, *_: (0, j)),
        pl.BlockSpec((1, rows), lambda j, *_: (0, 0)),
    ]
    return specs, [jax.ShapeDtypeStruct((1, rows), jnp.float32)] * 2


def join(kernel, index, scale, place, tiles, inverse, behind, gram=()):
    rows = tiles[0].shape[0]
    mass_specs, mass_types = mass_shapes(rows)
    return pl.pallas_call(
        functools.partial(kernel, scale),
        grid_spec=pltpu.PrefetchScalarGridSpec(
            num_scalar_prefetch=1,
            grid=(rows // TALL,),
            in_specs=[pl.BlockSpec((TALL, rows), lambda j, place: (j, 0))] * len(tiles)
            + [
                pl.BlockSpec((TALL, 1), lambda j, place: (j, 0)),
                pl.BlockSpec((1, rows), lambda j, place: (0, 0)),
            ]
            + [pl.BlockSpec(memory_space=pl.ANY)] * len(gram),
            out_specs=[pl.BlockSpec((1, TALL, rows), lambda j, place: (index, j, 0))] + mass_specs,
        ),
        out_shape=[jax.ShapeDtypeStruct((2, rows, rows), jnp.float32)] + mass_types,
        input_output_aliases={len(tiles) + 3: 0} if gram else {},
        compiler_params=params(),
        cost_estimate=cost(60000 * rows * rows, 160 * rows * rows)
        if index
        else cost(8 * rows * rows, 12 * rows * rows),
    )(place, *tiles, inverse[:, None], behind[None, :], *gram)


def local(sketches, test_sketches, domain_map):
    rows, depth = sketches.shape
    size = lax.axis_size("blocks")
    index = lax.axis_index("blocks")
    half = depth // 2
    first = half - DEPTH
    blocks = range(size)
    upper = (index // 2) % 2
    core = index % 2
    place = jnp.stack([upper, core]).astype(jnp.int32)

    across = [(i, i ^ 2) for i in blocks]
    along = [(i, (i + (4 if i & 2 else -4)) % size) for i in blocks]
    swap = [(i, i ^ 1) for i in blocks]

    even = send(sketches, swap)
    out1, side1 = halves(place, sketches, 0, first, (1, 0))
    partner1 = send(out1, across)
    near1 = send(side1, along)
    out2, side2 = halves(place, after(sketches, side1), first, DEPTH, (1, 0))
    partner2 = send(out2, across)
    near2 = send(side2, along)

    inverse = inverse_norm(sketches)
    scale = 1.0 / math.sqrt(depth)

    test_inverse = inverse_norm(test_sketches)
    similarity = (
        nt(sketches, test_sketches) * inverse[:, None] * test_inverse[None, :] * scale
    ).astype(jnp.bfloat16)
    members = (
        domain_map[:, None] == lax.iota(jnp.int32, DOM_DEV * size)[None, :]
    ).astype(jnp.bfloat16)
    sums = lax.dot_general(
        members, similarity, (((0,), (0,)), ((), ())), preferred_element_type=jnp.float32
    )
    inside = nt(sketches, even)

    def halve(value, bit, *waits):
        count = value.shape[0] // 2
        mine = (index // bit) % 2
        away = lax.dynamic_slice_in_dim(value, (1 - mine) * count, count)
        kept = lax.dynamic_slice_in_dim(value, mine * count, count)
        return kept, send(after(away, *waits), [(i, i ^ bit) for i in blocks])

    bits = [size >> (step + 1) for step in range(size.bit_length() - 1)]
    back_v = [(i, (i + 4) % size) for i in blocks if not i & 2]
    back_y = [(i, i ^ 3) for i in blocks if i & 1]
    back_z = [pair for pair in back_v if pair[0] % 2 == 0]
    partner1 = after(partner1, inside, sums)
    u, v = early_tiles(place, sketches, partner1, near1)
    other1 = send(partner1, swap)
    behind1 = send(after(inverse, partner1), [(i, (i + 1) % size) for i in blocks])
    for bit in bits[:-4]:
        kept, came = halve(sums, bit, partner1)
        sums = kept + came
    kept, came = halve(sums, bits[-4], u)
    partner2, near2, u, v, behind1, came = lax.optimization_barrier(
        (partner2, near2, u, v, behind1, came)
    )
    behind2 = send(after(inverse, partner2), [(i, (i + 2) % size) for i in blocks])
    u, v = late_tiles(place, side2, partner2, near2, u, v)
    u, v, behind2 = lax.optimization_barrier((u, v, behind2))
    other2 = send(after(partner2, u), swap)
    ur, vr = send(u, across), send(v, back_v)
    kept, came = halve(kept + came, bits[-3], u)
    x = cross_tile(place, sketches, near1, near2, after(other1, u), other2)
    y, z = send(x, back_y), send(x, back_z)

    gram, row_mass2, column_mass2 = join(
        second_kernel, 1, scale, place, (ur, vr, v), inverse, behind2
    )
    kept, came = halve(kept + after(came, row_mass2), bits[-2])
    kept, came = halve(kept + came, bits[-1])
    y, sums = lax.optimization_barrier((y, kept + came))
    gram, row_mass1, column_mass1 = join(
        first_kernel, 0, scale, place, (y, z, x, inside), inverse, behind1, (gram,)
    )
    domain_scores = sums * (1.0 / math.sqrt(rows / DOM_DEV))
    mass = (
        row_mass1[0]
        + row_mass2[0]
        + send(column_mass1[0], [(i, (i - 1) % size) for i in blocks])
        + send(after(column_mass2[0], row_mass1), [(i, (i - 2) % size) for i in blocks])
    )
    redundancy = mass / float(2 * ROUNDS * rows)
    return (gram, redundancy, domain_scores)


def solution(mesh):
    in_specs = (P(("groups", "blocks"), None), P(), P(("groups", "blocks")))
    out_specs = (
        P(None, ("groups", "blocks"), None),
        P(("groups", "blocks")),
        P(("groups", "blocks"), None),
    )
    return jax.shard_map(local, mesh=mesh, in_specs=in_specs, out_specs=out_specs, check_vma=False)
```

```python
import functools
import math

import jax
import jax.numpy as jnp
from jax import lax
from jax.experimental import pallas as pl
from jax.experimental.pallas import tpu as pltpu
from jax.sharding import PartitionSpec as P

ROUNDS = 2
DOM_DEV = 4
DEPTH = 1024
TALL = 384
BAND = 256
PIECES = 4
NT = (((1,), (1,)), ((), ()))
VMEM_LIMIT = 40 * 2**20


def send(value, pairs):
    return lax.ppermute(value, "blocks", pairs)


def after(value, *others):
    return lax.optimization_barrier((value, *others))[0]


def inverse_norm(matrix):
    values = matrix.astype(jnp.float32)
    return lax.rsqrt(jnp.mean(values * values, axis=1) + 1e-06)


def nt(left, right):
    return lax.dot_general(left, right, NT, preferred_element_type=jnp.float32)


def params():
    return pltpu.CompilerParams(vmem_limit_bytes=VMEM_LIMIT)


def cost(flops, bytes_accessed):
    return pl.CostEstimate(flops=flops, bytes_accessed=bytes_accessed, transcendentals=0)


def clear(*totals):
    @pl.when(pl.program_id(0) == 0)
    def _():
        for total in totals:
            total[...] = jnp.zeros_like(total)


def halves_kernel(start, sides, place, own, *rest):
    count = len(sides)
    outs, (buffer, reads, writes) = rest[:count], rest[count:]
    rows, width = outs[0].shape
    half = own.shape[1] // 2
    piece = rows // PIECES
    inward, outward = [], []
    for number, (side, out) in enumerate(zip(sides, outs)):
        left = pl.multiple_of(((place[0] + side) % 2) * half + start, 128)
        for i in range(PIECES):
            part = pl.ds(i * piece, piece)
            slot = number * PIECES + i
            held = buffer.at[number, part]
            inward.append(
                pltpu.make_async_copy(own.at[part, pl.ds(left, width)], held, reads.at[slot])
            )
            outward.append(pltpu.make_async_copy(held, out.at[part], writes.at[slot]))
    for copy in inward:
        copy.start()
    for arrived, copy in zip(inward, outward):
        arrived.wait()
        copy.start()
    for copy in outward:
        copy.wait()


def halves(place, own, start, width, sides):
    rows = own.shape[0]
    slots = PIECES * len(sides)
    anywhere = pl.BlockSpec(memory_space=pltpu.HBM)
    return pl.pallas_call(
        functools.partial(halves_kernel, start, sides),
        in_specs=[pl.BlockSpec(memory_space=pltpu.SMEM), anywhere],
        out_specs=[anywhere] * len(sides),
        out_shape=[jax.ShapeDtypeStruct((rows, width), own.dtype) for _ in sides],
        scratch_shapes=[
            pltpu.VMEM((len(sides), rows, width), own.dtype),
            pltpu.SemaphoreType.DMA((slots,)),
            pltpu.SemaphoreType.DMA((slots,)),
        ],
        compiler_params=params(),
        cost_estimate=cost(0, 4 * rows * width * len(sides)),
    )(place, own)


def early_kernel(place, own, partner, near, u, v):
    clear(u, v)

    @pl.when(place[0] == 0)
    def _():
        u[...] += nt(partner[...], own[...])
        v[...] += nt(near[...], partner[...])

    @pl.when(place[0] == 1)
    def _():
        u[...] += nt(partner[...], near[...])
        v[...] += nt(own[...], partner[...])


def early_tiles(place, own, partner, near):
    rows, width = partner.shape
    half = own.shape[1] // 2
    block = pl.BlockSpec((rows, DEPTH), lambda k, place: (0, k))
    mine = pl.BlockSpec((rows, DEPTH), lambda k, place: (0, place[0] * (half // DEPTH) + k))
    whole = pl.BlockSpec((rows, rows), lambda k, place: (0, 0))
    return pl.pallas_call(
        early_kernel,
        grid_spec=pltpu.PrefetchScalarGridSpec(
            num_scalar_prefetch=1,
            grid=(width // DEPTH,),
            in_specs=[mine, block, block],
            out_specs=[whole] * 2,
        ),
        out_shape=[jax.ShapeDtypeStruct((rows, rows), jnp.float32)] * 2,
        compiler_params=params(),
        cost_estimate=cost(rows, rows),
    )(place, own, partner, near)


def late_kernel(place, mine, partner, near, u, v, u_out, v_out):
    def add(s, w):
        for start in range(0, u.shape[0], BAND):
            rows = pl.ds(start, BAND)
            u_out[rows, :] = (u[rows, :] + nt(partner[rows, :], s[...])).astype(u_out.dtype)
            v_out[rows, :] = (v[rows, :] + nt(w[rows, :], partner[...])).astype(v_out.dtype)

    @pl.when(place[0] == 0)
    def _():
        add(mine, near)

    @pl.when(place[0] == 1)
    def _():
        add(near, mine)


def late_tiles(place, mine, partner, near, u, v):
    rows, width = partner.shape
    return pl.pallas_call(
        late_kernel,
        in_specs=[pl.BlockSpec(memory_space=pltpu.SMEM)]
        + [pl.BlockSpec(memory_space=pltpu.VMEM)] * 5,
        out_specs=[pl.BlockSpec(memory_space=pltpu.VMEM)] * 2,
        out_shape=[pltpu.VMEM((rows, rows), jnp.bfloat16)] * 2,
        compiler_params=params(),
        cost_estimate=cost(60000 * rows * rows, 160 * rows * rows),
    )(place, mine, partner, near, u, v)


def cross_kernel(place, own, near1, near2, other1, other2, out, x):
    clear(x)
    step = pl.program_id(0)
    last = pl.num_programs(0) - 1
    code = place[0] * 2 + place[1]

    def add(near, other):
        pairs = ((near, other), (other, own), (own, other), (other, near))
        for number, (left, right) in enumerate(pairs):

            @pl.when(code == number)
            def _(left=left, right=right):
                x[...] += nt(left[...], right[...])

    pl.when(step < last)(functools.partial(add, near1, other1))
    pl.when(step == last)(functools.partial(add, near2, other2))

    @pl.when(step == last)
    def _():
        out[...] = x[...].astype(out.dtype)


def cross_tile(place, own, near1, near2, other1, other2):
    rows, width = near1.shape
    steps = own.shape[1] // 2 // DEPTH
    block1 = pl.BlockSpec((rows, DEPTH), lambda k, place: (0, jnp.minimum(k, steps - 2)))
    block2 = pl.BlockSpec((rows, DEPTH), lambda k, place: (0, 0))
    mine = pl.BlockSpec((rows, DEPTH), lambda k, place: (0, place[0] * steps + k))
    return pl.pallas_call(
        cross_kernel,
        grid_spec=pltpu.PrefetchScalarGridSpec(
            num_scalar_prefetch=1,
            grid=(steps,),
            in_specs=[mine] + [block1, block2] * 2,
            out_specs=pl.BlockSpec((rows, rows), lambda k, place: (0, 0)),
            scratch_shapes=[pltpu.VMEM((rows, rows), jnp.float32)],
        ),
        out_shape=jax.ShapeDtypeStruct((rows, rows), jnp.bfloat16),
        compiler_params=params(),
        cost_estimate=cost(2 * rows * rows * width, 6 * rows * width),
    )(place, own, near1, near2, other1, other2)


def inside_kernel(place, mine, other, out):
    clear(out)

    @pl.when(place[1] == 1)
    def _():
        out[...] += nt(mine[...], other[...])


def inside_tile(place, mine, other):
    rows, depth = mine.shape
    block = pl.BlockSpec((rows, DEPTH), lambda k, place: (0, k))
    return pl.pallas_call(
        inside_kernel,
        grid_spec=pltpu.PrefetchScalarGridSpec(
            num_scalar_prefetch=1,
            grid=(depth // DEPTH,),
            in_specs=[block, block],
            out_specs=pl.BlockSpec((rows, rows), lambda k, place: (0, 0)),
        ),
        out_shape=jax.ShapeDtypeStruct((rows, rows), jnp.float32),
        compiler_params=params(),
        cost_estimate=cost(2 * rows * rows * depth, 4 * rows * depth),
    )(place, mine, other)


def finish(tile, gram, row_mass, column_mass):
    @pl.when(pl.program_id(0) == 0)
    def _():
        column_mass[...] = jnp.zeros_like(column_mass)

    gram[0] = tile
    squared = tile * tile
    column_mass[...] += jnp.sum(squared, axis=0, keepdims=True)
    sums = jnp.sum(squared, axis=1, keepdims=True)
    size = sums.shape[0]
    row_mass[...] = jnp.broadcast_to(sums, (size, size)).T[0:1]


def second_kernel(scale, place, u, v, kept, inverse, behind, gram, row_mass, column_mass):
    other = jnp.where(place[0] == 1, kept[...], v[...])
    tile = u[...].astype(jnp.float32) + other.astype(jnp.float32)
    finish(tile * inverse[...] * behind[...] * scale, gram, row_mass, column_mass)


def first_kernel(
    scale, place, y, z, kept, local, inverse, behind, gram_in, gram, row_mass, column_mass
):
    del gram_in
    other = jnp.where(place[0] == 1, kept[...], z[...])
    tile = y[...].astype(jnp.float32) + other.astype(jnp.float32)
    tile = jnp.where(place[1] == 1, local[...], tile)
    finish(tile * inverse[...] * behind[...] * scale, gram, row_mass, column_mass)


def mass_shapes(rows):
    specs = [
        pl.BlockSpec((1, TALL), lambda j, *_: (0, j)),
        pl.BlockSpec((1, rows), lambda j, *_: (0, 0)),
    ]
    return specs, [jax.ShapeDtypeStruct((1, rows), jnp.float32)] * 2


def join(kernel, index, scale, place, tiles, inverse, behind, gram=()):
    rows = tiles[0].shape[0]
    mass_specs, mass_types = mass_shapes(rows)
    return pl.pallas_call(
        functools.partial(kernel, scale),
        grid_spec=pltpu.PrefetchScalarGridSpec(
            num_scalar_prefetch=1,
            grid=(rows // TALL,),
            in_specs=[pl.BlockSpec((TALL, rows), lambda j, place: (j, 0))] * len(tiles)
            + [
                pl.BlockSpec((TALL, 1), lambda j, place: (j, 0)),
                pl.BlockSpec((1, rows), lambda j, place: (0, 0)),
            ]
            + [pl.BlockSpec(memory_space=pl.ANY)] * len(gram),
            out_specs=[pl.BlockSpec((1, TALL, rows), lambda j, place: (index, j, 0))] + mass_specs,
        ),
        out_shape=[jax.ShapeDtypeStruct((2, rows, rows), jnp.float32)] + mass_types,
        input_output_aliases={len(tiles) + 3: 0} if gram else {},
        compiler_params=params(),
        cost_estimate=cost(60000 * rows * rows, 160 * rows * rows)
        if index
        else cost(8 * rows * rows, 12 * rows * rows),
    )(place, *tiles, inverse, behind, *gram)


def local(sketches, test_sketches, domain_map):
    rows, depth = sketches.shape
    size = lax.axis_size("blocks")
    index = lax.axis_index("blocks")
    half = depth // 2
    first = half - DEPTH
    blocks = range(size)
    upper = (index // 2) % 2
    core = index % 2
    place = jnp.stack([upper, core]).astype(jnp.int32)

    across = [(i, i ^ 2) for i in blocks]
    along = [(i, (i + (4 if i & 2 else -4)) % size) for i in blocks]
    swap = [(i, i ^ 1) for i in blocks]

    out1, side1 = halves(place, sketches, 0, first, (1, 0))
    even = send(after(sketches, out1), swap)
    partner1 = send(out1, across)
    near1 = send(side1, along)
    out2, side2 = halves(place, after(sketches, side1), first, DEPTH, (1, 0))
    partner2 = send(out2, across)
    near2 = send(side2, along)

    inverse = inverse_norm(sketches)
    scale = 1.0 / math.sqrt(depth)

    test_inverse = inverse_norm(test_sketches)
    similarity = (
        nt(sketches, test_sketches) * inverse[:, None] * test_inverse[None, :] * scale
    ).astype(jnp.bfloat16)
    members = (
        domain_map[:, None] == lax.iota(jnp.int32, DOM_DEV * size)[None, :]
    ).astype(jnp.bfloat16)
    sums = lax.dot_general(
        members, similarity, (((0,), (0,)), ((), ())), preferred_element_type=jnp.float32
    )
    inside = inside_tile(place, sketches, even)
    across_lanes, down_rows = inverse[None, :], inverse[:, None]

    def doubled(value, bit, *waits):
        return send(after(value, *waits), [(i, i ^ bit) for i in blocks])

    bits = [size >> (step + 1) for step in range(size.bit_length() - 1)]
    back_v = [(i, (i + 4) % size) for i in blocks if not i & 2]
    back_y = [(i, i ^ 3) for i in blocks if i & 1]
    back_z = [pair for pair in back_v if pair[0] % 2 == 0]
    partner1 = after(partner1, inside, sums, across_lanes, down_rows)
    u, v = early_tiles(place, sketches, partner1, near1)
    other1 = send(partner1, swap)
    behind1 = send(after(across_lanes, partner1), [(i, (i + 1) % size) for i in blocks])
    for bit in bits[:-4]:
        sums = sums + doubled(sums, bit, partner1)
    came = doubled(sums, bits[-4], u)
    partner2, near2, u, v, behind1, came = lax.optimization_barrier(
        (partner2, near2, u, v, behind1, came)
    )
    behind2 = send(after(across_lanes, partner2), [(i, (i + 2) % size) for i in blocks])
    u, v = late_tiles(place, side2, partner2, near2, u, v)
    u, v, behind2 = lax.optimization_barrier((u, v, behind2))
    other2 = send(after(partner2, u), swap)
    ur, vr = send(u, across), send(v, back_v)
    sums = sums + came
    came = doubled(sums, bits[-3], u)
    x = cross_tile(place, sketches, near1, near2, after(other1, u), other2)
    y, z = send(x, back_y), send(x, back_z)

    gram, row_mass2, column_mass2 = join(
        second_kernel, 1, scale, place, (ur, vr, v), down_rows, behind2
    )
    sums = sums + after(came, row_mass2)
    sums = sums + doubled(sums, bits[-2])
    came = doubled(sums, bits[-1])
    y, came = lax.optimization_barrier((y, came))
    gram, row_mass1, column_mass1 = join(
        first_kernel, 0, scale, place, (y, z, x, inside), down_rows, behind1, (gram,)
    )
    sums = lax.dynamic_slice_in_dim(sums + came, index * DOM_DEV, DOM_DEV)
    domain_scores = sums * (1.0 / math.sqrt(rows / DOM_DEV))
    mass = (
        row_mass1
        + row_mass2
        + send(column_mass1, [(i, (i - 1) % size) for i in blocks])
        + send(after(column_mass2, row_mass1), [(i, (i - 2) % size) for i in blocks])
    )
    redundancy = mass[0] / float(2 * ROUNDS * rows)
    return (gram, redundancy, domain_scores)


def solution(mesh):
    in_specs = (P(("groups", "blocks"), None), P(), P(("groups", "blocks")))
    out_specs = (
        P(None, ("groups", "blocks"), None),
        P(("groups", "blocks")),
        P(("groups", "blocks"), None),
    )
    return jax.shard_map(local, mesh=mesh, in_specs=in_specs, out_specs=out_specs, check_vma=False)
```

```python
import functools
import math

import jax
import jax.numpy as jnp
from jax import lax
from jax.experimental import pallas as pl
from jax.experimental.pallas import tpu as pltpu
from jax.sharding import PartitionSpec as P

ROUNDS = 2
DOM_DEV = 4
DEPTH = 1024
TALL = 384
BAND = 256
PIECES = 4
NT = (((1,), (1,)), ((), ()))
VMEM_LIMIT = 40 * 2**20


def send(value, pairs):
    return lax.ppermute(value, "blocks", pairs)


def after(value, *others):
    return lax.optimization_barrier((value, *others))[0]


def inverse_norm(matrix):
    values = matrix.astype(jnp.float32)
    return lax.rsqrt(jnp.mean(values * values, axis=1) + 1e-06)


def nt(left, right):
    return lax.dot_general(left, right, NT, preferred_element_type=jnp.float32)


def params():
    return pltpu.CompilerParams(vmem_limit_bytes=VMEM_LIMIT)


def cost(flops, bytes_accessed):
    return pl.CostEstimate(flops=flops, bytes_accessed=bytes_accessed, transcendentals=0)


def clear(*totals):
    @pl.when(pl.program_id(0) == 0)
    def _():
        for total in totals:
            total[...] = jnp.zeros_like(total)


def halves_kernel(start, sides, place, own, *rest):
    count = len(sides)
    outs, (buffer, reads, writes) = rest[:count], rest[count:]
    rows, width = outs[0].shape
    half = own.shape[1] // 2
    piece = rows // PIECES
    inward, outward = [], []
    for number, (side, out) in enumerate(zip(sides, outs)):
        left = pl.multiple_of(((place[0] + side) % 2) * half + start, 128)
        for i in range(PIECES):
            part = pl.ds(i * piece, piece)
            slot = number * PIECES + i
            held = buffer.at[number, part]
            inward.append(
                pltpu.make_async_copy(own.at[part, pl.ds(left, width)], held, reads.at[slot])
            )
            outward.append(pltpu.make_async_copy(held, out.at[part], writes.at[slot]))
    for copy in inward:
        copy.start()
    for arrived, copy in zip(inward, outward):
        arrived.wait()
        copy.start()
    for copy in outward:
        copy.wait()


def halves(place, own, start, width, sides):
    rows = own.shape[0]
    slots = PIECES * len(sides)
    anywhere = pl.BlockSpec(memory_space=pltpu.HBM)
    return pl.pallas_call(
        functools.partial(halves_kernel, start, sides),
        in_specs=[pl.BlockSpec(memory_space=pltpu.SMEM), anywhere],
        out_specs=[anywhere] * len(sides),
        out_shape=[jax.ShapeDtypeStruct((rows, width), own.dtype) for _ in sides],
        scratch_shapes=[
            pltpu.VMEM((len(sides), rows, width), own.dtype),
            pltpu.SemaphoreType.DMA((slots,)),
            pltpu.SemaphoreType.DMA((slots,)),
        ],
        compiler_params=params(),
        cost_estimate=cost(0, 4 * rows * width * len(sides)),
    )(place, own)


def early_kernel(place, own, partner, near, u, v):
    clear(u, v)

    @pl.when(place[0] == 0)
    def _():
        u[...] += nt(partner[...], own[...])
        v[...] += nt(near[...], partner[...])

    @pl.when(place[0] == 1)
    def _():
        u[...] += nt(partner[...], near[...])
        v[...] += nt(own[...], partner[...])


def early_tiles(place, own, partner, near):
    rows, width = partner.shape
    half = own.shape[1] // 2
    block = pl.BlockSpec((rows, DEPTH), lambda k, place: (0, k))
    mine = pl.BlockSpec((rows, DEPTH), lambda k, place: (0, place[0] * (half // DEPTH) + k))
    whole = pl.BlockSpec((rows, rows), lambda k, place: (0, 0))
    return pl.pallas_call(
        early_kernel,
        grid_spec=pltpu.PrefetchScalarGridSpec(
            num_scalar_prefetch=1,
            grid=(width // DEPTH,),
            in_specs=[mine, block, block],
            out_specs=[whole] * 2,
        ),
        out_shape=[jax.ShapeDtypeStruct((rows, rows), jnp.float32)] * 2,
        compiler_params=params(),
        cost_estimate=cost(rows, rows),
    )(place, own, partner, near)


def late_kernel(place, mine, partner, near, u, v, u_out, v_out):
    def add(s, w):
        for start in range(0, u.shape[0], BAND):
            rows = pl.ds(start, BAND)
            u_out[rows, :] = (u[rows, :] + nt(partner[rows, :], s[...])).astype(u_out.dtype)
            v_out[rows, :] = (v[rows, :] + nt(w[rows, :], partner[...])).astype(v_out.dtype)

    @pl.when(place[0] == 0)
    def _():
        add(mine, near)

    @pl.when(place[0] == 1)
    def _():
        add(near, mine)


def late_tiles(place, mine, partner, near, u, v):
    rows, width = partner.shape
    return pl.pallas_call(
        late_kernel,
        in_specs=[pl.BlockSpec(memory_space=pltpu.SMEM)]
        + [pl.BlockSpec(memory_space=pltpu.VMEM)] * 5,
        out_specs=[pl.BlockSpec(memory_space=pltpu.VMEM)] * 2,
        out_shape=[pltpu.VMEM((rows, rows), jnp.bfloat16)] * 2,
        compiler_params=params(),
        cost_estimate=cost(60000 * rows * rows, 160 * rows * rows),
    )(place, mine, partner, near, u, v)


def cross_kernel(place, own, near1, near2, other1, other2, out, x):
    clear(x)
    step = pl.program_id(0)
    last = pl.num_programs(0) - 1
    code = place[0] * 2 + place[1]

    def add(near, other):
        pairs = ((near, other), (other, own), (own, other), (other, near))
        for number, (left, right) in enumerate(pairs):

            @pl.when(code == number)
            def _(left=left, right=right):
                x[...] += nt(left[...], right[...])

    pl.when(step < last)(functools.partial(add, near1, other1))
    pl.when(step == last)(functools.partial(add, near2, other2))

    @pl.when(step == last)
    def _():
        out[...] = x[...].astype(out.dtype)


def cross_tile(place, own, near1, near2, other1, other2):
    rows, width = near1.shape
    steps = own.shape[1] // 2 // DEPTH
    block1 = pl.BlockSpec((rows, DEPTH), lambda k, place: (0, jnp.minimum(k, steps - 2)))
    block2 = pl.BlockSpec((rows, DEPTH), lambda k, place: (0, 0))
    mine = pl.BlockSpec((rows, DEPTH), lambda k, place: (0, place[0] * steps + k))
    return pl.pallas_call(
        cross_kernel,
        grid_spec=pltpu.PrefetchScalarGridSpec(
            num_scalar_prefetch=1,
            grid=(steps,),
            in_specs=[mine] + [block1, block2] * 2,
            out_specs=pl.BlockSpec((rows, rows), lambda k, place: (0, 0)),
            scratch_shapes=[pltpu.VMEM((rows, rows), jnp.float32)],
        ),
        out_shape=jax.ShapeDtypeStruct((rows, rows), jnp.bfloat16),
        compiler_params=params(),
        cost_estimate=cost(2 * rows * rows * width, 6 * rows * width),
    )(place, own, near1, near2, other1, other2)


def inside_kernel(place, mine, other, out):
    clear(out)

    @pl.when(place[1] == 1)
    def _():
        out[...] += nt(mine[...], other[...])


def inside_tile(place, mine, other):
    rows, depth = mine.shape
    block = pl.BlockSpec((rows, DEPTH), lambda k, place: (0, k))
    return pl.pallas_call(
        inside_kernel,
        grid_spec=pltpu.PrefetchScalarGridSpec(
            num_scalar_prefetch=1,
            grid=(depth // DEPTH,),
            in_specs=[block, block],
            out_specs=pl.BlockSpec((rows, rows), lambda k, place: (0, 0)),
        ),
        out_shape=jax.ShapeDtypeStruct((rows, rows), jnp.float32),
        compiler_params=params(),
        cost_estimate=cost(2 * rows * rows * depth, 4 * rows * depth),
    )(place, mine, other)


def finish(tile, gram, row_mass, column_mass):
    @pl.when(pl.program_id(0) == 0)
    def _():
        column_mass[...] = jnp.zeros_like(column_mass)

    gram[0] = tile
    squared = tile * tile
    column_mass[...] += jnp.sum(squared, axis=0, keepdims=True)
    sums = jnp.sum(squared, axis=1, keepdims=True)
    size = sums.shape[0]
    row_mass[...] = jnp.broadcast_to(sums, (size, size)).T[0:1]


def down(row):
    return jnp.broadcast_to(row, (128, row.shape[1])).T[:, 0:1]


def second_kernel(scale, place, u, v, kept, inverse, behind, gram, row_mass, column_mass):
    other = jnp.where(place[0] == 1, kept[...], v[...])
    tile = u[...].astype(jnp.float32) + other.astype(jnp.float32)
    finish(tile * down(inverse[...]) * behind[...] * scale, gram, row_mass, column_mass)


def first_kernel(
    scale, place, y, z, kept, local, inverse, behind, gram_in, gram, row_mass, column_mass
):
    del gram_in
    other = jnp.where(place[0] == 1, kept[...], z[...])
    tile = y[...].astype(jnp.float32) + other.astype(jnp.float32)
    tile = jnp.where(place[1] == 1, local[...], tile)
    finish(tile * down(inverse[...]) * behind[...] * scale, gram, row_mass, column_mass)


def mass_shapes(rows):
    specs = [
        pl.BlockSpec((1, TALL), lambda j, *_: (0, j)),
        pl.BlockSpec((1, rows), lambda j, *_: (0, 0)),
    ]
    return specs, [jax.ShapeDtypeStruct((1, rows), jnp.float32)] * 2


def join(kernel, index, scale, place, tiles, inverse, behind, gram=()):
    rows = tiles[0].shape[0]
    mass_specs, mass_types = mass_shapes(rows)
    return pl.pallas_call(
        functools.partial(kernel, scale),
        grid_spec=pltpu.PrefetchScalarGridSpec(
            num_scalar_prefetch=1,
            grid=(rows // TALL,),
            in_specs=[pl.BlockSpec((TALL, rows), lambda j, place: (j, 0))] * len(tiles)
            + [
                pl.BlockSpec((1, TALL), lambda j, place: (0, j)),
                pl.BlockSpec((1, rows), lambda j, place: (0, 0)),
            ]
            + [pl.BlockSpec(memory_space=pl.ANY)] * len(gram),
            out_specs=[pl.BlockSpec((1, TALL, rows), lambda j, place: (index, j, 0))] + mass_specs,
        ),
        out_shape=[jax.ShapeDtypeStruct((2, rows, rows), jnp.float32)] + mass_types,
        input_output_aliases={len(tiles) + 3: 0} if gram else {},
        compiler_params=params(),
        cost_estimate=cost(60000 * rows * rows, 160 * rows * rows)
        if index
        else cost(8 * rows * rows, 12 * rows * rows),
    )(place, *tiles, inverse, behind, *gram)


def local(sketches, test_sketches, domain_map):
    rows, depth = sketches.shape
    size = lax.axis_size("blocks")
    index = lax.axis_index("blocks")
    half = depth // 2
    first = half - DEPTH
    blocks = range(size)
    upper = (index // 2) % 2
    core = index % 2
    place = jnp.stack([upper, core]).astype(jnp.int32)

    across = [(i, i ^ 2) for i in blocks]
    along = [(i, (i + (4 if i & 2 else -4)) % size) for i in blocks]
    swap = [(i, i ^ 1) for i in blocks]

    out1, side1 = halves(place, sketches, 0, first, (1, 0))
    even = send(after(sketches, out1), swap)
    partner1 = send(out1, across)
    near1 = send(side1, along)
    out2, side2 = halves(place, after(sketches, side1), first, DEPTH, (1, 0))
    partner2 = send(out2, across)
    near2 = send(side2, along)

    inverse = inverse_norm(sketches)
    scale = 1.0 / math.sqrt(depth)

    test_inverse = inverse_norm(test_sketches)
    similarity = (
        nt(sketches, test_sketches) * inverse[:, None] * test_inverse[None, :] * scale
    ).astype(jnp.bfloat16)
    members = (
        domain_map[:, None] == lax.iota(jnp.int32, DOM_DEV * size)[None, :]
    ).astype(jnp.bfloat16)
    sums = lax.dot_general(
        members, similarity, (((0,), (0,)), ((), ())), preferred_element_type=jnp.float32
    )
    inside = inside_tile(place, sketches, even)
    across_lanes = inverse[None, :]

    def doubled(value, bit, *waits):
        return send(after(value, *waits), [(i, i ^ bit) for i in blocks])

    bits = [size >> (step + 1) for step in range(size.bit_length() - 1)]
    back_v = [(i, (i + 4) % size) for i in blocks if not i & 2]
    back_y = [(i, i ^ 3) for i in blocks if i & 1]
    back_z = [pair for pair in back_v if pair[0] % 2 == 0]
    partner1 = after(partner1, inside, sums, across_lanes)
    u, v = early_tiles(place, sketches, partner1, near1)
    other1 = send(partner1, swap)
    behind1 = send(after(across_lanes, partner1), [(i, (i + 1) % size) for i in blocks])
    for bit in bits[:-4]:
        sums = sums + doubled(sums, bit, partner1)
    came = doubled(sums, bits[-4], u)
    partner2, near2, u, v, behind1, came = lax.optimization_barrier(
        (partner2, near2, u, v, behind1, came)
    )
    behind2 = send(after(across_lanes, partner2), [(i, (i + 2) % size) for i in blocks])
    u, v = late_tiles(place, side2, partner2, near2, u, v)
    vr = send(v, back_v)
    ur = send(u, across)
    other2 = send(after(partner2, u, behind2), swap)
    sums = sums + came
    came = doubled(sums, bits[-3], u)
    x = cross_tile(place, sketches, near1, near2, after(other1, u), other2)
    y, z = send(x, back_y), send(x, back_z)

    gram, row_mass2, column_mass2 = join(
        second_kernel, 1, scale, place, (ur, vr, v), across_lanes, behind2
    )
    sums = sums + after(came, row_mass2)
    sums = sums + doubled(sums, bits[-2])
    came = doubled(sums, bits[-1])
    y, came = lax.optimization_barrier((y, came))
    gram, row_mass1, column_mass1 = join(
        first_kernel, 0, scale, place, (y, z, x, inside), across_lanes, behind1, (gram,)
    )
    sums = lax.dynamic_slice_in_dim(sums + came, index * DOM_DEV, DOM_DEV)
    domain_scores = sums * (1.0 / math.sqrt(rows / DOM_DEV))
    mass = (
        row_mass1
        + row_mass2
        + send(column_mass1, [(i, (i - 1) % size) for i in blocks])
        + send(after(column_mass2, row_mass1), [(i, (i - 2) % size) for i in blocks])
    )
    redundancy = mass[0] / float(2 * ROUNDS * rows)
    return (gram, redundancy, domain_scores)


def solution(mesh):
    in_specs = (P(("groups", "blocks"), None), P(), P(("groups", "blocks")))
    out_specs = (
        P(None, ("groups", "blocks"), None),
        P(("groups", "blocks")),
        P(("groups", "blocks"), None),
    )
    return jax.shard_map(local, mesh=mesh, in_specs=in_specs, out_specs=out_specs, check_vma=False)
```

```python
import functools
import math

import jax
import jax.numpy as jnp
from jax import lax
from jax.experimental import pallas as pl
from jax.experimental.pallas import tpu as pltpu
from jax.sharding import PartitionSpec as P

ROUNDS = 2
DOM_DEV = 4
DEPTH = 1024
TALL = 384
BAND = 256
PIECES = 16
NT = (((1,), (1,)), ((), ()))
VMEM_LIMIT = 40 * 2**20


def send(value, pairs):
    return lax.ppermute(value, "blocks", pairs)


def after(value, *others):
    return lax.optimization_barrier((value, *others))[0]


def inverse_norm(matrix):
    values = matrix.astype(jnp.float32)
    return lax.rsqrt(jnp.mean(values * values, axis=1) + 1e-06)


def nt(left, right):
    return lax.dot_general(left, right, NT, preferred_element_type=jnp.float32)


def params():
    return pltpu.CompilerParams(vmem_limit_bytes=VMEM_LIMIT)


def cost(flops, bytes_accessed):
    return pl.CostEstimate(flops=flops, bytes_accessed=bytes_accessed, transcendentals=0)


def clear(*totals):
    @pl.when(pl.program_id(0) == 0)
    def _():
        for total in totals:
            total[...] = jnp.zeros_like(total)


def halves_kernel(start, sides, place, own, *rest):
    count = len(sides)
    outs, (buffer, reads, writes) = rest[:count], rest[count:]
    rows, width = outs[0].shape
    half = own.shape[1] // 2
    piece = rows // PIECES
    inward, outward = [], []
    for number, (side, out) in enumerate(zip(sides, outs)):
        left = pl.multiple_of(((place[0] + side) % 2) * half + start, 128)
        for i in range(PIECES):
            part = pl.ds(i * piece, piece)
            slot = number * PIECES + i
            held = buffer.at[number, part]
            inward.append(
                pltpu.make_async_copy(own.at[part, pl.ds(left, width)], held, reads.at[slot])
            )
            outward.append(pltpu.make_async_copy(held, out.at[part], writes.at[slot]))
    for copy in inward:
        copy.start()
    for arrived, copy in zip(inward, outward):
        arrived.wait()
        copy.start()
    for copy in outward:
        copy.wait()


def halves(place, own, start, width, sides):
    rows = own.shape[0]
    slots = PIECES * len(sides)
    anywhere = pl.BlockSpec(memory_space=pltpu.HBM)
    return pl.pallas_call(
        functools.partial(halves_kernel, start, sides),
        in_specs=[pl.BlockSpec(memory_space=pltpu.SMEM), anywhere],
        out_specs=[anywhere] * len(sides),
        out_shape=[jax.ShapeDtypeStruct((rows, width), own.dtype) for _ in sides],
        scratch_shapes=[
            pltpu.VMEM((len(sides), rows, width), own.dtype),
            pltpu.SemaphoreType.DMA((slots,)),
            pltpu.SemaphoreType.DMA((slots,)),
        ],
        compiler_params=params(),
        cost_estimate=cost(0, 4 * rows * width * len(sides)),
    )(place, own)


def early_kernel(place, own, partner, near, u, v):
    clear(u, v)

    @pl.when(place[0] == 0)
    def _():
        u[...] += nt(partner[...], own[...])
        v[...] += nt(near[...], partner[...])

    @pl.when(place[0] == 1)
    def _():
        u[...] += nt(partner[...], near[...])
        v[...] += nt(own[...], partner[...])


def early_tiles(place, own, partner, near):
    rows, width = partner.shape
    half = own.shape[1] // 2
    block = pl.BlockSpec((rows, DEPTH), lambda k, place: (0, k))
    mine = pl.BlockSpec((rows, DEPTH), lambda k, place: (0, place[0] * (half // DEPTH) + k))
    whole = pl.BlockSpec((rows, rows), lambda k, place: (0, 0))
    return pl.pallas_call(
        early_kernel,
        grid_spec=pltpu.PrefetchScalarGridSpec(
            num_scalar_prefetch=1,
            grid=(width // DEPTH,),
            in_specs=[mine, block, block],
            out_specs=[whole] * 2,
        ),
        out_shape=[jax.ShapeDtypeStruct((rows, rows), jnp.float32)] * 2,
        compiler_params=params(),
        cost_estimate=cost(rows, rows),
    )(place, own, partner, near)


def late_kernel(place, mine, partner, near, u, v, u_out, v_out):
    def add(s, w):
        for start in range(0, u.shape[0], BAND):
            rows = pl.ds(start, BAND)
            u_out[rows, :] = (u[rows, :] + nt(partner[rows, :], s[...])).astype(u_out.dtype)
            v_out[rows, :] = (v[rows, :] + nt(w[rows, :], partner[...])).astype(v_out.dtype)

    @pl.when(place[0] == 0)
    def _():
        add(mine, near)

    @pl.when(place[0] == 1)
    def _():
        add(near, mine)


def late_tiles(place, mine, partner, near, u, v):
    rows, width = partner.shape
    return pl.pallas_call(
        late_kernel,
        in_specs=[pl.BlockSpec(memory_space=pltpu.SMEM)]
        + [pl.BlockSpec(memory_space=pltpu.VMEM)] * 5,
        out_specs=[pl.BlockSpec(memory_space=pltpu.VMEM)] * 2,
        out_shape=[pltpu.VMEM((rows, rows), jnp.bfloat16)] * 2,
        compiler_params=params(),
        cost_estimate=cost(60000 * rows * rows, 160 * rows * rows),
    )(place, mine, partner, near, u, v)


def cross_kernel(place, own, near1, near2, other1, other2, out, x):
    clear(x)
    step = pl.program_id(0)
    last = pl.num_programs(0) - 1
    code = place[0] * 2 + place[1]

    def add(near, other):
        pairs = ((near, other), (other, own), (own, other), (other, near))
        for number, (left, right) in enumerate(pairs):

            @pl.when(code == number)
            def _(left=left, right=right):
                x[...] += nt(left[...], right[...])

    pl.when(step < last)(functools.partial(add, near1, other1))
    pl.when(step == last)(functools.partial(add, near2, other2))

    @pl.when(step == last)
    def _():
        out[...] = x[...].astype(out.dtype)


def cross_tile(place, own, near1, near2, other1, other2):
    rows, width = near1.shape
    steps = own.shape[1] // 2 // DEPTH
    block1 = pl.BlockSpec((rows, DEPTH), lambda k, place: (0, jnp.minimum(k, steps - 2)))
    block2 = pl.BlockSpec((rows, DEPTH), lambda k, place: (0, 0))
    mine = pl.BlockSpec((rows, DEPTH), lambda k, place: (0, place[0] * steps + k))
    return pl.pallas_call(
        cross_kernel,
        grid_spec=pltpu.PrefetchScalarGridSpec(
            num_scalar_prefetch=1,
            grid=(steps,),
            in_specs=[mine] + [block1, block2] * 2,
            out_specs=pl.BlockSpec((rows, rows), lambda k, place: (0, 0)),
            scratch_shapes=[pltpu.VMEM((rows, rows), jnp.float32)],
        ),
        out_shape=jax.ShapeDtypeStruct((rows, rows), jnp.bfloat16),
        compiler_params=params(),
        cost_estimate=cost(2 * rows * rows * width, 6 * rows * width),
    )(place, own, near1, near2, other1, other2)


def inside_kernel(place, mine, other, out):
    clear(out)

    @pl.when(place[1] == 1)
    def _():
        out[...] += nt(mine[...], other[...])


def inside_tile(place, mine, other):
    rows, depth = mine.shape
    block = pl.BlockSpec((rows, DEPTH), lambda k, place: (0, k))
    return pl.pallas_call(
        inside_kernel,
        grid_spec=pltpu.PrefetchScalarGridSpec(
            num_scalar_prefetch=1,
            grid=(depth // DEPTH,),
            in_specs=[block, block],
            out_specs=pl.BlockSpec((rows, rows), lambda k, place: (0, 0)),
        ),
        out_shape=jax.ShapeDtypeStruct((rows, rows), jnp.float32),
        compiler_params=params(),
        cost_estimate=cost(2 * rows * rows * depth, 4 * rows * depth),
    )(place, mine, other)


def finish(tile, gram, row_mass, column_mass):
    @pl.when(pl.program_id(0) == 0)
    def _():
        column_mass[...] = jnp.zeros_like(column_mass)

    gram[0] = tile
    squared = tile * tile
    column_mass[...] += jnp.sum(squared, axis=0, keepdims=True)
    sums = jnp.sum(squared, axis=1, keepdims=True)
    size = sums.shape[0]
    row_mass[...] = jnp.broadcast_to(sums, (size, size)).T[0:1]


def down(row):
    return jnp.broadcast_to(row, (128, row.shape[1])).T[:, 0:1]


def second_kernel(scale, place, u, v, kept, inverse, behind, gram, row_mass, column_mass):
    other = jnp.where(place[0] == 1, kept[...], v[...])
    tile = u[...].astype(jnp.float32) + other.astype(jnp.float32)
    finish(tile * down(inverse[...]) * behind[...] * scale, gram, row_mass, column_mass)


def first_kernel(
    scale, place, y, z, kept, local, inverse, behind, gram_in, gram, row_mass, column_mass
):
    del gram_in
    other = jnp.where(place[0] == 1, kept[...], z[...])
    tile = y[...].astype(jnp.float32) + other.astype(jnp.float32)
    tile = jnp.where(place[1] == 1, local[...], tile)
    finish(tile * down(inverse[...]) * behind[...] * scale, gram, row_mass, column_mass)


def mass_shapes(rows):
    specs = [
        pl.BlockSpec((1, TALL), lambda j, *_: (0, j)),
        pl.BlockSpec((1, rows), lambda j, *_: (0, 0)),
    ]
    return specs, [jax.ShapeDtypeStruct((1, rows), jnp.float32)] * 2


def join(kernel, index, scale, place, tiles, inverse, behind, gram=()):
    rows = tiles[0].shape[0]
    mass_specs, mass_types = mass_shapes(rows)
    return pl.pallas_call(
        functools.partial(kernel, scale),
        grid_spec=pltpu.PrefetchScalarGridSpec(
            num_scalar_prefetch=1,
            grid=(rows // TALL,),
            in_specs=[pl.BlockSpec((TALL, rows), lambda j, place: (j, 0))] * len(tiles)
            + [
                pl.BlockSpec((1, TALL), lambda j, place: (0, j)),
                pl.BlockSpec((1, rows), lambda j, place: (0, 0)),
            ]
            + [pl.BlockSpec(memory_space=pl.ANY)] * len(gram),
            out_specs=[pl.BlockSpec((1, TALL, rows), lambda j, place: (index, j, 0))] + mass_specs,
        ),
        out_shape=[jax.ShapeDtypeStruct((2, rows, rows), jnp.float32)] + mass_types,
        input_output_aliases={len(tiles) + 3: 0} if gram else {},
        compiler_params=params(),
        cost_estimate=cost(60000 * rows * rows, 160 * rows * rows)
        if index
        else cost(8 * rows * rows, 12 * rows * rows),
    )(place, *tiles, inverse, behind, *gram)


def local(sketches, test_sketches, domain_map):
    rows, depth = sketches.shape
    size = lax.axis_size("blocks")
    index = lax.axis_index("blocks")
    half = depth // 2
    first = half - DEPTH
    blocks = range(size)
    upper = (index // 2) % 2
    core = index % 2
    place = jnp.stack([upper, core]).astype(jnp.int32)

    across = [(i, i ^ 2) for i in blocks]
    along = [(i, (i + (4 if i & 2 else -4)) % size) for i in blocks]
    swap = [(i, i ^ 1) for i in blocks]

    out1, side1 = halves(place, sketches, 0, first, (1, 0))
    even = send(after(sketches, out1), swap)
    partner1 = send(out1, across)
    near1 = send(side1, along)
    out2, side2 = halves(place, after(sketches, side1), first, DEPTH, (1, 0))
    partner2 = send(out2, across)
    near2 = send(side2, along)

    inverse = inverse_norm(sketches)
    scale = 1.0 / math.sqrt(depth)

    test_inverse = inverse_norm(test_sketches)
    similarity = (
        nt(sketches, test_sketches) * inverse[:, None] * test_inverse[None, :] * scale
    ).astype(jnp.bfloat16)
    members = (
        domain_map[:, None] == lax.iota(jnp.int32, DOM_DEV * size)[None, :]
    ).astype(jnp.bfloat16)
    sums = lax.dot_general(
        members, similarity, (((0,), (0,)), ((), ())), preferred_element_type=jnp.float32
    )
    inside = inside_tile(place, sketches, even)
    across_lanes = inverse[None, :]

    def doubled(value, bit, *waits):
        return send(after(value, *waits), [(i, i ^ bit) for i in blocks])

    bits = [size >> (step + 1) for step in range(size.bit_length() - 1)]
    back_v = [(i, (i + 4) % size) for i in blocks if not i & 2]
    back_y = [(i, i ^ 3) for i in blocks if i & 1]
    back_z = [pair for pair in back_v if pair[0] % 2 == 0]
    partner1 = after(partner1, inside, sums, across_lanes)
    u, v = early_tiles(place, sketches, partner1, near1)
    behind1 = send(after(across_lanes, partner1), [(i, (i + 1) % size) for i in blocks])
    behind2 = send(after(across_lanes, partner1), [(i, (i + 2) % size) for i in blocks])
    for bit in bits[:-4]:
        sums = sums + doubled(sums, bit, partner1)
    came = doubled(sums, bits[-4], u)
    partner2, near2, u, v, behind1, behind2, came = lax.optimization_barrier(
        (partner2, near2, u, v, behind1, behind2, came)
    )
    other1 = send(after(partner1, partner2), swap)
    u, v = late_tiles(place, side2, partner2, near2, u, v)
    vr = send(v, back_v)
    ur = send(u, across)
    other2 = send(after(partner2, u), swap)
    sums = sums + came
    came = doubled(sums, bits[-3], u)
    x = cross_tile(place, sketches, near1, near2, after(other1, u), other2)
    y, z = send(x, back_y), send(x, back_z)

    gram, row_mass2, column_mass2 = join(
        second_kernel, 1, scale, place, (ur, vr, v), across_lanes, behind2
    )
    sums = sums + after(came, row_mass2)
    sums = sums + doubled(sums, bits[-2])
    came = doubled(sums, bits[-1])
    y, came = lax.optimization_barrier((y, came))
    gram, row_mass1, column_mass1 = join(
        first_kernel, 0, scale, place, (y, z, x, inside), across_lanes, behind1, (gram,)
    )
    sums = lax.dynamic_slice_in_dim(sums + came, index * DOM_DEV, DOM_DEV)
    domain_scores = sums * (1.0 / math.sqrt(rows / DOM_DEV))
    mass = (
        row_mass1
        + row_mass2
        + send(column_mass1, [(i, (i - 1) % size) for i in blocks])
        + send(after(column_mass2, row_mass1), [(i, (i - 2) % size) for i in blocks])
    )
    redundancy = mass[0] / float(2 * ROUNDS * rows)
    return (gram, redundancy, domain_scores)


def solution(mesh):
    in_specs = (P(("groups", "blocks"), None), P(), P(("groups", "blocks")))
    out_specs = (
        P(None, ("groups", "blocks"), None),
        P(("groups", "blocks")),
        P(("groups", "blocks"), None),
    )
    return jax.shard_map(local, mesh=mesh, in_specs=in_specs, out_specs=out_specs, check_vma=False)
```

```python
import functools
import math

import jax
import jax.numpy as jnp
from jax import lax
from jax.experimental import pallas as pl
from jax.experimental.pallas import tpu as pltpu
from jax.sharding import PartitionSpec as P

ROUNDS = 2
DOM_DEV = 4
DEPTH = 1024
TALL = 384
BAND = 256
PIECES = 2
NT = (((1,), (1,)), ((), ()))
VMEM_LIMIT = 40 * 2**20


def send(value, pairs):
    return lax.ppermute(value, "blocks", pairs)


def after(value, *others):
    return lax.optimization_barrier((value, *others))[0]


def inverse_norm(matrix):
    values = matrix.astype(jnp.float32)
    return lax.rsqrt(jnp.mean(values * values, axis=1) + 1e-06)


def nt(left, right):
    return lax.dot_general(left, right, NT, preferred_element_type=jnp.float32)


def params():
    return pltpu.CompilerParams(vmem_limit_bytes=VMEM_LIMIT)


def cost(flops, bytes_accessed):
    return pl.CostEstimate(flops=flops, bytes_accessed=bytes_accessed, transcendentals=0)


def clear(*totals):
    @pl.when(pl.program_id(0) == 0)
    def _():
        for total in totals:
            total[...] = jnp.zeros_like(total)


def halves_kernel(start, sides, place, own, *rest):
    count = len(sides)
    outs, (buffer, reads, writes) = rest[:count], rest[count:]
    rows, width = outs[0].shape
    half = own.shape[1] // 2
    piece = rows // PIECES
    inward, outward = [], []
    for number, (side, out) in enumerate(zip(sides, outs)):
        left = pl.multiple_of(((place[0] + side) % 2) * half + start, 128)
        for i in range(PIECES):
            part = pl.ds(i * piece, piece)
            slot = number * PIECES + i
            held = buffer.at[number, part]
            inward.append(
                pltpu.make_async_copy(own.at[part, pl.ds(left, width)], held, reads.at[slot])
            )
            outward.append(pltpu.make_async_copy(held, out.at[part], writes.at[slot]))
    for copy in inward:
        copy.start()
    for arrived, copy in zip(inward, outward):
        arrived.wait()
        copy.start()
    for copy in outward:
        copy.wait()


def halves(place, own, start, width, sides):
    rows = own.shape[0]
    slots = PIECES * len(sides)
    anywhere = pl.BlockSpec(memory_space=pltpu.HBM)
    return pl.pallas_call(
        functools.partial(halves_kernel, start, sides),
        in_specs=[pl.BlockSpec(memory_space=pltpu.SMEM), anywhere],
        out_specs=[anywhere] * len(sides),
        out_shape=[jax.ShapeDtypeStruct((rows, width), own.dtype) for _ in sides],
        scratch_shapes=[
            pltpu.VMEM((len(sides), rows, width), own.dtype),
            pltpu.SemaphoreType.DMA((slots,)),
            pltpu.SemaphoreType.DMA((slots,)),
        ],
        compiler_params=params(),
        cost_estimate=cost(0, 4 * rows * width * len(sides)),
    )(place, own)


def early_kernel(place, own, partner, near, u, v):
    clear(u, v)

    @pl.when(place[0] == 0)
    def _():
        u[...] += nt(partner[...], own[...])
        v[...] += nt(near[...], partner[...])

    @pl.when(place[0] == 1)
    def _():
        u[...] += nt(partner[...], near[...])
        v[...] += nt(own[...], partner[...])


def early_tiles(place, own, partner, near):
    rows, width = partner.shape
    half = own.shape[1] // 2
    block = pl.BlockSpec((rows, DEPTH), lambda k, place: (0, k))
    mine = pl.BlockSpec((rows, DEPTH), lambda k, place: (0, place[0] * (half // DEPTH) + k))
    whole = pl.BlockSpec((rows, rows), lambda k, place: (0, 0))
    return pl.pallas_call(
        early_kernel,
        grid_spec=pltpu.PrefetchScalarGridSpec(
            num_scalar_prefetch=1,
            grid=(width // DEPTH,),
            in_specs=[mine, block, block],
            out_specs=[whole] * 2,
        ),
        out_shape=[jax.ShapeDtypeStruct((rows, rows), jnp.float32)] * 2,
        compiler_params=params(),
        cost_estimate=cost(rows, rows),
    )(place, own, partner, near)


def late_kernel(place, mine, partner, near, u, v, u_out, v_out):
    def add(s, w):
        for start in range(0, u.shape[0], BAND):
            rows = pl.ds(start, BAND)
            u_out[rows, :] = (u[rows, :] + nt(partner[rows, :], s[...])).astype(u_out.dtype)
            v_out[rows, :] = (v[rows, :] + nt(w[rows, :], partner[...])).astype(v_out.dtype)

    @pl.when(place[0] == 0)
    def _():
        add(mine, near)

    @pl.when(place[0] == 1)
    def _():
        add(near, mine)


def late_tiles(place, mine, partner, near, u, v):
    rows, width = partner.shape
    return pl.pallas_call(
        late_kernel,
        in_specs=[pl.BlockSpec(memory_space=pltpu.SMEM)]
        + [pl.BlockSpec(memory_space=pltpu.VMEM)] * 5,
        out_specs=[pl.BlockSpec(memory_space=pltpu.VMEM)] * 2,
        out_shape=[pltpu.VMEM((rows, rows), jnp.bfloat16)] * 2,
        compiler_params=params(),
        cost_estimate=cost(60000 * rows * rows, 160 * rows * rows),
    )(place, mine, partner, near, u, v)


def cross_kernel(place, own, near1, near2, other1, other2, out, x):
    clear(x)
    step = pl.program_id(0)
    last = pl.num_programs(0) - 1
    code = place[0] * 2 + place[1]

    def add(near, other):
        pairs = ((near, other), (other, own), (own, other), (other, near))
        for number, (left, right) in enumerate(pairs):

            @pl.when(code == number)
            def _(left=left, right=right):
                x[...] += nt(left[...], right[...])

    pl.when(step < last)(functools.partial(add, near1, other1))
    pl.when(step == last)(functools.partial(add, near2, other2))

    @pl.when(step == last)
    def _():
        out[...] = x[...].astype(out.dtype)


def cross_tile(place, own, near1, near2, other1, other2):
    rows, width = near1.shape
    steps = own.shape[1] // 2 // DEPTH
    block1 = pl.BlockSpec((rows, DEPTH), lambda k, place: (0, jnp.minimum(k, steps - 2)))
    block2 = pl.BlockSpec((rows, DEPTH), lambda k, place: (0, 0))
    mine = pl.BlockSpec((rows, DEPTH), lambda k, place: (0, place[0] * steps + k))
    return pl.pallas_call(
        cross_kernel,
        grid_spec=pltpu.PrefetchScalarGridSpec(
            num_scalar_prefetch=1,
            grid=(steps,),
            in_specs=[mine] + [block1, block2] * 2,
            out_specs=pl.BlockSpec((rows, rows), lambda k, place: (0, 0)),
            scratch_shapes=[pltpu.VMEM((rows, rows), jnp.float32)],
        ),
        out_shape=jax.ShapeDtypeStruct((rows, rows), jnp.bfloat16),
        compiler_params=params(),
        cost_estimate=cost(2 * rows * rows * width, 6 * rows * width),
    )(place, own, near1, near2, other1, other2)


def inside_kernel(place, mine, other, out):
    clear(out)

    @pl.when(place[1] == 1)
    def _():
        out[...] += nt(mine[...], other[...])


def inside_tile(place, mine, other):
    rows, depth = mine.shape
    block = pl.BlockSpec((rows, DEPTH), lambda k, place: (0, k))
    return pl.pallas_call(
        inside_kernel,
        grid_spec=pltpu.PrefetchScalarGridSpec(
            num_scalar_prefetch=1,
            grid=(depth // DEPTH,),
            in_specs=[block, block],
            out_specs=pl.BlockSpec((rows, rows), lambda k, place: (0, 0)),
        ),
        out_shape=jax.ShapeDtypeStruct((rows, rows), jnp.float32),
        compiler_params=params(),
        cost_estimate=cost(2 * rows * rows * depth, 4 * rows * depth),
    )(place, mine, other)


def finish(tile, gram, row_mass, column_mass):
    @pl.when(pl.program_id(0) == 0)
    def _():
        column_mass[...] = jnp.zeros_like(column_mass)

    gram[0] = tile
    squared = tile * tile
    column_mass[...] += jnp.sum(squared, axis=0, keepdims=True)
    sums = jnp.sum(squared, axis=1, keepdims=True)
    size = sums.shape[0]
    row_mass[...] = jnp.broadcast_to(sums, (size, size)).T[0:1]


def down(row):
    return jnp.broadcast_to(row, (128, row.shape[1])).T[:, 0:1]


def second_kernel(scale, place, u, v, kept, inverse, behind, gram, row_mass, column_mass):
    other = jnp.where(place[0] == 1, kept[...], v[...])
    tile = u[...].astype(jnp.float32) + other.astype(jnp.float32)
    finish(tile * down(inverse[...]) * behind[...] * scale, gram, row_mass, column_mass)


def first_kernel(
    scale, place, y, z, kept, local, inverse, behind, gram_in, gram, row_mass, column_mass
):
    del gram_in
    other = jnp.where(place[0] == 1, kept[...], z[...])
    tile = y[...].astype(jnp.float32) + other.astype(jnp.float32)
    tile = jnp.where(place[1] == 1, local[...], tile)
    finish(tile * down(inverse[...]) * behind[...] * scale, gram, row_mass, column_mass)


def mass_shapes(rows):
    specs = [
        pl.BlockSpec((1, TALL), lambda j, *_: (0, j)),
        pl.BlockSpec((1, rows), lambda j, *_: (0, 0)),
    ]
    return specs, [jax.ShapeDtypeStruct((1, rows), jnp.float32)] * 2


def join(kernel, index, scale, place, tiles, inverse, behind, gram=()):
    rows = tiles[0].shape[0]
    mass_specs, mass_types = mass_shapes(rows)
    return pl.pallas_call(
        functools.partial(kernel, scale),
        grid_spec=pltpu.PrefetchScalarGridSpec(
            num_scalar_prefetch=1,
            grid=(rows // TALL,),
            in_specs=[pl.BlockSpec((TALL, rows), lambda j, place: (j, 0))] * len(tiles)
            + [
                pl.BlockSpec((1, TALL), lambda j, place: (0, j)),
                pl.BlockSpec((1, rows), lambda j, place: (0, 0)),
            ]
            + [pl.BlockSpec(memory_space=pl.ANY)] * len(gram),
            out_specs=[pl.BlockSpec((1, TALL, rows), lambda j, place: (index, j, 0))] + mass_specs,
        ),
        out_shape=[jax.ShapeDtypeStruct((2, rows, rows), jnp.float32)] + mass_types,
        input_output_aliases={len(tiles) + 3: 0} if gram else {},
        compiler_params=params(),
        cost_estimate=cost(60000 * rows * rows, 160 * rows * rows)
        if index
        else cost(8 * rows * rows, 12 * rows * rows),
    )(place, *tiles, inverse, behind, *gram)


def local(sketches, test_sketches, domain_map):
    rows, depth = sketches.shape
    size = lax.axis_size("blocks")
    index = lax.axis_index("blocks")
    half = depth // 2
    first = half - DEPTH
    blocks = range(size)
    upper = (index // 2) % 2
    core = index % 2
    place = jnp.stack([upper, core]).astype(jnp.int32)

    across = [(i, i ^ 2) for i in blocks]
    along = [(i, (i + (4 if i & 2 else -4)) % size) for i in blocks]
    swap = [(i, i ^ 1) for i in blocks]

    out1, side1 = halves(place, sketches, 0, first, (1, 0))
    even = send(after(sketches, out1), swap)
    partner1 = send(out1, across)
    near1 = send(side1, along)
    out2, side2 = halves(place, after(sketches, side1), first, DEPTH, (1, 0))
    partner2 = send(out2, across)
    near2 = send(side2, along)

    inverse = inverse_norm(sketches)
    scale = 1.0 / math.sqrt(depth)

    test_inverse = inverse_norm(test_sketches)
    similarity = (
        nt(sketches, test_sketches) * inverse[:, None] * test_inverse[None, :] * scale
    ).astype(jnp.bfloat16)
    members = (
        domain_map[:, None] == lax.iota(jnp.int32, DOM_DEV * size)[None, :]
    ).astype(jnp.bfloat16)
    sums = lax.dot_general(
        members, similarity, (((0,), (0,)), ((), ())), preferred_element_type=jnp.float32
    )
    inside = inside_tile(place, sketches, even)
    across_lanes = inverse[None, :]

    def doubled(value, bit, *waits):
        return send(after(value, *waits), [(i, i ^ bit) for i in blocks])

    bits = [size >> (step + 1) for step in range(size.bit_length() - 1)]
    back_v = [(i, (i + 4) % size) for i in blocks if not i & 2]
    back_y = [(i, i ^ 3) for i in blocks if i & 1]
    back_z = [pair for pair in back_v if pair[0] % 2 == 0]
    partner1 = after(partner1, inside, sums, across_lanes)
    u, v = early_tiles(place, sketches, partner1, near1)
    behind1 = send(after(across_lanes, partner1), [(i, (i + 1) % size) for i in blocks])
    behind2 = send(after(across_lanes, partner1), [(i, (i + 2) % size) for i in blocks])
    for bit in bits[:-4]:
        sums = sums + doubled(sums, bit, partner1)
    came = doubled(sums, bits[-4], u)
    partner2, near2, u, v, behind1, behind2, came = lax.optimization_barrier(
        (partner2, near2, u, v, behind1, behind2, came)
    )
    other1 = send(after(partner1, partner2), swap)
    u, v = late_tiles(place, side2, partner2, near2, u, v)
    vr = send(v, back_v)
    ur = send(u, across)
    other2 = send(after(partner2, u), swap)
    sums = sums + came
    came = doubled(sums, bits[-3], u)
    x = cross_tile(place, sketches, near1, near2, after(other1, u), other2)
    y, z = send(x, back_y), send(x, back_z)

    gram, row_mass2, column_mass2 = join(
        second_kernel, 1, scale, place, (ur, vr, v), across_lanes, behind2
    )
    sums = sums + after(came, row_mass2)
    sums = sums + doubled(sums, bits[-2])
    sums = sums + doubled(sums, bits[-1])
    sums = lax.dynamic_slice_in_dim(sums, index * DOM_DEV, DOM_DEV)
    domain_scores = sums * (1.0 / math.sqrt(rows / DOM_DEV))
    y, z, domain_scores = lax.optimization_barrier((y, z, domain_scores))
    from_second = send(after(column_mass2, sums), [(i, (i - 2) % size) for i in blocks])
    gram, row_mass1, column_mass1 = join(
        first_kernel, 0, scale, place, (y, z, x, inside), across_lanes, behind1, (gram,)
    )
    mass = (
        row_mass1
        + row_mass2
        + send(column_mass1, [(i, (i - 1) % size) for i in blocks])
        + from_second
    )
    redundancy = mass[0] / float(2 * ROUNDS * rows)
    return (gram, redundancy, domain_scores)


def solution(mesh):
    in_specs = (P(("groups", "blocks"), None), P(), P(("groups", "blocks")))
    out_specs = (
        P(None, ("groups", "blocks"), None),
        P(("groups", "blocks")),
        P(("groups", "blocks"), None),
    )
    return jax.shard_map(local, mesh=mesh, in_specs=in_specs, out_specs=out_specs, check_vma=False)
```

```python
import functools
import math

import jax
import jax.numpy as jnp
from jax import lax
from jax.experimental import pallas as pl
from jax.experimental.pallas import tpu as pltpu
from jax.sharding import PartitionSpec as P

ROUNDS = 2
DOM_DEV = 4
DEPTH = 1024
TALL = 384
BAND = 256
PIECES = 4
NT = (((1,), (1,)), ((), ()))
VMEM_LIMIT = 40 * 2**20


def send(value, pairs):
    return lax.ppermute(value, "blocks", pairs)


def after(value, *others):
    return lax.optimization_barrier((value, *others))[0]


def inverse_norm(matrix):
    values = matrix.astype(jnp.float32)
    return lax.rsqrt(jnp.mean(values * values, axis=1) + 1e-06)


def nt(left, right):
    return lax.dot_general(left, right, NT, preferred_element_type=jnp.float32)


def params():
    return pltpu.CompilerParams(vmem_limit_bytes=VMEM_LIMIT)


def cost(flops, bytes_accessed):
    return pl.CostEstimate(flops=flops, bytes_accessed=bytes_accessed, transcendentals=0)


def clear(*totals):
    @pl.when(pl.program_id(0) == 0)
    def _():
        for total in totals:
            total[...] = jnp.zeros_like(total)


def halves_kernel(start, sides, place, own, *rest):
    count = len(sides)
    outs, (buffer, reads, writes) = rest[:count], rest[count:]
    rows, width = outs[0].shape
    half = own.shape[1] // 2
    piece = rows // PIECES
    inward, outward = [], []
    for number, (side, out) in enumerate(zip(sides, outs)):
        left = pl.multiple_of(((place[0] + side) % 2) * half + start, 128)
        for i in range(PIECES):
            part = pl.ds(i * piece, piece)
            slot = number * PIECES + i
            held = buffer.at[number, part]
            inward.append(
                pltpu.make_async_copy(own.at[part, pl.ds(left, width)], held, reads.at[slot])
            )
            outward.append(pltpu.make_async_copy(held, out.at[part], writes.at[slot]))
    for copy in inward:
        copy.start()
    for arrived, copy in zip(inward, outward):
        arrived.wait()
        copy.start()
    for copy in outward:
        copy.wait()


def halves(place, own, start, width, sides):
    rows = own.shape[0]
    slots = PIECES * len(sides)
    anywhere = pl.BlockSpec(memory_space=pltpu.HBM)
    return pl.pallas_call(
        functools.partial(halves_kernel, start, sides),
        in_specs=[pl.BlockSpec(memory_space=pltpu.SMEM), anywhere],
        out_specs=[anywhere] * len(sides),
        out_shape=[jax.ShapeDtypeStruct((rows, width), own.dtype) for _ in sides],
        scratch_shapes=[
            pltpu.VMEM((len(sides), rows, width), own.dtype),
            pltpu.SemaphoreType.DMA((slots,)),
            pltpu.SemaphoreType.DMA((slots,)),
        ],
        compiler_params=params(),
        cost_estimate=cost(0, 4 * rows * width * len(sides)),
    )(place, own)


def early_kernel(place, own, partner, near, u, v):
    clear(u, v)

    @pl.when(place[0] == 0)
    def _():
        u[...] += nt(partner[...], own[...])
        v[...] += nt(near[...], partner[...])

    @pl.when(place[0] == 1)
    def _():
        u[...] += nt(partner[...], near[...])
        v[...] += nt(own[...], partner[...])


def early_tiles(place, own, partner, near):
    rows, width = partner.shape
    half = own.shape[1] // 2
    block = pl.BlockSpec((rows, DEPTH), lambda k, place: (0, k))
    mine = pl.BlockSpec((rows, DEPTH), lambda k, place: (0, place[0] * (half // DEPTH) + k))
    whole = pl.BlockSpec((rows, rows), lambda k, place: (0, 0))
    return pl.pallas_call(
        early_kernel,
        grid_spec=pltpu.PrefetchScalarGridSpec(
            num_scalar_prefetch=1,
            grid=(width // DEPTH,),
            in_specs=[mine, block, block],
            out_specs=[whole] * 2,
        ),
        out_shape=[jax.ShapeDtypeStruct((rows, rows), jnp.float32)] * 2,
        compiler_params=params(),
        cost_estimate=cost(rows, rows),
    )(place, own, partner, near)


def late_kernel(place, mine, partner, near, u, v, u_out, v_out):
    def add(s, w):
        for start in range(0, u.shape[0], BAND):
            rows = pl.ds(start, BAND)
            u_out[rows, :] = (u[rows, :] + nt(partner[rows, :], s[...])).astype(u_out.dtype)
            v_out[rows, :] = (v[rows, :] + nt(w[rows, :], partner[...])).astype(v_out.dtype)

    @pl.when(place[0] == 0)
    def _():
        add(mine, near)

    @pl.when(place[0] == 1)
    def _():
        add(near, mine)


def late_tiles(place, mine, partner, near, u, v):
    rows, width = partner.shape
    return pl.pallas_call(
        late_kernel,
        in_specs=[pl.BlockSpec(memory_space=pltpu.SMEM)]
        + [pl.BlockSpec(memory_space=pltpu.VMEM)] * 5,
        out_specs=[pl.BlockSpec(memory_space=pltpu.VMEM)] * 2,
        out_shape=[pltpu.VMEM((rows, rows), jnp.bfloat16)] * 2,
        compiler_params=params(),
        cost_estimate=cost(60000 * rows * rows, 160 * rows * rows),
    )(place, mine, partner, near, u, v)


def cross_kernel(place, own, near1, near2, other1, other2, out, x):
    clear(x)
    step = pl.program_id(0)
    last = pl.num_programs(0) - 1
    code = place[0] * 2 + place[1]

    def add(near, other):
        pairs = ((near, other), (other, own), (own, other), (other, near))
        for number, (left, right) in enumerate(pairs):

            @pl.when(code == number)
            def _(left=left, right=right):
                x[...] += nt(left[...], right[...])

    pl.when(step < last)(functools.partial(add, near1, other1))
    pl.when(step == last)(functools.partial(add, near2, other2))

    @pl.when(step == last)
    def _():
        out[...] = x[...].astype(out.dtype)


def cross_tile(place, own, near1, near2, other1, other2):
    rows, width = near1.shape
    steps = own.shape[1] // 2 // DEPTH
    block1 = pl.BlockSpec((rows, DEPTH), lambda k, place: (0, jnp.minimum(k, steps - 2)))
    block2 = pl.BlockSpec((rows, DEPTH), lambda k, place: (0, 0))
    mine = pl.BlockSpec((rows, DEPTH), lambda k, place: (0, place[0] * steps + k))
    return pl.pallas_call(
        cross_kernel,
        grid_spec=pltpu.PrefetchScalarGridSpec(
            num_scalar_prefetch=1,
            grid=(steps,),
            in_specs=[mine] + [block1, block2] * 2,
            out_specs=pl.BlockSpec((rows, rows), lambda k, place: (0, 0)),
            scratch_shapes=[pltpu.VMEM((rows, rows), jnp.float32)],
        ),
        out_shape=jax.ShapeDtypeStruct((rows, rows), jnp.bfloat16),
        compiler_params=params(),
        cost_estimate=cost(2 * rows * rows * width, 6 * rows * width),
    )(place, own, near1, near2, other1, other2)


def inside_kernel(place, mine, other, out):
    clear(out)

    @pl.when(place[1] == 1)
    def _():
        out[...] += nt(mine[...], other[...])


def inside_tile(place, mine, other):
    rows, depth = mine.shape
    block = pl.BlockSpec((rows, DEPTH), lambda k, place: (0, k))
    return pl.pallas_call(
        inside_kernel,
        grid_spec=pltpu.PrefetchScalarGridSpec(
            num_scalar_prefetch=1,
            grid=(depth // DEPTH,),
            in_specs=[block, block],
            out_specs=pl.BlockSpec((rows, rows), lambda k, place: (0, 0)),
        ),
        out_shape=jax.ShapeDtypeStruct((rows, rows), jnp.float32),
        compiler_params=params(),
        cost_estimate=cost(2 * rows * rows * depth, 4 * rows * depth),
    )(place, mine, other)


def finish(tile, gram, row_mass, column_mass):
    @pl.when(pl.program_id(0) == 0)
    def _():
        column_mass[...] = jnp.zeros_like(column_mass)

    gram[0] = tile
    squared = tile * tile
    column_mass[...] += jnp.sum(squared, axis=0, keepdims=True)
    sums = jnp.sum(squared, axis=1, keepdims=True)
    size = sums.shape[0]
    row_mass[...] = jnp.broadcast_to(sums, (size, size)).T[0:1]


def down(row):
    return jnp.broadcast_to(row, (128, row.shape[1])).T[:, 0:1]


def second_kernel(scale, place, u, v, kept, inverse, behind, gram, row_mass, column_mass):
    other = jnp.where(place[0] == 1, kept[...], v[...])
    tile = u[...].astype(jnp.float32) + other.astype(jnp.float32)
    finish(tile * down(inverse[...]) * behind[...] * scale, gram, row_mass, column_mass)


def first_kernel(
    scale, place, y, z, kept, local, inverse, behind, gram_in, gram, row_mass, column_mass
):
    del gram_in
    other = jnp.where(place[0] == 1, kept[...], z[...])
    tile = y[...].astype(jnp.float32) + other.astype(jnp.float32)
    tile = jnp.where(place[1] == 1, local[...], tile)
    finish(tile * down(inverse[...]) * behind[...] * scale, gram, row_mass, column_mass)


def mass_shapes(rows):
    specs = [
        pl.BlockSpec((1, TALL), lambda j, *_: (0, j)),
        pl.BlockSpec((1, rows), lambda j, *_: (0, 0)),
    ]
    return specs, [jax.ShapeDtypeStruct((1, rows), jnp.float32)] * 2


def join(kernel, index, scale, place, tiles, inverse, behind, gram=()):
    rows = tiles[0].shape[0]
    mass_specs, mass_types = mass_shapes(rows)
    return pl.pallas_call(
        functools.partial(kernel, scale),
        grid_spec=pltpu.PrefetchScalarGridSpec(
            num_scalar_prefetch=1,
            grid=(rows // TALL,),
            in_specs=[pl.BlockSpec((TALL, rows), lambda j, place: (j, 0))] * len(tiles)
            + [
                pl.BlockSpec((1, TALL), lambda j, place: (0, j)),
                pl.BlockSpec((1, rows), lambda j, place: (0, 0)),
            ]
            + [pl.BlockSpec(memory_space=pl.ANY)] * len(gram),
            out_specs=[pl.BlockSpec((1, TALL, rows), lambda j, place: (index, j, 0))] + mass_specs,
        ),
        out_shape=[jax.ShapeDtypeStruct((2, rows, rows), jnp.float32)] + mass_types,
        input_output_aliases={len(tiles) + 3: 0} if gram else {},
        compiler_params=params(),
        cost_estimate=cost(60000 * rows * rows, 160 * rows * rows)
        if index
        else cost(8 * rows * rows, 12 * rows * rows),
    )(place, *tiles, inverse, behind, *gram)


def local(sketches, test_sketches, domain_map):
    rows, depth = sketches.shape
    size = lax.axis_size("blocks")
    index = lax.axis_index("blocks")
    half = depth // 2
    first = half - DEPTH
    blocks = range(size)
    upper = (index // 2) % 2
    core = index % 2
    place = jnp.stack([upper, core]).astype(jnp.int32)

    across = [(i, i ^ 2) for i in blocks]
    along = [(i, (i + (4 if i & 2 else -4)) % size) for i in blocks]
    swap = [(i, i ^ 1) for i in blocks]

    out1, side1 = halves(place, sketches, 0, first, (1, 0))
    even = send(after(sketches, out1), swap)
    partner1 = send(out1, across)
    near1 = send(side1, along)
    out2, side2 = halves(place, after(sketches, side1), first, DEPTH, (1, 0))
    partner2 = send(out2, across)
    near2 = send(side2, along)

    inverse = inverse_norm(sketches)
    scale = 1.0 / math.sqrt(depth)

    test_inverse = inverse_norm(test_sketches)
    similarity = (
        nt(sketches, test_sketches) * inverse[:, None] * test_inverse[None, :] * scale
    ).astype(jnp.bfloat16)
    members = (
        domain_map[:, None] == lax.iota(jnp.int32, DOM_DEV * size)[None, :]
    ).astype(jnp.bfloat16)
    sums = lax.dot_general(
        members, similarity, (((0,), (0,)), ((), ())), preferred_element_type=jnp.float32
    )
    inside = inside_tile(place, sketches, even)
    across_lanes = inverse[None, :]

    def doubled(value, bit, *waits):
        return send(after(value, *waits), [(i, i ^ bit) for i in blocks])

    bits = [size >> (step + 1) for step in range(size.bit_length() - 1)]
    back_v = [(i, (i + 4) % size) for i in blocks if not i & 2]
    back_y = [(i, i ^ 3) for i in blocks if i & 1]
    back_z = [pair for pair in back_v if pair[0] % 2 == 0]
    partner1 = after(partner1, inside, sums, across_lanes)
    u, v = early_tiles(place, sketches, partner1, near1)
    behind1 = send(after(across_lanes, partner1), [(i, (i + 1) % size) for i in blocks])
    behind2 = send(after(across_lanes, partner1), [(i, (i + 2) % size) for i in blocks])
    for bit in bits[:-4]:
        sums = sums + doubled(sums, bit, partner1)
    came = doubled(sums, bits[-4], u)
    partner2, near2, u, v, behind1, behind2, came = lax.optimization_barrier(
        (partner2, near2, u, v, behind1, behind2, came)
    )
    other1 = send(after(partner1, partner2), swap)
    u, v = late_tiles(place, side2, partner2, near2, u, v)
    vr = send(v, back_v)
    ur = send(u, across)
    other2 = send(after(partner2, u), swap)
    sums = sums + came
    came = doubled(sums, bits[-3], u)
    x = cross_tile(place, sketches, near1, near2, after(other1, u), other2)
    y, z = send(x, back_y), send(x, back_z)

    gram, row_mass2, column_mass2 = join(
        second_kernel, 1, scale, place, (ur, vr, v), across_lanes, behind2
    )
    sums = sums + after(came, row_mass2)
    sums = sums + doubled(sums, bits[-2])
    sums = sums + doubled(sums, bits[-1])
    sums = lax.dynamic_slice_in_dim(sums, index * DOM_DEV, DOM_DEV)
    domain_scores = sums * (1.0 / math.sqrt(rows / DOM_DEV))
    y, z, domain_scores = lax.optimization_barrier((y, z, domain_scores))
    gram, row_mass1, column_mass1 = join(
        first_kernel, 0, scale, place, (y, z, x, inside), across_lanes, behind1, (gram,)
    )
    mass = (
        row_mass1
        + row_mass2
        + send(column_mass1, [(i, (i - 1) % size) for i in blocks])
        + send(after(column_mass2, row_mass1), [(i, (i - 2) % size) for i in blocks])
    )
    redundancy = mass[0] / float(2 * ROUNDS * rows)
    return (gram, redundancy, domain_scores)


def solution(mesh):
    in_specs = (P(("groups", "blocks"), None), P(), P(("groups", "blocks")))
    out_specs = (
        P(None, ("groups", "blocks"), None),
        P(("groups", "blocks")),
        P(("groups", "blocks"), None),
    )
    return jax.shard_map(local, mesh=mesh, in_specs=in_specs, out_specs=out_specs, check_vma=False)
```

```python
import functools
import math

import jax
import jax.numpy as jnp
from jax import lax
from jax.experimental import pallas as pl
from jax.experimental.pallas import tpu as pltpu
from jax.sharding import PartitionSpec as P

ROUNDS = 2
DOM_DEV = 4
DEPTH = 1024
TALL = 384
BAND = 256
PIECES = 4
NT = (((1,), (1,)), ((), ()))
VMEM_LIMIT = 40 * 2**20


def send(value, pairs):
    return lax.ppermute(value, "blocks", pairs)


def after(value, *others):
    return lax.optimization_barrier((value, *others))[0]


def inverse_norm(matrix):
    values = matrix.astype(jnp.float32)
    return lax.rsqrt(jnp.mean(values * values, axis=1) + 1e-06)


def nt(left, right):
    return lax.dot_general(left, right, NT, preferred_element_type=jnp.float32)


def params():
    return pltpu.CompilerParams(vmem_limit_bytes=VMEM_LIMIT)


def cost(flops, bytes_accessed):
    return pl.CostEstimate(flops=flops, bytes_accessed=bytes_accessed, transcendentals=0)


def clear(*totals):
    @pl.when(pl.program_id(0) == 0)
    def _():
        for total in totals:
            total[...] = jnp.zeros_like(total)


def halves_kernel(start, sides, place, own, *rest):
    count = len(sides)
    outs, (buffer, reads, writes) = rest[:count], rest[count:]
    rows, width = outs[0].shape
    half = own.shape[1] // 2
    piece = rows // PIECES
    inward, outward = [], []
    for number, (side, out) in enumerate(zip(sides, outs)):
        left = pl.multiple_of(((place[0] + side) % 2) * half + start, 128)
        for i in range(PIECES):
            part = pl.ds(i * piece, piece)
            slot = number * PIECES + i
            held = buffer.at[number, part]
            inward.append(
                pltpu.make_async_copy(own.at[part, pl.ds(left, width)], held, reads.at[slot])
            )
            outward.append(pltpu.make_async_copy(held, out.at[part], writes.at[slot]))
    for copy in inward:
        copy.start()
    for arrived, copy in zip(inward, outward):
        arrived.wait()
        copy.start()
    for copy in outward:
        copy.wait()


def halves(place, own, start, width, sides):
    rows = own.shape[0]
    slots = PIECES * len(sides)
    anywhere = pl.BlockSpec(memory_space=pltpu.HBM)
    return pl.pallas_call(
        functools.partial(halves_kernel, start, sides),
        in_specs=[pl.BlockSpec(memory_space=pltpu.SMEM), anywhere],
        out_specs=[anywhere] * len(sides),
        out_shape=[jax.ShapeDtypeStruct((rows, width), own.dtype) for _ in sides],
        scratch_shapes=[
            pltpu.VMEM((len(sides), rows, width), own.dtype),
            pltpu.SemaphoreType.DMA((slots,)),
            pltpu.SemaphoreType.DMA((slots,)),
        ],
        compiler_params=params(),
        cost_estimate=cost(0, 4 * rows * width * len(sides)),
    )(place, own)


def early_kernel(place, own, partner, near, u, v):
    clear(u, v)

    @pl.when(place[0] == 0)
    def _():
        u[...] += nt(partner[...], own[...])
        v[...] += nt(near[...], partner[...])

    @pl.when(place[0] == 1)
    def _():
        u[...] += nt(partner[...], near[...])
        v[...] += nt(own[...], partner[...])


def early_tiles(place, own, partner, near):
    rows, width = partner.shape
    half = own.shape[1] // 2
    block = pl.BlockSpec((rows, DEPTH), lambda k, place: (0, k))
    mine = pl.BlockSpec((rows, DEPTH), lambda k, place: (0, place[0] * (half // DEPTH) + k))
    whole = pl.BlockSpec((rows, rows), lambda k, place: (0, 0))
    return pl.pallas_call(
        early_kernel,
        grid_spec=pltpu.PrefetchScalarGridSpec(
            num_scalar_prefetch=1,
            grid=(width // DEPTH,),
            in_specs=[mine, block, block],
            out_specs=[whole] * 2,
        ),
        out_shape=[jax.ShapeDtypeStruct((rows, rows), jnp.float32)] * 2,
        compiler_params=params(),
        cost_estimate=cost(rows, rows),
    )(place, own, partner, near)


def late_kernel(place, mine, partner, near, u, v, u_out, v_out):
    def add(s, w):
        for start in range(0, u.shape[0], BAND):
            rows = pl.ds(start, BAND)
            u_out[rows, :] = (u[rows, :] + nt(partner[rows, :], s[...])).astype(u_out.dtype)
            v_out[rows, :] = (v[rows, :] + nt(w[rows, :], partner[...])).astype(v_out.dtype)

    @pl.when(place[0] == 0)
    def _():
        add(mine, near)

    @pl.when(place[0] == 1)
    def _():
        add(near, mine)


def late_tiles(place, mine, partner, near, u, v):
    rows, width = partner.shape
    return pl.pallas_call(
        late_kernel,
        in_specs=[pl.BlockSpec(memory_space=pltpu.SMEM)]
        + [pl.BlockSpec(memory_space=pltpu.VMEM)] * 5,
        out_specs=[pl.BlockSpec(memory_space=pltpu.VMEM)] * 2,
        out_shape=[pltpu.VMEM((rows, rows), jnp.bfloat16)] * 2,
        compiler_params=params(),
        cost_estimate=cost(60000 * rows * rows, 160 * rows * rows),
    )(place, mine, partner, near, u, v)


def cross_kernel(place, own, near1, near2, other1, other2, out, x):
    clear(x)
    step = pl.program_id(0)
    last = pl.num_programs(0) - 1
    code = place[0] * 2 + place[1]

    def add(near, other):
        pairs = ((near, other), (other, own), (own, other), (other, near))
        for number, (left, right) in enumerate(pairs):

            @pl.when(code == number)
            def _(left=left, right=right):
                x[...] += nt(left[...], right[...])

    pl.when(step < last)(functools.partial(add, near1, other1))
    pl.when(step == last)(functools.partial(add, near2, other2))

    @pl.when(step == last)
    def _():
        out[...] = x[...].astype(out.dtype)


def cross_tile(place, own, near1, near2, other1, other2):
    rows, width = near1.shape
    steps = own.shape[1] // 2 // DEPTH
    block1 = pl.BlockSpec((rows, DEPTH), lambda k, place: (0, jnp.minimum(k, steps - 2)))
    block2 = pl.BlockSpec((rows, DEPTH), lambda k, place: (0, 0))
    mine = pl.BlockSpec((rows, DEPTH), lambda k, place: (0, place[0] * steps + k))
    return pl.pallas_call(
        cross_kernel,
        grid_spec=pltpu.PrefetchScalarGridSpec(
            num_scalar_prefetch=1,
            grid=(steps,),
            in_specs=[mine] + [block1, block2] * 2,
            out_specs=pl.BlockSpec((rows, rows), lambda k, place: (0, 0)),
            scratch_shapes=[pltpu.VMEM((rows, rows), jnp.float32)],
        ),
        out_shape=jax.ShapeDtypeStruct((rows, rows), jnp.bfloat16),
        compiler_params=params(),
        cost_estimate=cost(2 * rows * rows * width, 6 * rows * width),
    )(place, own, near1, near2, other1, other2)


def inside_kernel(place, mine, other, out):
    clear(out)

    @pl.when(place[1] == 1)
    def _():
        out[...] += nt(mine[...], other[...])


def inside_tile(place, mine, other):
    rows, depth = mine.shape
    block = pl.BlockSpec((rows, DEPTH), lambda k, place: (0, k))
    return pl.pallas_call(
        inside_kernel,
        grid_spec=pltpu.PrefetchScalarGridSpec(
            num_scalar_prefetch=1,
            grid=(depth // DEPTH,),
            in_specs=[block, block],
            out_specs=pl.BlockSpec((rows, rows), lambda k, place: (0, 0)),
        ),
        out_shape=jax.ShapeDtypeStruct((rows, rows), jnp.float32),
        compiler_params=params(),
        cost_estimate=cost(2 * rows * rows * depth, 4 * rows * depth),
    )(place, mine, other)


def finish(tile, gram, row_mass, column_mass):
    @pl.when(pl.program_id(0) == 0)
    def _():
        column_mass[...] = jnp.zeros_like(column_mass)

    gram[0] = tile
    squared = tile * tile
    column_mass[...] += jnp.sum(squared, axis=0, keepdims=True)
    sums = jnp.sum(squared, axis=1, keepdims=True)
    size = sums.shape[0]
    row_mass[...] = jnp.broadcast_to(sums, (size, size)).T[0:1]


def down(row):
    return jnp.broadcast_to(row, (128, row.shape[1])).T[:, 0:1]


def second_kernel(scale, place, u, v, kept, inverse, behind, gram, row_mass, column_mass):
    other = jnp.where(place[0] == 1, kept[...], v[...])
    tile = u[...].astype(jnp.float32) + other.astype(jnp.float32)
    finish(tile * down(inverse[...]) * behind[...] * scale, gram, row_mass, column_mass)


def first_kernel(
    scale, place, y, z, kept, local, inverse, behind, gram_in, gram, row_mass, column_mass
):
    del gram_in
    other = jnp.where(place[0] == 1, kept[...], z[...])
    tile = y[...].astype(jnp.float32) + other.astype(jnp.float32)
    tile = jnp.where(place[1] == 1, local[...], tile)
    finish(tile * down(inverse[...]) * behind[...] * scale, gram, row_mass, column_mass)


def mass_shapes(rows):
    specs = [
        pl.BlockSpec((1, TALL), lambda j, *_: (0, j)),
        pl.BlockSpec((1, rows), lambda j, *_: (0, 0)),
    ]
    return specs, [jax.ShapeDtypeStruct((1, rows), jnp.float32)] * 2


def join(kernel, index, scale, place, tiles, inverse, behind, gram=()):
    rows = tiles[0].shape[0]
    mass_specs, mass_types = mass_shapes(rows)
    return pl.pallas_call(
        functools.partial(kernel, scale),
        grid_spec=pltpu.PrefetchScalarGridSpec(
            num_scalar_prefetch=1,
            grid=(rows // TALL,),
            in_specs=[pl.BlockSpec((TALL, rows), lambda j, place: (j, 0))] * len(tiles)
            + [
                pl.BlockSpec((1, TALL), lambda j, place: (0, j)),
                pl.BlockSpec((1, rows), lambda j, place: (0, 0)),
            ]
            + [pl.BlockSpec(memory_space=pl.ANY)] * len(gram),
            out_specs=[pl.BlockSpec((1, TALL, rows), lambda j, place: (index, j, 0))] + mass_specs,
        ),
        out_shape=[jax.ShapeDtypeStruct((2, rows, rows), jnp.float32)] + mass_types,
        input_output_aliases={len(tiles) + 3: 0} if gram else {},
        compiler_params=params(),
        cost_estimate=cost(60000 * rows * rows, 160 * rows * rows)
        if index
        else cost(8 * rows * rows, 12 * rows * rows),
    )(place, *tiles, inverse, behind, *gram)


def local(sketches, test_sketches, domain_map):
    rows, depth = sketches.shape
    size = lax.axis_size("blocks")
    index = lax.axis_index("blocks")
    half = depth // 2
    first = half - DEPTH
    blocks = range(size)
    upper = (index // 2) % 2
    core = index % 2
    place = jnp.stack([upper, core]).astype(jnp.int32)

    across = [(i, i ^ 2) for i in blocks]
    along = [(i, (i + (4 if i & 2 else -4)) % size) for i in blocks]
    swap = [(i, i ^ 1) for i in blocks]

    out1, side1 = halves(place, sketches, 0, first, (1, 0))
    even = send(after(sketches, out1), swap)
    partner1 = send(out1, across)
    near1 = send(side1, along)
    out2, side2 = halves(place, after(sketches, side1), first, DEPTH, (1, 0))
    partner2 = send(out2, across)
    near2 = send(side2, along)

    inverse = inverse_norm(sketches)
    scale = 1.0 / math.sqrt(depth)

    test_inverse = inverse_norm(test_sketches)
    similarity = (
        nt(sketches, test_sketches) * inverse[:, None] * test_inverse[None, :] * scale
    ).astype(jnp.bfloat16)
    members = (
        domain_map[:, None] == lax.iota(jnp.int32, DOM_DEV * size)[None, :]
    ).astype(jnp.bfloat16)
    sums = lax.dot_general(
        members, similarity, (((0,), (0,)), ((), ())), preferred_element_type=jnp.float32
    )
    inside = inside_tile(place, sketches, even)
    across_lanes = inverse[None, :]

    def doubled(value, bit, *waits):
        return send(after(value, *waits), [(i, i ^ bit) for i in blocks])

    bits = [size >> (step + 1) for step in range(size.bit_length() - 1)]
    back_v = [(i, (i + 4) % size) for i in blocks if not i & 2]
    back_y = [(i, i ^ 3) for i in blocks if i & 1]
    back_z = [pair for pair in back_v if pair[0] % 2 == 0]
    partner1 = after(partner1, inside, sums, across_lanes)
    u, v = early_tiles(place, sketches, partner1, near1)
    behind1 = send(after(across_lanes, partner1), [(i, (i + 1) % size) for i in blocks])
    behind2 = send(after(across_lanes, partner1), [(i, (i + 2) % size) for i in blocks])
    for bit in bits[:-4]:
        sums = sums + doubled(sums, bit, partner1)
    came = doubled(sums, bits[-4], u)
    partner2, near2, u, v, behind1, behind2, came = lax.optimization_barrier(
        (partner2, near2, u, v, behind1, behind2, came)
    )
    other1 = send(after(partner1, partner2), swap)
    u, v = late_tiles(place, side2, partner2, near2, u, v)
    vr = send(v, back_v)
    ur = send(u, across)
    other2 = send(after(partner2, u), swap)
    sums = sums + came
    came = doubled(sums, bits[-3], u)
    x = cross_tile(place, sketches, near1, near2, after(other1, u), other2)
    y, z = send(x, back_y), send(x, back_z)

    gram, row_mass2, column_mass2 = join(
        second_kernel, 1, scale, place, (ur, vr, v), across_lanes, behind2
    )
    sums = sums + after(came, row_mass2)
    sums = sums + doubled(sums, bits[-2])
    came = doubled(sums, bits[-1])
    y, came = lax.optimization_barrier((y, came))
    gram, row_mass1, column_mass1 = join(
        first_kernel, 0, scale, place, (y, z, x, inside), across_lanes, behind1, (gram,)
    )
    sums = lax.dynamic_slice_in_dim(sums + came, index * DOM_DEV, DOM_DEV)
    domain_scores = sums * (1.0 / math.sqrt(rows / DOM_DEV))
    mass = (
        row_mass1
        + row_mass2
        + send(column_mass1, [(i, (i - 1) % size) for i in blocks])
        + send(after(column_mass2, row_mass1), [(i, (i - 2) % size) for i in blocks])
    )
    redundancy = mass[0] / float(2 * ROUNDS * rows)
    return (gram, redundancy, domain_scores)


def solution(mesh):
    in_specs = (P(("groups", "blocks"), None), P(), P(("groups", "blocks")))
    out_specs = (
        P(None, ("groups", "blocks"), None),
        P(("groups", "blocks")),
        P(("groups", "blocks"), None),
    )
    return jax.shard_map(local, mesh=mesh, in_specs=in_specs, out_specs=out_specs, check_vma=False)
```
